256 devices in a mesh: chan: 4 (over x_hi, core), wide: 64 (over z, y, x_lo).
Axes of the slice: x: 4 (x_hi: 2, x_lo: 2; x = x_hi * 2 + x_lo), y: 4, z: 8, core: 2. Of those that a mesh axis runs over, the one named last changes fastest.
Arguments:
- echoes: float32 [2, 4, 1024, 8192], P(None, 'chan', 'wide'), may hold values from -6 to 6
- range_chirp: float32 [2, 4, 512], P(None, 'chan'), may hold values from -0.1875 to 0.1875
- azimuth_filter: float32 [2, 4, 1024], P(None, 'chan'), may hold values from -0.125 to 0.125
- pairing: int32 [4], replicated, may hold values from 0 to 3, each once
- offsets: int32 [8, 2], replicated, may hold values from -4 to 4, as said below
Outputs:
- coherence: float32 [2, 1024, 8192], P(None, 'chan', 'wide')
The draws below stay inside these ranges and needn't reach their ends.
Inputs may be any that keep to these rules, and one draw needn't show every extreme that they name: `pairing`: each receiver appears once. both -4 and 4 appear among the offsets.
All inputs are finite; a program needn't handle non-finite values.
Results may differ from the reference program's by a relative error of at most 0.00012.
Values sent between devices are 32-bit elements; how exact they have to be, the bound alone decides.
No kernel may reach another device: no remote copies, remote signals or barrier semaphores. Data moves between devices by JAX's collectives and lax.ppermute only.
A program may use at most 128 MiB of HBM per device.

```python
import jax
import jax.numpy as jnp
from jax import lax

RTAPS = 512
ATAPS = 1024
RADIUS = 4
OGROUPS = 8
CH = 4
P_SIZE = 1024
R = 8192


def draw_offsets(key, part):
    key = jax.random.fold_in(key, 7)
    first_key, second_key = jax.random.split(key)
    values = jax.random.randint(first_key, (OGROUPS * 2,), -RADIUS, RADIUS + 1)
    spots = jax.random.permutation(second_key, OGROUPS * 2)
    values = values.at[spots[0]].set(RADIUS).at[spots[1]].set(-RADIUS)
    return values.reshape(OGROUPS, 2).astype(jnp.int32)


def steps_of(own_key, extent, shards, least, largest):
    gain = 1.0
    for dim, blocks in shards:
        steps = jax.random.uniform(jax.random.fold_in(jax.random.fold_in(own_key, 6), dim), (blocks,), jnp.float32, least / len(shards), largest / len(shards))
        gain = gain * jnp.repeat(jnp.exp(steps), extent[dim] // blocks).reshape((-1,) + (1,) * (len(extent) - 1 - dim))
    return gain


def scatter_about(own_key, dims, width, most, cuts=(), held_as=jnp.bfloat16):
    factor_of = steps_of(own_key, dims, cuts, -0.22, 0.18) if cuts else 1.0
    entries = jax.random.normal(own_key, dims, jnp.float32) * width * factor_of
    return jnp.minimum(jnp.maximum(entries, -most), most).astype(held_as)


def setup_inputs(seed: int = 0) -> dict:
    key_list = jax.random.split(jax.random.key(seed), 6)
    echoes = scatter_about(key_list[0], (2, CH, P_SIZE, R), 1.0, 6.0, ((1, 4), (2, 64)), jnp.float32)
    range_chirp = scatter_about(key_list[1], (2, CH, RTAPS), (2 * RTAPS) ** -0.5, 0.1875, ((1, 4),), jnp.float32)
    azimuth_filter = scatter_about(key_list[2], (2, CH, ATAPS), (2 * ATAPS) ** -0.5, 0.125, ((1, 4),), jnp.float32)
    pairing = jax.random.permutation(key_list[3], CH).astype(jnp.int32)
    offsets = draw_offsets(jax.random.fold_in(key_list[5], 71), 0)
    return dict(echoes=echoes, range_chirp=range_chirp, azimuth_filter=azimuth_filter, pairing=pairing, offsets=offsets)


def band(filter_taps, out_count, in_width):
    tap_count = filter_taps.shape[0]
    padded_line = jnp.concatenate([filter_taps, jnp.zeros((in_width + 1 - tap_count,), jnp.float32)])
    tiled = jnp.tile(padded_line, out_count)[:out_count * in_width]
    return tiled.reshape(out_count, in_width)

def range_matrix(chirp, range_block):
    in_width = range_block + chirp.shape[1]
    real_part = band(chirp[0], range_block, in_width).T
    imag_part = band(chirp[1], range_block, in_width).T
    upper_rows = jnp.concatenate([real_part, imag_part], 1)
    lower_rows = jnp.concatenate([-imag_part, real_part], 1)
    return jnp.concatenate([upper_rows, lower_rows], 0)

def azimuth_matrix(filter_taps, az_block):
    in_width = az_block + filter_taps.shape[1]
    real_part = band(filter_taps[0], az_block, in_width)
    imag_part = band(filter_taps[1], az_block, in_width)
    upper_rows = jnp.concatenate([real_part, -imag_part], 1)
    lower_rows = jnp.concatenate([imag_part, real_part], 1)
    return jnp.concatenate([upper_rows, lower_rows], 0)

def compress_range(signal, chirp):
    tap_count = chirp.shape[1]
    row_count = signal.shape[1]
    bins = signal.shape[2]
    range_block = min(512, bins)
    in_width = range_block + tap_count
    matrix = range_matrix(chirp, range_block)
    padded = jnp.pad(signal, ((0, 0), (0, 0), (0, tap_count)))

    def one_block(block_index):
        window = lax.dynamic_slice_in_dim(padded, block_index * range_block, in_width, 2)
        stacked = jnp.concatenate([window[0], window[1]], 1)
        return jnp.dot(stacked, matrix, precision=lax.Precision.HIGHEST, preferred_element_type=jnp.float32)
    block_count = bins // range_block
    blocks = lax.map(one_block, jnp.arange(block_count, dtype=jnp.int32))
    blocks = blocks.reshape(block_count, row_count, 2, range_block).transpose(2, 1, 0, 3)
    return blocks.reshape(2, row_count, bins)

def compress_azimuth(signal, matrix):
    az_block = matrix.shape[0] // 2
    in_width = matrix.shape[1] // 2
    margin = (in_width - az_block) // 2
    pulses = signal.shape[1]
    columns = signal.shape[2]
    padded = jnp.pad(signal, ((0, 0), (margin, margin), (0, 0)))

    def one_block(block_index):
        window = lax.dynamic_slice_in_dim(padded, block_index * az_block, in_width, 1)
        stacked = window.reshape(2 * in_width, columns)
        return jnp.dot(matrix, stacked, precision=lax.Precision.HIGHEST, preferred_element_type=jnp.float32)
    block_count = pulses // az_block
    blocks = lax.map(one_block, jnp.arange(block_count, dtype=jnp.int32))
    blocks = blocks.reshape(block_count, 2, az_block, columns).transpose(1, 0, 2, 3)
    return blocks.reshape(2, pulses, columns)

def quantities(fore_re, fore_im, aft_re, aft_im):
    return jnp.stack([fore_re * aft_re + fore_im * aft_im, fore_im * aft_re - fore_re * aft_im, fore_re * fore_re + fore_im * fore_im, aft_re * aft_re + aft_im * aft_im])

def coherence_of(window_sums):
    scale = jnp.sqrt(jnp.maximum(window_sums[2], 1.0) * jnp.maximum(window_sums[3], 1.0))
    return jnp.stack([window_sums[0] / scale, window_sums[1] / scale])

def reference(echoes, range_chirp, azimuth_filter, pairing, offsets):
    fore_ids = pairing[:CH // 2]
    fore_image = jnp.zeros((2, P_SIZE, R), jnp.float32)
    aft_image = jnp.zeros((2, P_SIZE, R), jnp.float32)
    for channel in range(CH):
        compressed = compress_range(echoes[:, channel], range_chirp[:, channel])
        matrix = azimuth_matrix(azimuth_filter[:, channel], min(512, P_SIZE))
        focused = compress_azimuth(compressed, matrix)
        member = jnp.any(fore_ids == channel)
        fore_image = fore_image + jnp.where(member, focused, 0.0)
        aft_image = aft_image + jnp.where(member, 0.0, focused)
    products = quantities(fore_image[0], fore_image[1], aft_image[0], aft_image[1])
    reach = 2 * RADIUS
    padded = jnp.pad(products, ((0, 0), (reach, reach), (reach, reach)))
    group_of = (jnp.arange(P_SIZE, dtype=jnp.int32) // (P_SIZE // OGROUPS)).astype(jnp.int32)
    row_shift = offsets[:, 0][group_of]
    col_shift = offsets[:, 1][group_of]
    windowed = padded[:, 0:P_SIZE + reach, :]
    for step in range(1, reach + 1):
        windowed = windowed + padded[:, step:step + P_SIZE + reach, :]
    picked = jnp.zeros((4, P_SIZE, R + 2 * reach), jnp.float32)
    for step in range(-RADIUS, RADIUS + 1):
        chosen = (row_shift == step)[None, :, None]
        picked = picked + jnp.where(chosen, windowed[:, RADIUS + step:RADIUS + step + P_SIZE, :], 0.0)
    col_windowed = picked[:, :, 0:R + reach]
    for step in range(1, reach + 1):
        col_windowed = col_windowed + picked[:, :, step:step + R + reach]
    window_sums = jnp.zeros((4, P_SIZE, R), jnp.float32)
    for step in range(-RADIUS, RADIUS + 1):
        chosen = (col_shift == step)[None, :, None]
        window_sums = window_sums + jnp.where(chosen, col_windowed[:, :, RADIUS + step:RADIUS + step + R], 0.0)
    return coherence_of(window_sums)
```

```python
import jax
import jax.numpy as jnp
from jax import lax
from jax.experimental import pallas as pl
from jax.experimental.pallas import tpu as pltpu
from jax.sharding import PartitionSpec as P

RADIUS = 4
REACH = 2 * RADIUS
F32 = jnp.float32
BF16 = jnp.bfloat16
VMEM_LIMIT = 48 * 1024 * 1024


def split(x):
    hi = x.astype(BF16)
    return hi, (x - hi.astype(F32)).astype(BF16)


def dot_nn(a, b):
    return lax.dot_general(a, b, (((1,), (0,)), ((), ())), preferred_element_type=F32)


def dot_nt(a, b):
    return lax.dot_general(a, b, (((1,), (1,)), ((), ())), preferred_element_type=F32)


def toeplitz(taps, rows, width):
    line = jnp.concatenate([taps, jnp.zeros((1, width - taps.shape[1]), F32)], 1)
    return pltpu.roll(jnp.broadcast_to(line, (rows, width)), 0, 1, stride=1, stride_axis=0)


def range_kernel(echo_ref, chirp_ref, out_ref, e_hi, e_lo, w_hi, w_lo):
    real = split(toeplitz(chirp_ref[0], 128, 640))
    imag = split(toeplitz(chirp_ref[1], 128, 640))
    for w_ref, re, im in ((w_hi, real[0], imag[0]), (w_lo, real[1], imag[1])):
        for j in range(5):
            cols = slice(128 * j, 128 * j + 128)
            w_ref[0:128, 256 * j:256 * j + 128] = re[:, cols]
            w_ref[0:128, 256 * j + 128:256 * j + 256] = -im[:, cols]
            w_ref[128:256, 256 * j:256 * j + 128] = im[:, cols]
            w_ref[128:256, 256 * j + 128:256 * j + 256] = re[:, cols]
    for n in range(64):
        for part in range(2):
            hi, lo = split(echo_ref[part, :, 128 * n:128 * n + 128])
            e_hi[16 * n:16 * n + 16, 128 * part:128 * part + 128] = hi
            e_lo[16 * n:16 * n + 16, 128 * part:128 * part + 128] = lo
    e_hi[1024:1088, :] = jnp.zeros((64, 256), BF16)
    e_lo[1024:1088, :] = jnp.zeros((64, 256), BF16)

    @pl.loop(0, 4)
    def _(m):
        starts = [pl.multiple_of(256 * m + 16 * j, 16) for j in range(5)]
        hi = jnp.concatenate([e_hi[pl.ds(s, 256), :] for s in starts], 1)
        lo = jnp.concatenate([e_lo[pl.ds(s, 256), :] for s in starts], 1)
        acc = dot_nt(hi, w_hi[...]) + dot_nt(hi, w_lo[...]) + dot_nt(lo, w_hi[...])
        out_ref[pl.ds(16 * m, 16), 0:16, :] = acc[:, 0:128].reshape(16, 16, 128)
        out_ref[pl.ds(16 * m, 16), 16:32, :] = acc[:, 128:256].reshape(16, 16, 128)


def taps_kernel(taps_ref, hi_ref, lo_ref):
    for part in range(2):
        hi, lo = split(toeplitz(taps_ref[part], 256, 1280))
        hi_ref[256 * part:256 * part + 256, :] = hi
        lo_ref[256 * part:256 * part + 256, :] = lo


def azimuth_kernel(x_ref, t_hi, t_lo, o0, o1, o2, o3, x_hi, x_lo, y_ref):
    for part in range(2):
        hi, lo = split(x_ref[:, 16 * part:16 * part + 16, :].reshape(1024, 128))
        x_hi[:, 128 * part:128 * part + 128] = hi
        x_lo[:, 128 * part:128 * part + 128] = lo
    for part in range(2):
        y_ref[part, 0:8, :] = jnp.zeros((8, 128), F32)
        y_ref[part, 1032:1040, :] = jnp.zeros((8, 128), F32)
    for q in range(4):
        first, last = max(q - 2, 0), min(q + 2, 3)
        taps = slice(256 * (first - q + 2), 256 * (last - q + 3))
        rows = slice(256 * first, 256 * last + 256)
        g = (
            dot_nn(t_hi[:, taps], x_hi[rows, :])
            + dot_nn(t_hi[:, taps], x_lo[rows, :])
            + dot_nn(t_lo[:, taps], x_hi[rows, :])
        )
        y_ref[0, 8 + 256 * q:264 + 256 * q, :] = g[0:256, 0:128] - g[256:512, 128:256]
        y_ref[1, 8 + 256 * q:264 + 256 * q, :] = g[0:256, 128:256] + g[256:512, 0:128]
    me = lax.axis_index("chan")
    for k, o_ref in enumerate((o0, o1, o2, o3)):
        start = pl.multiple_of(lax.rem(me + k, 4) * 256, 8)
        o_ref[...] = y_ref[:, pl.ds(start, 272), :]


def sum_kernel(pairing_ref, y0, y1, y2, y3, sums_ref, first_ref, last_ref):
    me = lax.axis_index("chan")
    first_ref[...] = jnp.zeros((32, 384), F32)
    last_ref[...] = jnp.zeros((32, 384), F32)
    member = []
    for k in range(4):
        channel = lax.rem(me + 4 - k, 4)
        member.append((pairing_ref[0] == channel) | (pairing_ref[1] == channel))
    for part in range(2):
        fore = jnp.zeros((272, 128), F32)
        aft = jnp.zeros((272, 128), F32)
        for k, y_ref in enumerate((y0, y1, y2, y3)):
            y = y_ref[part]
            fore = fore + jnp.where(member[k], y, 0.0)
            aft = aft + jnp.where(member[k], 0.0, y)
        for plane, value in ((part, fore), (2 + part, aft)):
            sums_ref[plane] = value
            turned = jnp.concatenate([value, jnp.zeros((112, 128), F32)], 0).T
            first_ref[8 * plane:8 * plane + 8, :] = turned[0:8]
            last_ref[8 * plane:8 * plane + 8, :] = turned[120:128]


def window_kernel(offsets_ref, sums_ref, before_ref, after_ref, out_ref, p_hi, p_lo):
    me = lax.axis_index("chan")
    halo = jnp.concatenate([before_ref[...], after_ref[...], jnp.zeros((64, 384), F32)], 0).T[0:272]
    main = [sums_ref[i] for i in range(4)]
    edge = [
        jnp.concatenate([halo[:, 8 * i:8 * i + 8], halo[:, 32 + 8 * i:40 + 8 * i], jnp.zeros((272, 112), F32)], 1)
        for i in range(4)
    ]
    for col, (fr, fi, ar, ai) in ((0, main), (128, edge)):
        planes = (fr * ar + fi * ai, fi * ar - fr * ai, fr * fr + fi * fi, ar * ar + ai * ai)
        for q, value in enumerate(planes):
            hi, lo = split(value)
            p_hi[0:272, 256 * q + col:256 * q + col + 128] = hi
            p_lo[0:272, 256 * q + col:256 * q + col + 128] = lo
    p_hi[272:384, :] = jnp.zeros((112, 1024), BF16)
    p_lo[272:384, :] = jnp.zeros((112, 1024), BF16)
    for g in range(2):
        oa = offsets_ref[2 * me + g, 0]
        orr = offsets_ref[2 * me + g, 1]
        row = lax.broadcasted_iota(jnp.int32, (128, 256), 0)
        src = lax.broadcasted_iota(jnp.int32, (128, 256), 1)
        rows = jnp.where(jnp.abs(src - REACH - row - oa) <= RADIUS, 1.0, 0.0).astype(BF16)
        sums = dot_nn(rows, p_hi[128 * g:128 * g + 256, :]) + dot_nn(rows, p_lo[128 * g:128 * g + 256, :])
        lane = lax.broadcasted_iota(jnp.int32, (256, 128), 0)
        bin_out = lax.broadcasted_iota(jnp.int32, (256, 128), 1)
        at = jnp.where(lane < 128, lane, jnp.where(lane < 136, lane - 136, jnp.where(lane < 144, lane - 8, 4096)))
        cols = jnp.where(jnp.abs(at - bin_out - orr) <= RADIUS, 1.0, 0.0).astype(BF16)
        stacked = jnp.concatenate([sums[:, 256 * q:256 * q + 256] for q in range(4)], 0)
        hi, lo = split(stacked)
        window = dot_nn(hi, cols) + dot_nn(lo, cols)
        scale = jnp.sqrt(jnp.maximum(window[256:384], 1.0) * jnp.maximum(window[384:512], 1.0))
        out_ref[0, 128 * g:128 * g + 128, :] = window[0:128] / scale
        out_ref[1, 128 * g:128 * g + 128, :] = window[128:256] / scale


def call(kernel, name, out_shape, scratch, n_in, smem=(), flops=0, moved=0):
    specs = [pl.BlockSpec(memory_space=pltpu.SMEM if i in smem else pltpu.VMEM) for i in range(n_in)]
    return pl.pallas_call(
        kernel,
        out_shape=out_shape,
        in_specs=specs,
        out_specs=jax.tree.map(lambda _: pl.BlockSpec(memory_space=pltpu.VMEM), out_shape),
        scratch_shapes=scratch,
        compiler_params=pltpu.CompilerParams(vmem_limit_bytes=VMEM_LIMIT),
        cost_estimate=pl.CostEstimate(flops=flops, bytes_accessed=moved, transcendentals=0),
        name=name,
    )


def shape(*dims, dtype=F32):
    return jax.ShapeDtypeStruct(dims, dtype)


def body(echoes, range_chirp, azimuth_filter, pairing, offsets):
    signal = echoes[:, 0]
    chirp = range_chirp.reshape(2, 1, 512)
    taps = azimuth_filter.reshape(2, 1, 1024)
    parted = call(
        range_kernel, "range_filter", shape(64, 32, 128),
        [pltpu.VMEM((1088, 256), BF16)] * 2 + [pltpu.VMEM((256, 1280), BF16)] * 2,
        2, flops=2_000_000_000, moved=2 << 20,
    )(signal, chirp)
    t_hi, t_lo = call(
        taps_kernel, "azimuth_taps", (shape(512, 1280, dtype=BF16), shape(512, 1280, dtype=BF16)), [],
        1, flops=1_000_000_000, moved=8 << 20,
    )(taps)
    turned = lax.all_to_all(parted, "wide", split_axis=0, concat_axis=0, tiled=True)
    pieces = call(
        azimuth_kernel, "azimuth_filter", (shape(2, 272, 128),) * 4,
        [pltpu.VMEM((1024, 256), BF16)] * 2 + [pltpu.VMEM((2, 1040, 128), F32)],
        3, flops=3_000_000_000, moved=4 << 20,
    )(turned, t_hi, t_lo)
    got = [pieces[0]]
    for k in range(1, 4):
        got.append(lax.ppermute(pieces[k], "chan", [(i, (i + k) % 4) for i in range(4)]))
    sums, first, last = call(
        sum_kernel, "fore_aft", (shape(4, 272, 128), shape(32, 384), shape(32, 384)), [],
        5, smem=(0,), flops=1_000_000, moved=2 << 20,
    )(pairing, *got)
    up = [(i, i + 1) for i in range(63)]
    before = lax.ppermute(last, "wide", up)
    after = lax.ppermute(first, "wide", [(j, i) for i, j in up])
    return call(
        window_kernel, "coherence", shape(2, 256, 128),
        [pltpu.VMEM((384, 1024), BF16)] * 2,
        4, smem=(0,), flops=1_000_000_000, moved=1 << 20,
    )(offsets, sums, before, after)


def solution(mesh):
    placed = (P(None, "chan", "wide", None), P(None, "chan", None), P(None, "chan", None), P(), P())
    return jax.shard_map(
        body, mesh=mesh, in_specs=placed, out_specs=P(None, "chan", "wide"), check_vma=False
    )
```

```python
import jax
import jax.numpy as jnp
from jax import lax
from jax.experimental import pallas as pl
from jax.experimental.pallas import tpu as pltpu
from jax.sharding import PartitionSpec as P

RADIUS = 4
REACH = 2 * RADIUS
F32 = jnp.float32
BF16 = jnp.bfloat16
VMEM_LIMIT = 24 * 1024 * 1024


def split(x):
    hi = x.astype(BF16)
    return hi, (x - hi.astype(F32)).astype(BF16)


def dot_nn(a, b):
    return lax.dot_general(a, b, (((1,), (0,)), ((), ())), preferred_element_type=F32)


def dot_nt(a, b):
    return lax.dot_general(a, b, (((1,), (1,)), ((), ())), preferred_element_type=F32)


def toeplitz(taps, rows, width):
    line = jnp.concatenate([taps, jnp.zeros((1, width - taps.shape[1]), F32)], 1)
    return pltpu.roll(jnp.broadcast_to(line, (rows, width)), 0, 1, stride=1, stride_axis=0)


def range_kernel(echo_hbm, chirp_hbm, out_ref, echo, chirp, e_hi, e_lo, w_hi, w_lo, sems):
    taps_copy = pltpu.make_async_copy(chirp_hbm, chirp, sems.at[4])
    taps_copy.start()
    copies = []
    for m in range(4):
        bins = pl.ds(2048 * m, 2048)
        copies.append(pltpu.make_async_copy(echo_hbm.at[:, :, bins], echo.at[:, :, bins], sems.at[m]))
        copies[m].start()
    e_hi[1024:1088, :] = jnp.zeros((64, 256), BF16)
    e_lo[1024:1088, :] = jnp.zeros((64, 256), BF16)
    taps_copy.wait()
    real = split(toeplitz(chirp[0], 128, 640))
    imag = split(toeplitz(chirp[1], 128, 640))
    for w_ref, re, im in ((w_hi, real[0], imag[0]), (w_lo, real[1], imag[1])):
        for j in range(5):
            cols = slice(128 * j, 128 * j + 128)
            w_ref[0:128, 256 * j:256 * j + 128] = re[:, cols]
            w_ref[0:128, 256 * j + 128:256 * j + 256] = -im[:, cols]
            w_ref[128:256, 256 * j:256 * j + 128] = im[:, cols]
            w_ref[128:256, 256 * j + 128:256 * j + 256] = re[:, cols]

    def fill(m):
        copies[m].wait()
        for n in range(16 * m, 16 * m + 16):
            for part in range(2):
                hi, lo = split(echo[part, :, 128 * n:128 * n + 128])
                e_hi[16 * n:16 * n + 16, 128 * part:128 * part + 128] = hi
                e_lo[16 * n:16 * n + 16, 128 * part:128 * part + 128] = lo

    fill(0)
    early = lax.broadcasted_iota(jnp.int32, (256, 128), 1) < REACH
    last = [jnp.zeros((16, 128), F32)] * 2
    for m in range(4):
        if m < 3:
            fill(m + 1)
        starts = [256 * m + 16 * j for j in range(5)]
        hi = jnp.concatenate([e_hi[s:s + 256, :] for s in starts], 1)
        lo = jnp.concatenate([e_lo[s:s + 256, :] for s in starts], 1)
        acc = dot_nt(hi, w_hi[...]) + dot_nt(hi, w_lo[...]) + dot_nt(lo, w_hi[...])
        for part in range(2):
            turned = pltpu.roll(acc[:, 128 * part:128 * part + 128], REACH, 1)
            before = jnp.concatenate([last[part], turned[0:240]], 0)
            out_ref[16 * m:16 * m + 16, 16 * part:16 * part + 16, :] = jnp.where(early, before, turned).reshape(16, 16, 128)
            last[part] = turned[240:256]
    for part in range(2):
        out_ref[0, 16 * part:16 * part + 16, 0:REACH] = last[part][:, 0:REACH]


def azimuth_kernel(x_ref, taps_ref, o0, o1, o2, o3, t_hi, t_lo, x_hi, x_lo, y_ref):
    for part in range(2):
        hi, lo = split(toeplitz(taps_ref[part], 256, 1280))
        t_hi[256 * part:256 * part + 256, :] = hi
        t_lo[256 * part:256 * part + 256, :] = lo
        hi, lo = split(x_ref[:, 16 * part:16 * part + 16, :].reshape(1024, 128))
        x_hi[:, 128 * part:128 * part + 128] = hi
        x_lo[:, 128 * part:128 * part + 128] = lo
        y_ref[part, 0:8, :] = jnp.zeros((8, 128), F32)
        y_ref[part, 1032:1040, :] = jnp.zeros((8, 128), F32)
    for q in range(4):
        first, last = max(q - 2, 0), min(q + 2, 3)
        taps = slice(256 * (first - q + 2), 256 * (last - q + 3))
        rows = slice(256 * first, 256 * last + 256)
        g = (
            dot_nn(t_hi[:, taps], x_hi[rows, :])
            + dot_nn(t_hi[:, taps], x_lo[rows, :])
            + dot_nn(t_lo[:, taps], x_hi[rows, :])
        )
        y_ref[0, 8 + 256 * q:264 + 256 * q, :] = g[0:256, 0:128] - g[256:512, 128:256]
        y_ref[1, 8 + 256 * q:264 + 256 * q, :] = g[0:256, 128:256] + g[256:512, 0:128]
    me = lax.axis_index("chan")
    for k, o_ref in enumerate((o0, o1, o2, o3)):
        start = pl.multiple_of((me ^ k) * 256, 8)
        o_ref[...] = y_ref[:, pl.ds(start, 272), :]


def sum_kernel(pairing_ref, y0, y1, y2, y3, sums_ref, edge_ref):
    me = lax.axis_index("chan")
    lane = lax.broadcasted_iota(jnp.int32, (272, 128), 1)
    edge = jnp.zeros((272, 128), F32)
    for part in range(2):
        fore = jnp.zeros((272, 128), F32)
        aft = jnp.zeros((272, 128), F32)
        for k, y_ref in enumerate((y0, y1, y2, y3)):
            channel = me ^ k
            member = (pairing_ref[0] == channel) | (pairing_ref[1] == channel)
            fore = fore + jnp.where(member, y_ref[part], 0.0)
            aft = aft + jnp.where(member, 0.0, y_ref[part])
        for plane, value in ((part, fore), (2 + part, aft)):
            sums_ref[plane] = value
            at = 16 * plane
            moved = pltpu.roll(value, at, 1) if at else value
            edge = jnp.where((lane >= at) & (lane < at + 16), moved, edge)
    edge_ref[...] = edge[0:136] + pltpu.roll(edge[136:272], 64, 1)


def quantities(fr, fi, ar, ai):
    return fr * ar + fi * ai, fi * ar - fr * ai, fr * fr + fi * fi, ar * ar + ai * ai


def row_window(oa):
    row = lax.broadcasted_iota(jnp.int32, (128, 256), 0)
    src = lax.broadcasted_iota(jnp.int32, (128, 256), 1)
    return jnp.where(jnp.abs(src - REACH - row - oa) <= RADIUS, 1.0, 0.0).astype(BF16)


def bin_window(orr, shift, wanted):
    lane = lax.broadcasted_iota(jnp.int32, (128, 128), 0)
    bin_out = lax.broadcasted_iota(jnp.int32, (128, 128), 1)
    near = (jnp.abs(lane + shift - bin_out - orr) <= RADIUS) & wanted(lane)
    return jnp.where(near, 1.0, 0.0).astype(BF16)


def main_kernel(offsets_ref, sums_ref, out_ref, p_hi, p_lo):
    me = lax.axis_index("chan")
    first = lax.axis_index("wide") == 0
    for q, value in enumerate(quantities(*[sums_ref[i] for i in range(4)])):
        hi, lo = split(value)
        p_hi[0:272, 128 * q:128 * q + 128] = hi
        p_lo[0:272, 128 * q:128 * q + 128] = lo
    p_hi[272:384, :] = jnp.zeros((112, 512), BF16)
    p_lo[272:384, :] = jnp.zeros((112, 512), BF16)
    for g in range(2):
        rows = row_window(offsets_ref[2 * me + g, 0])
        sums = dot_nn(rows, p_hi[128 * g:128 * g + 256, :]) + dot_nn(rows, p_lo[128 * g:128 * g + 256, :])
        cols = bin_window(offsets_ref[2 * me + g, 1], -REACH, lambda lane: (lane >= REACH) | jnp.logical_not(first))
        hi, lo = split(jnp.concatenate([sums[:, 128 * q:128 * q + 128] for q in range(4)], 0))
        out_ref[g] = dot_nn(hi, cols) + dot_nn(lo, cols)


def coherence_kernel(offsets_ref, main_ref, edge_ref, out_ref, p_hi, p_lo):
    me = lax.axis_index("chan")
    final = lax.axis_index("wide") == lax.axis_size("wide") - 1
    packed = edge_ref[...]
    edge = jnp.concatenate([packed, pltpu.roll(packed, 64, 1)], 0)
    lane = lax.broadcasted_iota(jnp.int32, (272, 128), 1)
    planes = [edge] + [pltpu.roll(edge, 128 - 16 * i, 1) for i in range(1, 4)]
    both = jnp.zeros((272, 128), F32)
    for q, value in enumerate(quantities(*planes)):
        moved = pltpu.roll(value, 16 * q, 1) if q else value
        both = jnp.where((lane >= 16 * q) & (lane < 16 * q + 16), moved, both)
    hi, lo = split(both)
    p_hi[0:272, :] = hi
    p_lo[0:272, :] = lo
    p_hi[272:384, :] = jnp.zeros((112, 128), BF16)
    p_lo[272:384, :] = jnp.zeros((112, 128), BF16)
    for g in range(2):
        rows = row_window(offsets_ref[2 * me + g, 0])
        sums = dot_nn(rows, p_hi[128 * g:128 * g + 256, :]) + dot_nn(rows, p_lo[128 * g:128 * g + 256, :])
        cols = bin_window(
            offsets_ref[2 * me + g, 1], 128 - REACH,
            lambda lane: (lane < REACH) | ((lane < 2 * REACH) & jnp.logical_not(final)),
        )
        hi, lo = split(jnp.concatenate([sums] + [pltpu.roll(sums, 128 - 16 * q, 1) for q in range(1, 4)], 0))
        window = main_ref[g] + dot_nn(hi, cols) + dot_nn(lo, cols)
        scale = jnp.sqrt(jnp.maximum(window[256:384], 1.0) * jnp.maximum(window[384:512], 1.0))
        out_ref[0, 128 * g:128 * g + 128, :] = window[0:128] / scale
        out_ref[1, 128 * g:128 * g + 128, :] = window[128:256] / scale


def call(kernel, name, out_shape, scratch, n_in, smem=(), hbm=(), flops=0, moved=0, vmem=VMEM_LIMIT):
    spaces = [pltpu.SMEM if i in smem else pltpu.HBM if i in hbm else pltpu.VMEM for i in range(n_in)]
    return pl.pallas_call(
        kernel,
        out_shape=out_shape,
        in_specs=[pl.BlockSpec(memory_space=space) for space in spaces],
        out_specs=jax.tree.map(lambda _: pl.BlockSpec(memory_space=pltpu.VMEM), out_shape),
        scratch_shapes=scratch,
        compiler_params=pltpu.CompilerParams(vmem_limit_bytes=vmem),
        cost_estimate=pl.CostEstimate(flops=flops, bytes_accessed=moved, transcendentals=0),
        name=name,
    )


def shape(*dims, dtype=F32):
    return jax.ShapeDtypeStruct(dims, dtype)


def body(echoes, range_chirp, azimuth_filter, pairing, offsets):
    signal = echoes[:, 0]
    chirp = range_chirp.reshape(2, 1, 512)
    taps = azimuth_filter.reshape(2, 1, 1024)
    parted = call(
        range_kernel, "range_filter", shape(64, 32, 128),
        [pltpu.VMEM((2, 16, 8192), F32), pltpu.VMEM((2, 1, 512), F32)]
        + [pltpu.VMEM((1088, 256), BF16)] * 2 + [pltpu.VMEM((256, 1280), BF16)] * 2
        + [pltpu.SemaphoreType.DMA((5,))],
        2, hbm=(0, 1), flops=2_000_000_000, moved=2 << 20, vmem=60 << 20,
    )(signal, chirp)
    turned = lax.all_to_all(parted, "wide", split_axis=0, concat_axis=0, tiled=True)
    pieces = call(
        azimuth_kernel, "azimuth_filter", (shape(2, 272, 128),) * 4,
        [pltpu.VMEM((512, 1280), BF16)] * 2 + [pltpu.VMEM((1024, 256), BF16)] * 2
        + [pltpu.VMEM((2, 1040, 128), F32)],
        2, flops=3_000_000_000, moved=4 << 20,
    )(turned, taps)
    got = [pieces[0]] + [
        lax.ppermute(pieces[k], "chan", [(i, i ^ k) for i in range(4)]) for k in range(1, 4)
    ]
    sums, edge = call(
        sum_kernel, "fore_aft", (shape(4, 272, 128), shape(136, 128)), [],
        5, smem=(0,), flops=1_000_000, moved=2 << 20,
    )(pairing, *got)
    after = lax.ppermute(edge, "wide", [(i, (i - 1) % 64) for i in range(64)])
    main = call(
        main_kernel, "window_sums", shape(2, 512, 128), [pltpu.VMEM((384, 512), BF16)] * 2,
        2, smem=(0,), flops=500_000_000, moved=1 << 20,
    )(offsets, sums)
    return call(
        coherence_kernel, "coherence", shape(2, 256, 128), [pltpu.VMEM((384, 128), BF16)] * 2,
        3, smem=(0,), flops=500_000_000, moved=1 << 20,
    )(offsets, main, after)


def solution(mesh):
    placed = (P(None, "chan", "wide", None), P(None, "chan", None), P(None, "chan", None), P(), P())
    return jax.shard_map(
        body, mesh=mesh, in_specs=placed, out_specs=P(None, "chan", "wide"), check_vma=False
    )
```

```python
import functools

import jax
import jax.numpy as jnp
from jax import lax
from jax.experimental import pallas as pl
from jax.experimental.pallas import tpu as pltpu
from jax.sharding import PartitionSpec as P

RADIUS = 4
REACH = 2 * RADIUS
XOR_ORDER = (0, 2, 3, 1)
F32 = jnp.float32
BF16 = jnp.bfloat16
VMEM_LIMIT = 24 * 1024 * 1024


def split(x):
    hi = x.astype(BF16)
    return hi, (x - hi.astype(F32)).astype(BF16)


def dot_nn(a, b):
    return lax.dot_general(a, b, (((1,), (0,)), ((), ())), preferred_element_type=F32)


def dot_nt(a, b):
    return lax.dot_general(a, b, (((1,), (1,)), ((), ())), preferred_element_type=F32)


def toeplitz(taps, rows, width, start=0):
    line = jnp.concatenate([taps, jnp.zeros((1, width - taps.shape[1]), F32)], 1)
    return pltpu.roll(jnp.broadcast_to(line, (rows, width)), start, 1, stride=1, stride_axis=0)


def range_kernel(echo_hbm, chirp_hbm, out_ref, echo, chirp, e_hi, e_lo, w_hi, w_lo, sems):
    taps_copy = pltpu.make_async_copy(chirp_hbm, chirp, sems.at[4])
    taps_copy.start()
    copies = []
    for m in range(4):
        bins = pl.ds(2048 * m, 2048)
        copies.append(pltpu.make_async_copy(echo_hbm.at[:, :, bins], echo.at[:, :, bins], sems.at[m]))
        copies[m].start()
    e_hi[1024:1088, :] = jnp.zeros((64, 256), BF16)
    e_lo[1024:1088, :] = jnp.zeros((64, 256), BF16)
    taps_copy.wait()
    real = split(toeplitz(chirp[0], 128, 640))
    imag = split(toeplitz(chirp[1], 128, 640))
    for w_ref, re, im in ((w_hi, real[0], imag[0]), (w_lo, real[1], imag[1])):
        for j in range(5):
            cols = slice(128 * j, 128 * j + 128)
            w_ref[0:128, 256 * j:256 * j + 128] = re[:, cols]
            w_ref[0:128, 256 * j + 128:256 * j + 256] = -im[:, cols]
            w_ref[128:256, 256 * j:256 * j + 128] = im[:, cols]
            w_ref[128:256, 256 * j + 128:256 * j + 256] = re[:, cols]

    def fill(m):
        copies[m].wait()
        for n in range(16 * m, 16 * m + 16):
            for part in range(2):
                hi, lo = split(echo[part, :, 128 * n:128 * n + 128])
                e_hi[16 * n:16 * n + 16, 128 * part:128 * part + 128] = hi
                e_lo[16 * n:16 * n + 16, 128 * part:128 * part + 128] = lo

    fill(0)
    early = lax.broadcasted_iota(jnp.int32, (256, 128), 1) < REACH
    last = [jnp.zeros((16, 128), F32)] * 2
    for m in range(4):
        if m < 3:
            fill(m + 1)
        starts = [256 * m + 16 * j for j in range(5)]
        hi = jnp.concatenate([e_hi[s:s + 256, :] for s in starts], 1)
        lo = jnp.concatenate([e_lo[s:s + 256, :] for s in starts], 1)
        acc = dot_nt(hi, w_hi[...]) + dot_nt(hi, w_lo[...]) + dot_nt(lo, w_hi[...])
        for part in range(2):
            turned = pltpu.roll(acc[:, 128 * part:128 * part + 128], REACH, 1)
            before = jnp.concatenate([last[part], turned[0:240]], 0)
            out_ref[16 * m:16 * m + 16, 16 * part:16 * part + 16, :] = jnp.where(early, before, turned).reshape(16, 16, 128)
            last[part] = turned[240:256]
    for part in range(2):
        out_ref[0, 16 * part:16 * part + 16, 0:REACH] = last[part][:, 0:REACH]


def prepare_kernel(pairing_ref, offsets_ref, weight_ref, rows_ref, near_ref, far_ref):
    me = lax.axis_index("chan")
    first = lax.axis_index("wide") == 0
    final = lax.axis_index("wide") == lax.axis_size("wide") - 1
    for i, k in enumerate(XOR_ORDER):
        member = (pairing_ref[0] == (me ^ k)) | (pairing_ref[1] == (me ^ k))
        weight_ref[i] = jnp.full((8, 128), jnp.where(member, 1.0, 0.0), F32)
    row = lax.broadcasted_iota(jnp.int32, (128, 256), 0)
    src = lax.broadcasted_iota(jnp.int32, (128, 256), 1)
    lane = lax.broadcasted_iota(jnp.int32, (128, 128), 0)
    bin_out = lax.broadcasted_iota(jnp.int32, (128, 128), 1)
    for g in range(2):
        oa = offsets_ref[2 * me + g, 0]
        orr = offsets_ref[2 * me + g, 1]
        rows_ref[g] = jnp.where(jnp.abs(src - REACH - row - oa) <= RADIUS, 1.0, 0.0).astype(BF16)
        near = (jnp.abs(lane - REACH - bin_out - orr) <= RADIUS) & ((lane >= REACH) | jnp.logical_not(first))
        near_ref[g] = jnp.where(near, 1.0, 0.0).astype(BF16)
        far = (jnp.abs(lane + 128 - REACH - bin_out - orr) <= RADIUS) & (
            (lane < REACH) | ((lane < 2 * REACH) & jnp.logical_not(final))
        )
        far_ref[g] = jnp.where(far, 1.0, 0.0).astype(BF16)


def azimuth_half(flip, x_ref, taps_ref, order_ref, o0, o1, done_ref, t_hi, t_lo, x_hi, x_lo, y_ref):
    done_ref[...] = jnp.zeros((8, 128), F32)
    for part in range(2):
        hi, lo = split(toeplitz(taps_ref[part], 272, 1280, 1280 - REACH))
        t_hi[part] = hi
        t_lo[part] = lo
        hi, lo = split(x_ref[:, 16 * part:16 * part + 16, :].reshape(1024, 128))
        x_hi[:, 128 * part:128 * part + 128] = hi
        x_lo[:, 128 * part:128 * part + 128] = lo
    me = lax.axis_index("chan")

    def quarter(q):
        first, last = max(q - 2, 0), min(q + 2, 3)
        cols = slice(256 * (first - q + 2), 256 * (last - q + 3))
        rows = slice(256 * first, 256 * last + 256)
        t = [ref[part, :, cols] for ref in (t_hi, t_lo) for part in range(2)]
        g = [dot_nn(t[i], x_hi[rows, :]) + dot_nn(t[i], x_lo[rows, :]) + dot_nn(t[2 + i], x_hi[rows, :]) for i in range(2)]
        return g[0][:, 0:128] - g[1][:, 128:256], g[0][:, 128:256] + g[1][:, 0:128]

    for half in range(2):
        @pl.when((me // 2) ^ flip == half)
        def _(half=half):
            for i in range(2):
                for part, value in enumerate(quarter(2 * half + i)):
                    y_ref[i, part] = value
            for part in range(2):
                y_ref[0, part, 264:272, :] = y_ref[1, part, 8:16, :]
                y_ref[1, part, 0:8, :] = y_ref[0, part, 256:264, :]
                if half == 0:
                    y_ref[0, part, 0:8, :] = jnp.zeros((8, 128), F32)
                else:
                    y_ref[1, part, 264:272, :] = jnp.zeros((8, 128), F32)

    o0[...] = y_ref[me % 2]
    o1[...] = y_ref[1 - me % 2]


def partial_kernel(weight_ref, y0, y2, y3, part_ref):
    for part in range(2):
        fore = aft = 0.0
        for k, y_ref in enumerate((y0, y2, y3)):
            weight = weight_ref[k, 0:1, :]
            y = y_ref[part]
            fore = fore + y * weight
            aft = aft + y * (1.0 - weight)
        part_ref[part] = fore
        part_ref[2 + part] = aft


def whole_sums(weight_ref, part_ref, y1):
    weight = weight_ref[3, 0:1, :]
    fore = [part_ref[part] + y1[part] * weight for part in range(2)]
    return fore + [part_ref[2 + part] + y1[part] * (1.0 - weight) for part in range(2)]


def edge_kernel(weight_ref, part_ref, y1, edge_ref):
    lane = lax.broadcasted_iota(jnp.int32, (272, 128), 1)
    edge = jnp.zeros((272, 128), F32)
    for plane, value in enumerate(whole_sums(weight_ref, part_ref, y1)):
        at = 16 * plane
        moved = pltpu.roll(value, at, 1) if at else value
        edge = jnp.where((lane >= at) & (lane < at + 16), moved, edge)
    edge_ref[...] = edge[0:136] + pltpu.roll(edge[136:272], 64, 1)


def quantities(fr, fi, ar, ai):
    return fr * ar + fi * ai, fi * ar - fr * ai, fr * fr + fi * fi, ar * ar + ai * ai


def main_kernel(weight_ref, rows_ref, near_ref, part_ref, y1, out_ref, p_hi, p_lo):
    for q, value in enumerate(quantities(*whole_sums(weight_ref, part_ref, y1))):
        hi, lo = split(value)
        p_hi[0:272, 128 * q:128 * q + 128] = hi
        p_lo[0:272, 128 * q:128 * q + 128] = lo
    p_hi[272:384, :] = jnp.zeros((112, 512), BF16)
    p_lo[272:384, :] = jnp.zeros((112, 512), BF16)
    for g in range(2):
        sums = dot_nn(rows_ref[g], p_hi[128 * g:128 * g + 256, :]) + dot_nn(rows_ref[g], p_lo[128 * g:128 * g + 256, :])
        hi, lo = split(jnp.concatenate([sums[:, 128 * q:128 * q + 128] for q in range(4)], 0))
        out_ref[g] = dot_nn(hi, near_ref[g]) + dot_nn(lo, near_ref[g])


def coherence_kernel(rows_ref, far_ref, main_ref, edge_ref, out_ref, p_hi, p_lo):
    packed = edge_ref[...]
    edge = jnp.concatenate([packed, pltpu.roll(packed, 64, 1)], 0)
    lane = lax.broadcasted_iota(jnp.int32, (272, 128), 1)
    planes = [edge] + [pltpu.roll(edge, 128 - 16 * i, 1) for i in range(1, 4)]
    both = jnp.zeros((272, 128), F32)
    for q, value in enumerate(quantities(*planes)):
        moved = pltpu.roll(value, 16 * q, 1) if q else value
        both = jnp.where((lane >= 16 * q) & (lane < 16 * q + 16), moved, both)
    hi, lo = split(both)
    p_hi[0:272, :] = hi
    p_lo[0:272, :] = lo
    p_hi[272:384, :] = jnp.zeros((112, 128), BF16)
    p_lo[272:384, :] = jnp.zeros((112, 128), BF16)
    for g in range(2):
        sums = dot_nn(rows_ref[g], p_hi[128 * g:128 * g + 256, :]) + dot_nn(rows_ref[g], p_lo[128 * g:128 * g + 256, :])
        hi, lo = split(jnp.concatenate([sums] + [pltpu.roll(sums, 128 - 16 * q, 1) for q in range(1, 4)], 0))
        window = main_ref[g] + dot_nn(hi, far_ref[g]) + dot_nn(lo, far_ref[g])
        scale = 1.0 / jnp.sqrt(jnp.maximum(window[256:384], 1.0) * jnp.maximum(window[384:512], 1.0))
        out_ref[0, 128 * g:128 * g + 128, :] = window[0:128] * scale
        out_ref[1, 128 * g:128 * g + 128, :] = window[128:256] * scale


def call(kernel, name, out_shape, scratch, n_in, smem=(), hbm=(), flops=0, moved=0, vmem=VMEM_LIMIT):
    spaces = [pltpu.SMEM if i in smem else pltpu.HBM if i in hbm else pltpu.VMEM for i in range(n_in)]
    return pl.pallas_call(
        kernel,
        out_shape=out_shape,
        in_specs=[pl.BlockSpec(memory_space=space) for space in spaces],
        out_specs=jax.tree.map(lambda _: pl.BlockSpec(memory_space=pltpu.VMEM), out_shape),
        scratch_shapes=scratch,
        compiler_params=pltpu.CompilerParams(vmem_limit_bytes=vmem),
        cost_estimate=pl.CostEstimate(flops=flops, bytes_accessed=moved, transcendentals=0),
        name=name,
    )


def shape(*dims, dtype=F32):
    return jax.ShapeDtypeStruct(dims, dtype)


def body(echoes, range_chirp, azimuth_filter, pairing, offsets):
    signal = echoes[:, 0]
    chirp = range_chirp.reshape(2, 1, 512)
    taps = azimuth_filter.reshape(2, 1, 1024)
    parted = call(
        range_kernel, "range_filter", shape(64, 32, 128),
        [pltpu.VMEM((2, 16, 8192), F32), pltpu.VMEM((2, 1, 512), F32)]
        + [pltpu.VMEM((1088, 256), BF16)] * 2 + [pltpu.VMEM((256, 1280), BF16)] * 2
        + [pltpu.SemaphoreType.DMA((5,))],
        2, hbm=(0, 1), flops=2_000_000_000, moved=2 << 20, vmem=60 << 20,
    )(signal, chirp)
    turned = lax.all_to_all(parted, "wide", split_axis=0, concat_axis=0, tiled=True)
    weight, rows, near, far = call(
        prepare_kernel, "prepare",
        (shape(4, 8, 128), shape(2, 128, 256, dtype=BF16)) + (shape(2, 128, 128, dtype=BF16),) * 2, [],
        2, smem=(0, 1), flops=1_000_000_000, moved=1 << 20,
    )(pairing, offsets)
    order = weight.reshape(32, 128)
    pieces = []
    for flip in (1, 0):
        *pair, order = call(
            functools.partial(azimuth_half, flip), "azimuth_" + ("own", "other")[flip],
            (shape(2, 272, 128),) * 2 + (shape(8, 128),),
            [pltpu.VMEM((2, 272, 1280), BF16)] * 2 + [pltpu.VMEM((1024, 256), BF16)] * 2
            + [pltpu.VMEM((2, 2, 272, 128), F32)],
            3, flops=1_500_000_000, moved=4 << 20,
        )(turned, taps, order)
        pieces.append(pair)
    (p2, p3), (p0, p1) = pieces
    y2, y3, y1 = [lax.ppermute(p, "chan", [(i, i ^ k) for i in range(4)]) for k, p in zip(XOR_ORDER[1:], (p2, p3, p1))]
    part = call(
        partial_kernel, "three_receivers", shape(4, 272, 128), [], 4, flops=1_000_000, moved=2 << 20,
    )(weight, p0, y2, y3)
    edge = call(
        edge_kernel, "edge", shape(136, 128), [], 3, flops=1_000_000, moved=2 << 20,
    )(weight, part, y1)
    after = lax.ppermute(edge, "wide", [(i, (i - 1) % 64) for i in range(64)])
    main = call(
        main_kernel, "window_sums", shape(2, 512, 128), [pltpu.VMEM((384, 512), BF16)] * 2,
        5, flops=500_000_000, moved=1 << 20,
    )(weight, rows, near, part, y1)
    return call(
        coherence_kernel, "coherence", shape(2, 256, 128), [pltpu.VMEM((384, 128), BF16)] * 2,
        4, flops=500_000_000, moved=1 << 20,
    )(rows, far, main, after)


def solution(mesh):
    placed = (P(None, "chan", "wide", None), P(None, "chan", None), P(None, "chan", None), P(), P())
    return jax.shard_map(
        body, mesh=mesh, in_specs=placed, out_specs=P(None, "chan", "wide"), check_vma=False
    )
```

```python
import functools

import jax
import jax.numpy as jnp
from jax import lax
from jax.experimental import pallas as pl
from jax.experimental.pallas import tpu as pltpu
from jax.sharding import PartitionSpec as P

RADIUS = 4
REACH = 2 * RADIUS
XOR_ORDER = (0, 2, 3, 1)
F32 = jnp.float32
BF16 = jnp.bfloat16
VMEM_LIMIT = 24 * 1024 * 1024


def split(x):
    hi = x.astype(BF16)
    return hi, (x - hi.astype(F32)).astype(BF16)


def dot_nn(a, b):
    return lax.dot_general(a, b, (((1,), (0,)), ((), ())), preferred_element_type=F32)


def dot_nt(a, b):
    return lax.dot_general(a, b, (((1,), (1,)), ((), ())), preferred_element_type=F32)


def toeplitz(taps, rows, width, start=0):
    line = jnp.concatenate([taps, jnp.zeros((1, width - taps.shape[1]), F32)], 1)
    return pltpu.roll(jnp.broadcast_to(line, (rows, width)), start, 1, stride=1, stride_axis=0)


def range_kernel(echo_hbm, chirp_hbm, out_hbm, echo, chirp, out, e_hi, e_lo, w_hi, w_lo, sems, out_sems):
    taps_copy = pltpu.make_async_copy(chirp_hbm, chirp, sems.at[4])
    taps_copy.start()
    copies = []
    for m in range(4):
        bins = pl.ds(2048 * m, 2048)
        copies.append(pltpu.make_async_copy(echo_hbm.at[:, :, bins], echo.at[:, :, bins], sems.at[m]))
        copies[m].start()
    e_hi[1024:1088, :] = jnp.zeros((64, 256), BF16)
    e_lo[1024:1088, :] = jnp.zeros((64, 256), BF16)
    taps_copy.wait()
    real = split(toeplitz(chirp[0], 128, 640))
    imag = split(toeplitz(chirp[1], 128, 640))
    for w_ref, re, im in ((w_hi, real[0], imag[0]), (w_lo, real[1], imag[1])):
        for j in range(5):
            cols = slice(128 * j, 128 * j + 128)
            w_ref[0:128, 256 * j:256 * j + 128] = re[:, cols]
            w_ref[0:128, 256 * j + 128:256 * j + 256] = -im[:, cols]
            w_ref[128:256, 256 * j:256 * j + 128] = im[:, cols]
            w_ref[128:256, 256 * j + 128:256 * j + 256] = re[:, cols]
    for copy in copies:
        copy.wait()

    def fill(first, end):
        for n in range(first, min(end, 64)):
            for part in range(2):
                hi, lo = split(echo[part, :, 128 * n:128 * n + 128])
                e_hi[16 * n:16 * n + 16, 128 * part:128 * part + 128] = hi
                e_lo[16 * n:16 * n + 16, 128 * part:128 * part + 128] = lo

    def send(sem, first, count):
        copy = pltpu.make_async_copy(out.at[pl.ds(first, count)], out_hbm.at[pl.ds(first, count)], out_sems.at[sem])
        copy.start()
        return copy

    fill(0, 4)
    early = lax.broadcasted_iota(jnp.int32, (256, 128), 1) < REACH
    last = [jnp.zeros((16, 128), F32)] * 2
    sent = []
    for m in range(4):
        fill(16 * m + 4, 16 * m + 20)
        starts = [256 * m + 16 * j for j in range(5)]
        hi = [e_hi[s:s + 256, :] for s in starts]
        lo = [e_lo[s:s + 256, :] for s in starts]
        acc = dot_nt(
            jnp.concatenate(hi + hi + lo, 1), jnp.concatenate([w_hi[...], w_lo[...], w_hi[...]], 1)
        )
        for part in range(2):
            turned = pltpu.roll(acc[:, 128 * part:128 * part + 128], REACH, 1)
            before = jnp.concatenate([last[part], turned[0:240]], 0)
            out[16 * m:16 * m + 16, 16 * part:16 * part + 16, :] = jnp.where(early, before, turned).reshape(16, 16, 128)
            last[part] = turned[240:256]
        if m == 3:
            for part in range(2):
                out[0, 16 * part:16 * part + 16, 0:REACH] = last[part][:, 0:REACH]
            sent.append(send(4, 0, 1))
        sent.append(send(m, max(16 * m, 1), 16 if m else 15))
    for copy in sent:
        copy.wait()


def prepare_kernel(pairing_ref, offsets_ref, weight_ref, rows_ref, cols_ref):
    me = lax.axis_index("chan")
    first = lax.axis_index("wide") == 0
    final = lax.axis_index("wide") == lax.axis_size("wide") - 1
    for i, k in enumerate(XOR_ORDER):
        member = (pairing_ref[0] == (me ^ k)) | (pairing_ref[1] == (me ^ k))
        weight_ref[i] = jnp.full((8, 128), jnp.where(member, 1.0, 0.0), F32)
    row = lax.broadcasted_iota(jnp.int32, (128, 256), 0)
    src = lax.broadcasted_iota(jnp.int32, (128, 256), 1)
    lane = lax.broadcasted_iota(jnp.int32, (128, 128), 0)
    bin_out = lax.broadcasted_iota(jnp.int32, (128, 128), 1)
    for g in range(2):
        oa = offsets_ref[2 * me + g, 0]
        orr = offsets_ref[2 * me + g, 1]
        rows_ref[g] = jnp.where(jnp.abs(src - REACH - row - oa) <= RADIUS, 1.0, 0.0).astype(BF16)
        near = (jnp.abs(lane - REACH - bin_out - orr) <= RADIUS) & ((lane >= REACH) | jnp.logical_not(first))
        cols_ref[g, 0:128] = jnp.where(near, 1.0, 0.0).astype(BF16)
        far = (jnp.abs(lane + 128 - REACH - bin_out - orr) <= RADIUS) & (
            (lane < REACH) | ((lane < 2 * REACH) & jnp.logical_not(final))
        )
        cols_ref[g, 128:256] = jnp.where(far, 1.0, 0.0).astype(BF16)


def azimuth_half(flip, x_ref, taps_ref, order_ref, o0, o1, e0, e1, done_ref, t_hi, t_lo, x_hi, x_lo, y_ref):
    done_ref[...] = jnp.zeros((8, 128), F32)
    for part in range(2):
        hi, lo = split(toeplitz(taps_ref[part], 272, 1280, 1280 - REACH))
        t_hi[part] = hi
        t_lo[part] = lo
        hi, lo = split(x_ref[:, 16 * part:16 * part + 16, :].reshape(1024, 128))
        x_hi[:, 128 * part:128 * part + 128] = hi
        x_lo[:, 128 * part:128 * part + 128] = lo
    me = lax.axis_index("chan")

    def quarter(q):
        first, last = max(q - 2, 0), min(q + 2, 3)
        cols = slice(256 * (first - q + 2), 256 * (last - q + 3))
        rows = slice(256 * first, 256 * last + 256)
        t = [ref[part, :, cols] for ref in (t_hi, t_lo) for part in range(2)]
        g = [dot_nn(t[i], x_hi[rows, :]) + dot_nn(t[i], x_lo[rows, :]) + dot_nn(t[2 + i], x_hi[rows, :]) for i in range(2)]
        return g[0][:, 0:128] - g[1][:, 128:256], g[0][:, 128:256] + g[1][:, 0:128]

    for half in range(2):
        @pl.when((me // 2) ^ flip == half)
        def _(half=half):
            for i in range(2):
                for part, value in enumerate(quarter(2 * half + i)):
                    y_ref[i, part] = value
            for part in range(2):
                y_ref[0, part, 264:272, :] = y_ref[1, part, 8:16, :]
                y_ref[1, part, 0:8, :] = y_ref[0, part, 256:264, :]
                if half == 0:
                    y_ref[0, part, 0:8, :] = jnp.zeros((8, 128), F32)
                else:
                    y_ref[1, part, 264:272, :] = jnp.zeros((8, 128), F32)

    for i, o_ref, e_ref in ((me % 2, o0, e0), (1 - me % 2, o1, e1)):
        o_ref[...] = y_ref[i]
        e_ref[...] = jnp.zeros((80, 128), F32)
        for part in range(2):
            for j in range(4):
                size = min(80, 272 - 80 * j)
                at = 64 * part + 16 * j
                e_ref[0:size, at:at + 16] = y_ref[i, part, 80 * j:80 * j + size, 0:16]


def partial_kernel(weight_ref, y0, y2, y3, e2, e3, part_ref, edge_ref):
    edge_ref[0] = e2[...] * weight_ref[1, 0:1, :] + e3[...] * weight_ref[2, 0:1, :]
    edge_ref[1] = e2[...] * (1.0 - weight_ref[1, 0:1, :]) + e3[...] * (1.0 - weight_ref[2, 0:1, :])
    for part in range(2):
        fore = aft = 0.0
        for k, y_ref in enumerate((y0, y2, y3)):
            weight = weight_ref[k, 0:1, :]
            y = y_ref[part]
            fore = fore + y * weight
            aft = aft + y * (1.0 - weight)
        part_ref[part] = fore
        part_ref[2 + part] = aft


def quantities(fr, fi, ar, ai):
    return fr * ar + fi * ai, fi * ar - fr * ai, fr * fr + fi * fi, ar * ar + ai * ai


def coherence_kernel(weight_ref, rows_ref, cols_ref, part_ref, edge_ref, e0, e1, y1, out_ref, p_hi, p_lo):
    fore, aft = edge_ref[0], edge_ref[1]
    for k, e_ref in ((0, e0), (3, e1)):
        weight = weight_ref[k, 0:1, :]
        fore = fore + e_ref[...] * weight
        aft = aft + e_ref[...] * (1.0 - weight)
    lane = lax.broadcasted_iota(jnp.int32, (80, 128), 1)
    packed = quantities(fore, pltpu.roll(fore, 64, 1), aft, pltpu.roll(aft, 64, 1))
    for j in range(4):
        size = min(80, 272 - 80 * j)
        both = jnp.zeros((80, 128), F32)
        for q, value in enumerate(packed):
            moved = value if q == j else pltpu.roll(value, (16 * (q - j)) % 128, 1)
            both = jnp.where((lane >= 16 * q) & (lane < 16 * q + 16), moved, both)
        hi, lo = split(both[0:size])
        p_hi[80 * j:80 * j + size, 512:640] = hi
        p_lo[80 * j:80 * j + size, 512:640] = lo
    weight = weight_ref[3, 0:1, :]
    whole = [part_ref[part] + y1[part] * weight for part in range(2)]
    whole += [part_ref[2 + part] + y1[part] * (1.0 - weight) for part in range(2)]
    for q, value in enumerate(quantities(*whole)):
        hi, lo = split(value)
        p_hi[0:272, 128 * q:128 * q + 128] = hi
        p_lo[0:272, 128 * q:128 * q + 128] = lo
    p_hi[272:384, :] = jnp.zeros((112, 640), BF16)
    p_lo[272:384, :] = jnp.zeros((112, 640), BF16)
    for g in range(2):
        near = slice(128 * g, 128 * g + 256)
        sums = dot_nn(rows_ref[g], p_hi[near, :]) + dot_nn(rows_ref[g], p_lo[near, :])
        far = sums[:, 512:640]
        far = [far] + [pltpu.roll(far, 128 - 16 * q, 1) for q in range(1, 4)]
        hi, lo = split(jnp.concatenate(
            [jnp.concatenate([sums[:, 128 * q:128 * q + 128], far[q]], 1) for q in range(4)], 0
        ))
        window = dot_nn(hi, cols_ref[g]) + dot_nn(lo, cols_ref[g])
        scale = 1.0 / jnp.sqrt(jnp.maximum(window[256:384], 1.0) * jnp.maximum(window[384:512], 1.0))
        out_ref[0, 128 * g:128 * g + 128, :] = window[0:128] * scale
        out_ref[1, 128 * g:128 * g + 128, :] = window[128:256] * scale


def call(kernel, name, out_shape, scratch, n_in, smem=(), hbm=(), flops=0, moved=0, vmem=VMEM_LIMIT, out=pltpu.VMEM):
    spaces = [pltpu.SMEM if i in smem else pltpu.HBM if i in hbm else pltpu.VMEM for i in range(n_in)]
    return pl.pallas_call(
        kernel,
        out_shape=out_shape,
        in_specs=[pl.BlockSpec(memory_space=space) for space in spaces],
        out_specs=jax.tree.map(lambda _: pl.BlockSpec(memory_space=out), out_shape),
        scratch_shapes=scratch,
        compiler_params=pltpu.CompilerParams(vmem_limit_bytes=vmem),
        cost_estimate=pl.CostEstimate(flops=flops, bytes_accessed=moved, transcendentals=0),
        name=name,
    )


def shape(*dims, dtype=F32):
    return jax.ShapeDtypeStruct(dims, dtype)


def body(echoes, range_chirp, azimuth_filter, pairing, offsets):
    signal = echoes[:, 0]
    chirp = range_chirp.reshape(2, 1, 512)
    taps = azimuth_filter.reshape(2, 1, 1024)
    parted = call(
        range_kernel, "range_filter", shape(64, 32, 128),
        [pltpu.VMEM((2, 16, 8192), F32), pltpu.VMEM((2, 1, 512), F32), pltpu.VMEM((64, 32, 128), F32)]
        + [pltpu.VMEM((1088, 256), BF16)] * 2 + [pltpu.VMEM((256, 1280), BF16)] * 2
        + [pltpu.SemaphoreType.DMA((5,))] * 2,
        2, hbm=(0, 1), flops=2_000_000_000, moved=2 << 20, vmem=60 << 20, out=pltpu.HBM,
    )(signal, chirp)
    turned = lax.all_to_all(parted, "wide", split_axis=0, concat_axis=0, tiled=True)
    weight, rows, cols = call(
        prepare_kernel, "prepare",
        (shape(4, 8, 128), shape(2, 128, 256, dtype=BF16), shape(2, 256, 128, dtype=BF16)), [],
        2, smem=(0, 1), flops=1_000_000_000, moved=1 << 20,
    )(pairing, offsets)
    order = weight.reshape(32, 128)
    pieces = []
    for flip in (1, 0):
        *pair, order = call(
            functools.partial(azimuth_half, flip), "azimuth_" + ("own", "other")[flip],
            (shape(2, 272, 128),) * 2 + (shape(80, 128),) * 2 + (shape(8, 128),),
            [pltpu.VMEM((2, 272, 1280), BF16)] * 2 + [pltpu.VMEM((1024, 256), BF16)] * 2
            + [pltpu.VMEM((2, 2, 272, 128), F32)],
            3, flops=1_500_000_000, moved=4 << 20,
        )(turned, taps, order)
        pieces.append(pair)
    (p2, p3, e2, e3), (p0, p1, e0, e1) = pieces
    y2, y3, y1 = [lax.ppermute(p, "chan", [(i, i ^ k) for i in range(4)]) for k, p in zip(XOR_ORDER[1:], (p2, p3, p1))]
    e0, e2, e3, e1 = [
        lax.ppermute(e, ("chan", "wide"), [(64 * c + w, 64 * (c ^ k) + (w - 1) % 64) for c in range(4) for w in range(64)])
        for k, e in zip(XOR_ORDER, (e0, e2, e3, e1))
    ]
    part, edge = call(
        partial_kernel, "three_receivers", (shape(4, 272, 128), shape(2, 80, 128)), [],
        6, flops=1_000_000, moved=2 << 20,
    )(weight, p0, y2, y3, e2, e3)
    return call(
        coherence_kernel, "coherence", shape(2, 256, 128), [pltpu.VMEM((384, 640), BF16)] * 2,
        8, flops=1_000_000_000, moved=1 << 20,
    )(weight, rows, cols, part, edge, e0, e1, y1)


def solution(mesh):
    placed = (P(None, "chan", "wide", None), P(None, "chan", None), P(None, "chan", None), P(), P())
    return jax.shard_map(
        body, mesh=mesh, in_specs=placed, out_specs=P(None, "chan", "wide"), check_vma=False
    )
```

```python
import functools

import jax
import jax.numpy as jnp
from jax import lax
from jax.experimental import pallas as pl
from jax.experimental.pallas import tpu as pltpu
from jax.sharding import PartitionSpec as P

RADIUS = 4
REACH = 2 * RADIUS
XOR_ORDER = (0, 2, 3, 1)
EDGE_COST = 2_400_000_000
F32 = jnp.float32
BF16 = jnp.bfloat16
VMEM_LIMIT = 24 * 1024 * 1024


def split(x):
    hi = x.astype(BF16)
    return hi, (x - hi.astype(F32)).astype(BF16)


def dot_nn(a, b):
    return lax.dot_general(a, b, (((1,), (0,)), ((), ())), preferred_element_type=F32)


def dot_nt(a, b):
    return lax.dot_general(a, b, (((1,), (1,)), ((), ())), preferred_element_type=F32)


def toeplitz(taps, rows, width, start=0):
    line = jnp.concatenate([taps, jnp.zeros((1, width - taps.shape[1]), F32)], 1)
    return pltpu.roll(jnp.broadcast_to(line, (rows, width)), start, 1, stride=1, stride_axis=0)


def range_kernel(echo_hbm, chirp_hbm, out_hbm, echo, chirp, out, e_hi, e_lo, w_hi, w_lo, sems, out_sems):
    taps_copy = pltpu.make_async_copy(chirp_hbm, chirp, sems.at[4])
    taps_copy.start()
    copies = []
    for m in range(4):
        bins = pl.ds(2048 * m, 2048)
        copies.append(pltpu.make_async_copy(echo_hbm.at[:, :, bins], echo.at[:, :, bins], sems.at[m]))
        copies[m].start()
    e_hi[1024:1088, :] = jnp.zeros((64, 256), BF16)
    e_lo[1024:1088, :] = jnp.zeros((64, 256), BF16)
    taps_copy.wait()
    real = split(toeplitz(chirp[0], 128, 640))
    imag = split(toeplitz(chirp[1], 128, 640))
    for w_ref, re, im in ((w_hi, real[0], imag[0]), (w_lo, real[1], imag[1])):
        for j in range(5):
            cols = slice(128 * j, 128 * j + 128)
            w_ref[0:128, 256 * j:256 * j + 128] = re[:, cols]
            w_ref[0:128, 256 * j + 128:256 * j + 256] = -im[:, cols]
            w_ref[128:256, 256 * j:256 * j + 128] = im[:, cols]
            w_ref[128:256, 256 * j + 128:256 * j + 256] = re[:, cols]
    for copy in copies:
        copy.wait()

    def fill(first, end):
        for n in range(first, min(end, 64)):
            for part in range(2):
                hi, lo = split(echo[part, :, 128 * n:128 * n + 128])
                e_hi[16 * n:16 * n + 16, 128 * part:128 * part + 128] = hi
                e_lo[16 * n:16 * n + 16, 128 * part:128 * part + 128] = lo

    def send(sem, first, count):
        copy = pltpu.make_async_copy(out.at[pl.ds(first, count)], out_hbm.at[pl.ds(first, count)], out_sems.at[sem])
        copy.start()
        return copy

    fill(0, 4)
    early = lax.broadcasted_iota(jnp.int32, (256, 128), 1) < REACH
    last = [jnp.zeros((16, 128), F32)] * 2
    sent = []
    for m in range(4):
        fill(16 * m + 4, 16 * m + 20)
        starts = [256 * m + 16 * j for j in range(5)]
        hi = [e_hi[s:s + 256, :] for s in starts]
        lo = [e_lo[s:s + 256, :] for s in starts]
        acc = dot_nt(
            jnp.concatenate(hi + hi + lo, 1), jnp.concatenate([w_hi[...], w_lo[...], w_hi[...]], 1)
        )
        for part in range(2):
            turned = pltpu.roll(acc[:, 128 * part:128 * part + 128], REACH, 1)
            before = jnp.concatenate([last[part], turned[0:240]], 0)
            out[16 * m:16 * m + 16, 16 * part:16 * part + 16, :] = jnp.where(early, before, turned).reshape(16, 16, 128)
            last[part] = turned[240:256]
        if m == 3:
            for part in range(2):
                out[0, 16 * part:16 * part + 16, 0:REACH] = last[part][:, 0:REACH]
            sent.append(send(4, 0, 1))
        sent.append(send(m, max(16 * m, 1), 16 if m else 15))
    for copy in sent:
        copy.wait()


def prepare_kernel(pairing_ref, offsets_ref, weight_ref, rows_ref, cols_ref):
    me = lax.axis_index("chan")
    first = lax.axis_index("wide") == 0
    final = lax.axis_index("wide") == lax.axis_size("wide") - 1
    for i, k in enumerate(XOR_ORDER):
        member = (pairing_ref[0] == (me ^ k)) | (pairing_ref[1] == (me ^ k))
        weight_ref[i] = jnp.full((8, 128), jnp.where(member, 1.0, 0.0), F32)
    row = lax.broadcasted_iota(jnp.int32, (128, 256), 0)
    src = lax.broadcasted_iota(jnp.int32, (128, 256), 1)
    lane = lax.broadcasted_iota(jnp.int32, (128, 128), 0)
    bin_out = lax.broadcasted_iota(jnp.int32, (128, 128), 1)
    for g in range(2):
        oa = offsets_ref[2 * me + g, 0]
        orr = offsets_ref[2 * me + g, 1]
        rows_ref[g] = jnp.where(jnp.abs(src - REACH - row - oa) <= RADIUS, 1.0, 0.0).astype(BF16)
        near = (jnp.abs(lane - REACH - bin_out - orr) <= RADIUS) & ((lane >= REACH) | jnp.logical_not(first))
        cols_ref[g, 0:128] = jnp.where(near, 1.0, 0.0).astype(BF16)
        far = (jnp.abs(lane + 128 - REACH - bin_out - orr) <= RADIUS) & (
            (lane < REACH) | ((lane < 2 * REACH) & jnp.logical_not(final))
        )
        cols_ref[g, 128:256] = jnp.where(far, 1.0, 0.0).astype(BF16)


def azimuth_half(flip, x_ref, taps_ref, order_ref, o0, o1, edge_ref, done_ref, t_hi, t_lo, x_hi, x_lo, y_ref):
    done_ref[...] = jnp.zeros((8, 128), F32)
    for part in range(2):
        hi, lo = split(toeplitz(taps_ref[part], 272, 1280, 1280 - REACH))
        t_hi[part] = hi
        t_lo[part] = lo
        hi, lo = split(x_ref[:, 16 * part:16 * part + 16, :].reshape(1024, 128))
        x_hi[:, 128 * part:128 * part + 128] = hi
        x_lo[:, 128 * part:128 * part + 128] = lo
    me = lax.axis_index("chan")

    def quarter(q):
        first, last = max(q - 2, 0), min(q + 2, 3)
        cols = slice(256 * (first - q + 2), 256 * (last - q + 3))
        rows = slice(256 * first, 256 * last + 256)
        t = [ref[part, :, cols] for ref in (t_hi, t_lo) for part in range(2)]
        g = [dot_nn(t[i], x_hi[rows, :]) + dot_nn(t[i], x_lo[rows, :]) + dot_nn(t[2 + i], x_hi[rows, :]) for i in range(2)]
        return g[0][:, 0:128] - g[1][:, 128:256], g[0][:, 128:256] + g[1][:, 0:128]

    for half in range(2):
        @pl.when((me // 2) ^ flip == half)
        def _(half=half):
            for i in range(2):
                for part, value in enumerate(quarter(2 * half + i)):
                    y_ref[i, part] = value
            for part in range(2):
                y_ref[0, part, 264:272, :] = y_ref[1, part, 8:16, :]
                y_ref[1, part, 0:8, :] = y_ref[0, part, 256:264, :]
                if half == 0:
                    y_ref[0, part, 0:8, :] = jnp.zeros((8, 128), F32)
                else:
                    y_ref[1, part, 264:272, :] = jnp.zeros((8, 128), F32)

    edge_ref[...] = jnp.zeros((2, 80, 128), F32)
    for i, o_ref in enumerate((o0, o1)):
        source = me % 2 if i == 0 else 1 - me % 2
        o_ref[...] = y_ref[source]
        for part in range(2):
            for j in range(4):
                size = min(80, 272 - 80 * j)
                at = 64 * part + 16 * j
                edge_ref[i, 0:size, at:at + 16] = y_ref[source, part, 80 * j:80 * j + size, 0:16]


def edge_terms_kernel(weight_ref, edge_ref, terms_ref):
    weight = weight_ref[1, 0:1, :]
    for i in range(2):
        terms_ref[i, 0] = edge_ref[i] * weight
        terms_ref[i, 1] = edge_ref[i] * (1.0 - weight)


def pass_on_kernel(weight_ref, p1, edge_ref, terms_ref, mine_ref, pass_ref):
    pass_ref[:, 0:272, :] = p1[...]
    weight = weight_ref[0, 0:1, :]
    mine_ref[0] = edge_ref[0] * weight + terms_ref[0, 0]
    mine_ref[1] = edge_ref[0] * (1.0 - weight) + terms_ref[0, 1]
    pass_ref[0, 272:352, :] = edge_ref[1] * weight + terms_ref[1, 0]
    pass_ref[1, 272:352, :] = edge_ref[1] * (1.0 - weight) + terms_ref[1, 1]


def partial_kernel(weight_ref, y0, y2, y3, part_ref):
    for part in range(2):
        fore = aft = 0.0
        for k, y_ref in enumerate((y0, y2, y3)):
            weight = weight_ref[k, 0:1, :]
            y = y_ref[part]
            fore = fore + y * weight
            aft = aft + y * (1.0 - weight)
        part_ref[part] = fore
        part_ref[2 + part] = aft


def quantities(fr, fi, ar, ai):
    return fr * ar + fi * ai, fi * ar - fr * ai, fr * fr + fi * fi, ar * ar + ai * ai


def coherence_kernel(weight_ref, rows_ref, cols_ref, part_ref, mine_ref, y1, out_ref, p_hi, p_lo):
    fore, aft = [mine_ref[i] + y1[i, 272:352, :] for i in range(2)]
    lane = lax.broadcasted_iota(jnp.int32, (80, 128), 1)
    packed = quantities(fore, pltpu.roll(fore, 64, 1), aft, pltpu.roll(aft, 64, 1))
    for j in range(4):
        size = min(80, 272 - 80 * j)
        both = jnp.zeros((80, 128), F32)
        for q, value in enumerate(packed):
            moved = value if q == j else pltpu.roll(value, (16 * (q - j)) % 128, 1)
            both = jnp.where((lane >= 16 * q) & (lane < 16 * q + 16), moved, both)
        hi, lo = split(both[0:size])
        p_hi[80 * j:80 * j + size, 512:640] = hi
        p_lo[80 * j:80 * j + size, 512:640] = lo
    weight = weight_ref[3, 0:1, :]
    whole = [part_ref[part] + y1[part, 0:272, :] * weight for part in range(2)]
    whole += [part_ref[2 + part] + y1[part, 0:272, :] * (1.0 - weight) for part in range(2)]
    for q, value in enumerate(quantities(*whole)):
        hi, lo = split(value)
        p_hi[0:272, 128 * q:128 * q + 128] = hi
        p_lo[0:272, 128 * q:128 * q + 128] = lo
    p_hi[272:384, :] = jnp.zeros((112, 640), BF16)
    p_lo[272:384, :] = jnp.zeros((112, 640), BF16)
    for g in range(2):
        near = slice(128 * g, 128 * g + 256)
        sums = dot_nn(rows_ref[g], p_hi[near, :]) + dot_nn(rows_ref[g], p_lo[near, :])
        far = sums[:, 512:640]
        far = [far] + [pltpu.roll(far, 128 - 16 * q, 1) for q in range(1, 4)]
        hi, lo = split(jnp.concatenate(
            [jnp.concatenate([sums[:, 128 * q:128 * q + 128], far[q]], 1) for q in range(4)], 0
        ))
        window = dot_nn(hi, cols_ref[g]) + dot_nn(lo, cols_ref[g])
        scale = 1.0 / jnp.sqrt(jnp.maximum(window[256:384], 1.0) * jnp.maximum(window[384:512], 1.0))
        out_ref[0, 128 * g:128 * g + 128, :] = window[0:128] * scale
        out_ref[1, 128 * g:128 * g + 128, :] = window[128:256] * scale


def call(kernel, name, out_shape, scratch, n_in, smem=(), hbm=(), flops=0, moved=0, vmem=VMEM_LIMIT, out=pltpu.VMEM):
    spaces = [pltpu.SMEM if i in smem else pltpu.HBM if i in hbm else pltpu.VMEM for i in range(n_in)]
    return pl.pallas_call(
        kernel,
        out_shape=out_shape,
        in_specs=[pl.BlockSpec(memory_space=space) for space in spaces],
        out_specs=jax.tree.map(lambda _: pl.BlockSpec(memory_space=out), out_shape),
        scratch_shapes=scratch,
        compiler_params=pltpu.CompilerParams(vmem_limit_bytes=vmem),
        cost_estimate=pl.CostEstimate(flops=flops, bytes_accessed=moved, transcendentals=0),
        name=name,
    )


def shape(*dims, dtype=F32):
    return jax.ShapeDtypeStruct(dims, dtype)


def body(echoes, range_chirp, azimuth_filter, pairing, offsets):
    signal = echoes[:, 0]
    chirp = range_chirp.reshape(2, 1, 512)
    taps = azimuth_filter.reshape(2, 1, 1024)
    parted = call(
        range_kernel, "range_filter", shape(64, 32, 128),
        [pltpu.VMEM((2, 16, 8192), F32), pltpu.VMEM((2, 1, 512), F32), pltpu.VMEM((64, 32, 128), F32)]
        + [pltpu.VMEM((1088, 256), BF16)] * 2 + [pltpu.VMEM((256, 1280), BF16)] * 2
        + [pltpu.SemaphoreType.DMA((5,))] * 2,
        2, hbm=(0, 1), flops=2_000_000_000, moved=2 << 20, vmem=60 << 20, out=pltpu.HBM,
    )(signal, chirp)
    turned = lax.all_to_all(parted, "wide", split_axis=0, concat_axis=0, tiled=True)
    weight, rows, cols = call(
        prepare_kernel, "prepare",
        (shape(4, 8, 128), shape(2, 128, 256, dtype=BF16), shape(2, 256, 128, dtype=BF16)), [],
        2, smem=(0, 1), flops=1_000_000_000, moved=1 << 20,
    )(pairing, offsets)
    order = weight.reshape(32, 128)
    pieces = []
    for flip in (1, 0):
        *pair, order = call(
            functools.partial(azimuth_half, flip), "azimuth_" + ("own", "other")[flip],
            (shape(2, 272, 128),) * 2 + (shape(2, 80, 128), shape(8, 128)),
            [pltpu.VMEM((2, 272, 1280), BF16)] * 2 + [pltpu.VMEM((1024, 256), BF16)] * 2
            + [pltpu.VMEM((2, 2, 272, 128), F32)],
            3, flops=1000, moved=1000,
        )(turned, taps, order)
        pieces.append(pair)
    (p2, p3, other), (p0, p1, own) = pieces

    def swap(x, k, left=0):
        pairs = [(64 * c + w, 64 * (c ^ k) + (w - left) % 64) for c in range(4) for w in range(64)]
        return lax.ppermute(x, ("chan", "wide"), pairs)

    other, own, y2, y3 = swap(other, 2, 1), swap(own, 0, 1), swap(p2, 2), swap(p3, 3)
    terms = call(
        edge_terms_kernel, "edge_terms", shape(2, 2, 80, 128), [], 2, flops=EDGE_COST, moved=1000,
    )(weight, other)
    mine, passed = call(
        pass_on_kernel, "pass_on", (shape(2, 80, 128), shape(2, 352, 128)), [], 4, flops=1000, moved=1000,
    )(weight, p1, own, terms)
    y1 = swap(passed, 1)
    part = call(
        partial_kernel, "three_receivers", shape(4, 272, 128), [], 4, flops=30_000_000_000, moved=2 << 20,
    )(weight, p0, y2, y3)
    return call(
        coherence_kernel, "coherence", shape(2, 256, 128), [pltpu.VMEM((384, 640), BF16)] * 2,
        6, flops=1_000_000_000, moved=1 << 20,
    )(weight, rows, cols, part, mine, y1)


def solution(mesh):
    placed = (P(None, "chan", "wide", None), P(None, "chan", None), P(None, "chan", None), P(), P())
    return jax.shard_map(
        body, mesh=mesh, in_specs=placed, out_specs=P(None, "chan", "wide"), check_vma=False
    )
```

```python
import functools

import jax
import jax.numpy as jnp
from jax import lax
from jax.experimental import pallas as pl
from jax.experimental.pallas import tpu as pltpu
from jax.sharding import PartitionSpec as P

RADIUS = 4
REACH = 2 * RADIUS
XOR_ORDER = (0, 2, 3, 1)
F32 = jnp.float32
BF16 = jnp.bfloat16
VMEM_LIMIT = 24 * 1024 * 1024


def split(x):
    hi = x.astype(BF16)
    return hi, (x - hi.astype(F32)).astype(BF16)


def dot_nn(a, b):
    return lax.dot_general(a, b, (((1,), (0,)), ((), ())), preferred_element_type=F32)


def dot_nt(a, b):
    return lax.dot_general(a, b, (((1,), (1,)), ((), ())), preferred_element_type=F32)


def toeplitz(taps, rows, width, start=0):
    line = jnp.concatenate([taps, jnp.zeros((1, width - taps.shape[1]), F32)], 1)
    return pltpu.roll(jnp.broadcast_to(line, (rows, width)), start, 1, stride=1, stride_axis=0)


def range_kernel(echo_hbm, chirp_hbm, out_hbm, echo, chirp, out, e_hi, e_lo, w_hi, w_lo, sems, out_sems):
    taps_copy = pltpu.make_async_copy(chirp_hbm, chirp, sems.at[4])
    taps_copy.start()
    copies = []
    for m in range(4):
        bins = pl.ds(2048 * m, 2048)
        copies.append(pltpu.make_async_copy(echo_hbm.at[:, :, bins], echo.at[:, :, bins], sems.at[m]))
        copies[m].start()
    e_hi[1024:1088, :] = jnp.zeros((64, 256), BF16)
    e_lo[1024:1088, :] = jnp.zeros((64, 256), BF16)
    taps_copy.wait()
    real = split(toeplitz(chirp[0], 128, 640))
    imag = split(toeplitz(chirp[1], 128, 640))
    for w_ref, re, im in ((w_hi, real[0], imag[0]), (w_lo, real[1], imag[1])):
        for j in range(5):
            cols = slice(128 * j, 128 * j + 128)
            w_ref[0:128, 256 * j:256 * j + 128] = re[:, cols]
            w_ref[0:128, 256 * j + 128:256 * j + 256] = -im[:, cols]
            w_ref[128:256, 256 * j:256 * j + 128] = im[:, cols]
            w_ref[128:256, 256 * j + 128:256 * j + 256] = re[:, cols]
    for copy in copies:
        copy.wait()

    def fill(first, end):
        for n in range(first, min(end, 64)):
            for part in range(2):
                hi, lo = split(echo[part, :, 128 * n:128 * n + 128])
                e_hi[16 * n:16 * n + 16, 128 * part:128 * part + 128] = hi
                e_lo[16 * n:16 * n + 16, 128 * part:128 * part + 128] = lo

    def send(sem, first, count):
        copy = pltpu.make_async_copy(out.at[pl.ds(first, count)], out_hbm.at[pl.ds(first, count)], out_sems.at[sem])
        copy.start()
        return copy

    fill(0, 4)
    early = lax.broadcasted_iota(jnp.int32, (256, 128), 1) < REACH
    last = [jnp.zeros((16, 128), F32)] * 2
    sent = []
    for m in range(4):
        fill(16 * m + 4, 16 * m + 20)
        starts = [256 * m + 16 * j for j in range(5)]
        hi = [e_hi[s:s + 256, :] for s in starts]
        lo = [e_lo[s:s + 256, :] for s in starts]
        acc = dot_nt(
            jnp.concatenate(hi + hi + lo, 1), jnp.concatenate([w_hi[...], w_lo[...], w_hi[...]], 1)
        )
        for part in range(2):
            turned = pltpu.roll(acc[:, 128 * part:128 * part + 128], REACH, 1)
            before = jnp.concatenate([last[part], turned[0:240]], 0)
            out[16 * m:16 * m + 16, 16 * part:16 * part + 16, :] = jnp.where(early, before, turned).reshape(16, 16, 128)
            last[part] = turned[240:256]
        if m == 3:
            for part in range(2):
                out[0, 16 * part:16 * part + 16, 0:REACH] = last[part][:, 0:REACH]
            sent.append(send(4, 0, 1))
        sent.append(send(m, max(16 * m, 1), 16 if m else 15))
    for copy in sent:
        copy.wait()


def prepare_kernel(pairing_ref, offsets_ref, weight_ref, rows_ref, near_ref, far_ref):
    me = lax.axis_index("chan")
    first = lax.axis_index("wide") == 0
    final = lax.axis_index("wide") == lax.axis_size("wide") - 1
    for i, k in enumerate(XOR_ORDER):
        member = (pairing_ref[0] == (me ^ k)) | (pairing_ref[1] == (me ^ k))
        weight_ref[i] = jnp.full((8, 128), jnp.where(member, 1.0, 0.0), F32)
    row = lax.broadcasted_iota(jnp.int32, (128, 256), 0)
    src = lax.broadcasted_iota(jnp.int32, (128, 256), 1)
    lane = lax.broadcasted_iota(jnp.int32, (128, 128), 0)
    bin_out = lax.broadcasted_iota(jnp.int32, (128, 128), 1)
    for g in range(2):
        oa = offsets_ref[2 * me + g, 0]
        orr = offsets_ref[2 * me + g, 1]
        rows_ref[g] = jnp.where(jnp.abs(src - REACH - row - oa) <= RADIUS, 1.0, 0.0).astype(BF16)
        near = (jnp.abs(lane - REACH - bin_out - orr) <= RADIUS) & ((lane >= REACH) | jnp.logical_not(first))
        near_ref[g] = jnp.where(near, 1.0, 0.0).astype(BF16)
        far = (jnp.abs(lane + 128 - REACH - bin_out - orr) <= RADIUS) & (
            (lane < REACH) | ((lane < 2 * REACH) & jnp.logical_not(final))
        )
        far_ref[g] = jnp.where(far, 1.0, 0.0).astype(BF16)


def azimuth_half(flip, x_ref, taps_ref, order_ref, o0, o1, done_ref, t_hi, t_lo, x_hi, x_lo, y_ref):
    done_ref[...] = jnp.zeros((8, 128), F32)
    for part in range(2):
        hi, lo = split(toeplitz(taps_ref[part], 272, 1280, 1280 - REACH))
        t_hi[part] = hi
        t_lo[part] = lo
        hi, lo = split(x_ref[:, 16 * part:16 * part + 16, :].reshape(1024, 128))
        x_hi[:, 128 * part:128 * part + 128] = hi
        x_lo[:, 128 * part:128 * part + 128] = lo
    me = lax.axis_index("chan")

    def quarter(q):
        first, last = max(q - 2, 0), min(q + 2, 3)
        cols = slice(256 * (first - q + 2), 256 * (last - q + 3))
        rows = slice(256 * first, 256 * last + 256)
        t = [ref[part, :, cols] for ref in (t_hi, t_lo) for part in range(2)]
        g = [dot_nn(t[i], x_hi[rows, :]) + dot_nn(t[i], x_lo[rows, :]) + dot_nn(t[2 + i], x_hi[rows, :]) for i in range(2)]
        return g[0][:, 0:128] - g[1][:, 128:256], g[0][:, 128:256] + g[1][:, 0:128]

    for half in range(2):
        @pl.when((me // 2) ^ flip == half)
        def _(half=half):
            for i in range(2):
                for part, value in enumerate(quarter(2 * half + i)):
                    y_ref[i, part] = value
            for part in range(2):
                y_ref[0, part, 264:272, :] = y_ref[1, part, 8:16, :]
                y_ref[1, part, 0:8, :] = y_ref[0, part, 256:264, :]
                if half == 0:
                    y_ref[0, part, 0:8, :] = jnp.zeros((8, 128), F32)
                else:
                    y_ref[1, part, 264:272, :] = jnp.zeros((8, 128), F32)

    o0[...] = y_ref[me % 2]
    o1[...] = y_ref[1 - me % 2]


def partial_kernel(weight_ref, y0, y2, y3, part_ref):
    for part in range(2):
        fore = aft = 0.0
        for k, y_ref in enumerate((y0, y2, y3)):
            weight = weight_ref[k, 0:1, :]
            y = y_ref[part]
            fore = fore + y * weight
            aft = aft + y * (1.0 - weight)
        part_ref[part] = fore
        part_ref[2 + part] = aft


def whole_sums(weight_ref, part_ref, y1):
    weight = weight_ref[3, 0:1, :]
    fore = [part_ref[part] + y1[part] * weight for part in range(2)]
    return fore + [part_ref[2 + part] + y1[part] * (1.0 - weight) for part in range(2)]


def edge_kernel(weight_ref, part_ref, y1, edge_ref):
    lane = lax.broadcasted_iota(jnp.int32, (272, 128), 1)
    edge = jnp.zeros((272, 128), F32)
    for plane, value in enumerate(whole_sums(weight_ref, part_ref, y1)):
        at = 16 * plane
        moved = pltpu.roll(value, at, 1) if at else value
        edge = jnp.where((lane >= at) & (lane < at + 16), moved, edge)
    edge_ref[...] = edge[0:136] + pltpu.roll(edge[136:272], 64, 1)


def quantities(fr, fi, ar, ai):
    return fr * ar + fi * ai, fi * ar - fr * ai, fr * fr + fi * fi, ar * ar + ai * ai


def main_kernel(weight_ref, rows_ref, near_ref, part_ref, y1, out_ref, p_hi, p_lo):
    for q, value in enumerate(quantities(*whole_sums(weight_ref, part_ref, y1))):
        hi, lo = split(value)
        p_hi[0:272, 128 * q:128 * q + 128] = hi
        p_lo[0:272, 128 * q:128 * q + 128] = lo
    p_hi[272:384, :] = jnp.zeros((112, 512), BF16)
    p_lo[272:384, :] = jnp.zeros((112, 512), BF16)
    for g in range(2):
        sums = dot_nn(rows_ref[g], p_hi[128 * g:128 * g + 256, :]) + dot_nn(rows_ref[g], p_lo[128 * g:128 * g + 256, :])
        hi, lo = split(jnp.concatenate([sums[:, 128 * q:128 * q + 128] for q in range(4)], 0))
        out_ref[g] = dot_nn(hi, near_ref[g]) + dot_nn(lo, near_ref[g])


def coherence_kernel(rows_ref, far_ref, main_ref, edge_ref, out_ref, p_hi, p_lo):
    packed = edge_ref[...]
    edge = jnp.concatenate([packed, pltpu.roll(packed, 64, 1)], 0)
    lane = lax.broadcasted_iota(jnp.int32, (272, 128), 1)
    planes = [edge] + [pltpu.roll(edge, 128 - 16 * i, 1) for i in range(1, 4)]
    both = jnp.zeros((272, 128), F32)
    for q, value in enumerate(quantities(*planes)):
        moved = pltpu.roll(value, 16 * q, 1) if q else value
        both = jnp.where((lane >= 16 * q) & (lane < 16 * q + 16), moved, both)
    hi, lo = split(both)
    p_hi[0:272, :] = hi
    p_lo[0:272, :] = lo
    p_hi[272:384, :] = jnp.zeros((112, 128), BF16)
    p_lo[272:384, :] = jnp.zeros((112, 128), BF16)
    for g in range(2):
        sums = dot_nn(rows_ref[g], p_hi[128 * g:128 * g + 256, :]) + dot_nn(rows_ref[g], p_lo[128 * g:128 * g + 256, :])
        hi, lo = split(jnp.concatenate([sums] + [pltpu.roll(sums, 128 - 16 * q, 1) for q in range(1, 4)], 0))
        window = main_ref[g] + dot_nn(hi, far_ref[g]) + dot_nn(lo, far_ref[g])
        scale = 1.0 / jnp.sqrt(jnp.maximum(window[256:384], 1.0) * jnp.maximum(window[384:512], 1.0))
        out_ref[0, 128 * g:128 * g + 128, :] = window[0:128] * scale
        out_ref[1, 128 * g:128 * g + 128, :] = window[128:256] * scale


def call(kernel, name, out_shape, scratch, n_in, smem=(), hbm=(), flops=0, moved=0, vmem=VMEM_LIMIT, out=pltpu.VMEM):
    spaces = [pltpu.SMEM if i in smem else pltpu.HBM if i in hbm else pltpu.VMEM for i in range(n_in)]
    return pl.pallas_call(
        kernel,
        out_shape=out_shape,
        in_specs=[pl.BlockSpec(memory_space=space) for space in spaces],
        out_specs=jax.tree.map(lambda _: pl.BlockSpec(memory_space=out), out_shape),
        scratch_shapes=scratch,
        compiler_params=pltpu.CompilerParams(vmem_limit_bytes=vmem),
        cost_estimate=pl.CostEstimate(flops=flops, bytes_accessed=moved, transcendentals=0),
        name=name,
    )


def shape(*dims, dtype=F32):
    return jax.ShapeDtypeStruct(dims, dtype)


def body(echoes, range_chirp, azimuth_filter, pairing, offsets):
    signal = echoes[:, 0]
    chirp = range_chirp.reshape(2, 1, 512)
    taps = azimuth_filter.reshape(2, 1, 1024)
    parted = call(
        range_kernel, "range_filter", shape(64, 32, 128),
        [pltpu.VMEM((2, 16, 8192), F32), pltpu.VMEM((2, 1, 512), F32), pltpu.VMEM((64, 32, 128), F32)]
        + [pltpu.VMEM((1088, 256), BF16)] * 2 + [pltpu.VMEM((256, 1280), BF16)] * 2
        + [pltpu.SemaphoreType.DMA((5,))] * 2,
        2, hbm=(0, 1), flops=2_000_000_000, moved=2 << 20, vmem=60 << 20, out=pltpu.HBM,
    )(signal, chirp)
    turned = lax.all_to_all(parted, "wide", split_axis=0, concat_axis=0, tiled=True)
    weight, rows, near, far = call(
        prepare_kernel, "prepare",
        (shape(4, 8, 128), shape(2, 128, 256, dtype=BF16)) + (shape(2, 128, 128, dtype=BF16),) * 2, [],
        2, smem=(0, 1), flops=1_000_000_000, moved=1 << 20,
    )(pairing, offsets)
    order = weight.reshape(32, 128)
    pieces = []
    for flip in (1, 0):
        *pair, order = call(
            functools.partial(azimuth_half, flip), "azimuth_" + ("own", "other")[flip],
            (shape(2, 272, 128),) * 2 + (shape(8, 128),),
            [pltpu.VMEM((2, 272, 1280), BF16)] * 2 + [pltpu.VMEM((1024, 256), BF16)] * 2
            + [pltpu.VMEM((2, 2, 272, 128), F32)],
            3, flops=1_500_000_000, moved=4 << 20,
        )(turned, taps, order)
        pieces.append(pair)
    (p2, p3), (p0, p1) = pieces
    y2, y3, y1 = [lax.ppermute(p, "chan", [(i, i ^ k) for i in range(4)]) for k, p in zip(XOR_ORDER[1:], (p2, p3, p1))]
    part = call(
        partial_kernel, "three_receivers", shape(4, 272, 128), [], 4, flops=1_000_000, moved=2 << 20,
    )(weight, p0, y2, y3)
    edge = call(
        edge_kernel, "edge", shape(136, 128), [], 3, flops=1_000_000, moved=2 << 20,
    )(weight, part, y1)
    after = lax.ppermute(edge, "wide", [(i, (i - 1) % 64) for i in range(64)])
    main = call(
        main_kernel, "window_sums", shape(2, 512, 128), [pltpu.VMEM((384, 512), BF16)] * 2,
        5, flops=500_000_000, moved=1 << 20,
    )(weight, rows, near, part, y1)
    return call(
        coherence_kernel, "coherence", shape(2, 256, 128), [pltpu.VMEM((384, 128), BF16)] * 2,
        4, flops=500_000_000, moved=1 << 20,
    )(rows, far, main, after)


def solution(mesh):
    placed = (P(None, "chan", "wide", None), P(None, "chan", None), P(None, "chan", None), P(), P())
    return jax.shard_map(
        body, mesh=mesh, in_specs=placed, out_specs=P(None, "chan", "wide"), check_vma=False
    )
```

```python
import functools

import jax
import jax.numpy as jnp
from jax import lax
from jax.experimental import pallas as pl
from jax.experimental.pallas import tpu as pltpu
from jax.sharding import PartitionSpec as P

RADIUS = 4
REACH = 2 * RADIUS
XOR_ORDER = (0, 2, 3, 1)
F32 = jnp.float32
BF16 = jnp.bfloat16
VMEM_LIMIT = 24 * 1024 * 1024


def split(x):
    hi = x.astype(BF16)
    return hi, (x - hi.astype(F32)).astype(BF16)


def dot_nn(a, b):
    return lax.dot_general(a, b, (((1,), (0,)), ((), ())), preferred_element_type=F32)


def dot_nt(a, b):
    return lax.dot_general(a, b, (((1,), (1,)), ((), ())), preferred_element_type=F32)


def toeplitz(taps, rows, width, start=0):
    line = jnp.concatenate([taps, jnp.zeros((1, width - taps.shape[1]), F32)], 1)
    return pltpu.roll(jnp.broadcast_to(line, (rows, width)), start, 1, stride=1, stride_axis=0)


def range_kernel(echo_hbm, chirp_hbm, out_hbm, echo, chirp, out, e_hi, e_lo, w_hi, w_lo, sems, out_sems):
    taps_copy = pltpu.make_async_copy(chirp_hbm, chirp, sems.at[4])
    taps_copy.start()
    copies = []
    for m in range(4):
        bins = pl.ds(2048 * m, 2048)
        copies.append(pltpu.make_async_copy(echo_hbm.at[:, :, bins], echo.at[:, :, bins], sems.at[m]))
        copies[m].start()
    e_hi[1024:1088, :] = jnp.zeros((64, 256), BF16)
    e_lo[1024:1088, :] = jnp.zeros((64, 256), BF16)
    taps_copy.wait()
    real = split(toeplitz(chirp[0], 128, 640))
    imag = split(toeplitz(chirp[1], 128, 640))
    for w_ref, re, im in ((w_hi, real[0], imag[0]), (w_lo, real[1], imag[1])):
        for j in range(5):
            cols = slice(128 * j, 128 * j + 128)
            w_ref[0:128, 256 * j:256 * j + 128] = re[:, cols]
            w_ref[0:128, 256 * j + 128:256 * j + 256] = -im[:, cols]
            w_ref[128:256, 256 * j:256 * j + 128] = im[:, cols]
            w_ref[128:256, 256 * j + 128:256 * j + 256] = re[:, cols]
    for copy in copies:
        copy.wait()

    def fill(first, end):
        for n in range(first, min(end, 64)):
            for part in range(2):
                hi, lo = split(echo[part, :, 128 * n:128 * n + 128])
                e_hi[16 * n:16 * n + 16, 128 * part:128 * part + 128] = hi
                e_lo[16 * n:16 * n + 16, 128 * part:128 * part + 128] = lo

    def send(sem, first, count):
        copy = pltpu.make_async_copy(out.at[pl.ds(first, count)], out_hbm.at[pl.ds(first, count)], out_sems.at[sem])
        copy.start()
        return copy

    fill(0, 4)
    early = lax.broadcasted_iota(jnp.int32, (256, 128), 1) < REACH
    last = [jnp.zeros((16, 128), F32)] * 2
    sent = []
    for m in range(4):
        fill(16 * m + 4, 16 * m + 20)
        starts = [256 * m + 16 * j for j in range(5)]
        hi = [e_hi[s:s + 256, :] for s in starts]
        lo = [e_lo[s:s + 256, :] for s in starts]
        acc = dot_nt(
            jnp.concatenate(hi + hi + lo, 1), jnp.concatenate([w_hi[...], w_lo[...], w_hi[...]], 1)
        )
        for part in range(2):
            turned = pltpu.roll(acc[:, 128 * part:128 * part + 128], REACH, 1)
            before = jnp.concatenate([last[part], turned[0:240]], 0)
            out[16 * m:16 * m + 16, 16 * part:16 * part + 16, :] = jnp.where(early, before, turned).reshape(16, 16, 128)
            last[part] = turned[240:256]
        if m == 3:
            for part in range(2):
                out[0, 16 * part:16 * part + 16, 0:REACH] = last[part][:, 0:REACH]
            sent.append(send(4, 0, 1))
        sent.append(send(m, max(16 * m, 1), 16 if m else 15))
    for copy in sent:
        copy.wait()


def prepare_kernel(pairing_ref, offsets_ref, weight_ref, rows_ref, near_ref, far_ref):
    me = lax.axis_index("chan")
    first = lax.axis_index("wide") == 0
    final = lax.axis_index("wide") == lax.axis_size("wide") - 1
    for i, k in enumerate(XOR_ORDER):
        member = (pairing_ref[0] == (me ^ k)) | (pairing_ref[1] == (me ^ k))
        weight_ref[i] = jnp.full((8, 128), jnp.where(member, 1.0, 0.0), F32)
    row = lax.broadcasted_iota(jnp.int32, (128, 256), 0)
    src = lax.broadcasted_iota(jnp.int32, (128, 256), 1)
    lane = lax.broadcasted_iota(jnp.int32, (128, 128), 0)
    bin_out = lax.broadcasted_iota(jnp.int32, (128, 128), 1)
    for g in range(2):
        oa = offsets_ref[2 * me + g, 0]
        orr = offsets_ref[2 * me + g, 1]
        rows_ref[g] = jnp.where(jnp.abs(src - REACH - row - oa) <= RADIUS, 1.0, 0.0).astype(BF16)
        near = (jnp.abs(lane - REACH - bin_out - orr) <= RADIUS) & ((lane >= REACH) | jnp.logical_not(first))
        near_ref[g] = jnp.where(near, 1.0, 0.0).astype(BF16)
        bin_in = lane % 16
        far = (jnp.abs(bin_in + REACH - bin_out % 16 - orr) <= RADIUS) & (lane // 16 == bin_out // 16) & (lane < 64)
        far = far & ((bin_in < REACH) | jnp.logical_not(final))
        far_ref[g] = jnp.where(far, 1.0, 0.0).astype(BF16)


def azimuth_half(flip, x_ref, taps_ref, order_ref, o0, o1, done_ref, t_hi, t_lo, x_hi, x_lo, y_ref):
    done_ref[...] = jnp.zeros((8, 128), F32)
    for part in range(2):
        hi, lo = split(toeplitz(taps_ref[part], 272, 1280, 1280 - REACH))
        t_hi[part] = hi
        t_lo[part] = lo
        hi, lo = split(x_ref[:, 16 * part:16 * part + 16, :].reshape(1024, 128))
        x_hi[:, 128 * part:128 * part + 128] = hi
        x_lo[:, 128 * part:128 * part + 128] = lo
    me = lax.axis_index("chan")

    def quarter(q):
        first, last = max(q - 2, 0), min(q + 2, 3)
        cols = slice(256 * (first - q + 2), 256 * (last - q + 3))
        rows = slice(256 * first, 256 * last + 256)
        t = [ref[part, :, cols] for ref in (t_hi, t_lo) for part in range(2)]
        g = [dot_nn(t[i], x_hi[rows, :]) + dot_nn(t[i], x_lo[rows, :]) + dot_nn(t[2 + i], x_hi[rows, :]) for i in range(2)]
        return g[0][:, 0:128] - g[1][:, 128:256], g[0][:, 128:256] + g[1][:, 0:128]

    for half in range(2):
        @pl.when((me // 2) ^ flip == half)
        def _(half=half):
            for i in range(2):
                for part, value in enumerate(quarter(2 * half + i)):
                    y_ref[i, part] = value
            for part in range(2):
                y_ref[0, part, 264:272, :] = y_ref[1, part, 8:16, :]
                y_ref[1, part, 0:8, :] = y_ref[0, part, 256:264, :]
                if half == 0:
                    y_ref[0, part, 0:8, :] = jnp.zeros((8, 128), F32)
                else:
                    y_ref[1, part, 264:272, :] = jnp.zeros((8, 128), F32)

    o0[...] = y_ref[me % 2]
    o1[...] = y_ref[1 - me % 2]


def partial_kernel(weight_ref, y0, y2, y3, part_ref):
    for part in range(2):
        fore = aft = 0.0
        for k, y_ref in enumerate((y0, y2, y3)):
            weight = weight_ref[k, 0:1, :]
            y = y_ref[part]
            fore = fore + y * weight
            aft = aft + y * (1.0 - weight)
        part_ref[part] = fore
        part_ref[2 + part] = aft


def whole_sums(weight_ref, part_ref, y1):
    weight = weight_ref[3, 0:1, :]
    fore = [part_ref[part] + y1[part] * weight for part in range(2)]
    return fore + [part_ref[2 + part] + y1[part] * (1.0 - weight) for part in range(2)]


def edge_kernel(weight_ref, part_ref, y1, edge_ref):
    lane = lax.broadcasted_iota(jnp.int32, (272, 128), 1)
    edge = jnp.zeros((272, 128), F32)
    for plane, value in enumerate(whole_sums(weight_ref, part_ref, y1)):
        at = 16 * plane
        moved = pltpu.roll(value, at, 1) if at else value
        edge = jnp.where((lane >= at) & (lane < at + 16), moved, edge)
    edge_ref[...] = edge[0:136] + pltpu.roll(edge[136:272], 64, 1)


def quantities(fr, fi, ar, ai):
    return fr * ar + fi * ai, fi * ar - fr * ai, fr * fr + fi * fi, ar * ar + ai * ai


def main_kernel(weight_ref, rows_ref, near_ref, part_ref, y1, out_ref, last_ref, p_hi, p_lo):
    lane = lax.broadcasted_iota(jnp.int32, (128, 128), 1)
    for q, value in enumerate(quantities(*whole_sums(weight_ref, part_ref, y1))):
        hi, lo = split(value)
        p_hi[0:272, 128 * q:128 * q + 128] = hi
        p_lo[0:272, 128 * q:128 * q + 128] = lo
    p_hi[272:384, :] = jnp.zeros((112, 512), BF16)
    p_lo[272:384, :] = jnp.zeros((112, 512), BF16)
    for g in range(2):
        sums = dot_nn(rows_ref[g], p_hi[128 * g:128 * g + 256, :]) + dot_nn(rows_ref[g], p_lo[128 * g:128 * g + 256, :])
        hi, lo = split(jnp.concatenate([sums[:, 128 * q:128 * q + 128] for q in range(4)], 0))
        window = dot_nn(hi, near_ref[g]) + dot_nn(lo, near_ref[g])
        planes = [window[128 * q:128 * q + 128] for q in range(4)]
        scale = 1.0 / jnp.sqrt(jnp.maximum(planes[2], 1.0) * jnp.maximum(planes[3], 1.0))
        packed = jnp.zeros((128, 128), F32)
        for q in range(4):
            moved = pltpu.roll(planes[q], 16 * q + 16, 1)
            packed = jnp.where((lane >= 16 * q) & (lane < 16 * q + 16), moved, packed)
        last_ref[128 * g:128 * g + 128] = packed
        for part in range(2):
            out_ref[part, 128 * g:128 * g + 128, :] = planes[part] * scale


def coherence_kernel(rows_ref, far_ref, most_ref, last_ref, edge_ref, out_ref, p_hi, p_lo):
    packed = edge_ref[...]
    edge = jnp.concatenate([packed, pltpu.roll(packed, 64, 1)], 0)
    lane = lax.broadcasted_iota(jnp.int32, (272, 128), 1)
    planes = [edge] + [pltpu.roll(edge, 128 - 16 * i, 1) for i in range(1, 4)]
    both = jnp.zeros((272, 128), F32)
    for q, value in enumerate(quantities(*planes)):
        moved = pltpu.roll(value, 16 * q, 1) if q else value
        both = jnp.where((lane >= 16 * q) & (lane < 16 * q + 16), moved, both)
    hi, lo = split(both)
    p_hi[0:272, :] = hi
    p_lo[0:272, :] = lo
    p_hi[272:384, :] = jnp.zeros((112, 128), BF16)
    p_lo[272:384, :] = jnp.zeros((112, 128), BF16)
    keep = lax.broadcasted_iota(jnp.int32, (128, 128), 1) < 112
    for g in range(2):
        sums = dot_nn(rows_ref[g], p_hi[128 * g:128 * g + 256, :]) + dot_nn(rows_ref[g], p_lo[128 * g:128 * g + 256, :])
        hi, lo = split(sums)
        window = last_ref[128 * g:128 * g + 128] + dot_nn(hi, far_ref[g]) + dot_nn(lo, far_ref[g])
        power = jnp.maximum(window, 1.0)
        scale = 1.0 / jnp.sqrt(power * pltpu.roll(power, 112, 1))
        rows = slice(128 * g, 128 * g + 128)
        for part in range(2):
            value = window * pltpu.roll(scale, 96 + 16 * part, 1)
            out_ref[part, rows, :] = jnp.where(keep, most_ref[part, rows, :], pltpu.roll(value, 112 - 16 * part, 1))


def call(kernel, name, out_shape, scratch, n_in, smem=(), hbm=(), flops=0, moved=0, vmem=VMEM_LIMIT, out=pltpu.VMEM):
    spaces = [pltpu.SMEM if i in smem else pltpu.HBM if i in hbm else pltpu.VMEM for i in range(n_in)]
    return pl.pallas_call(
        kernel,
        out_shape=out_shape,
        in_specs=[pl.BlockSpec(memory_space=space) for space in spaces],
        out_specs=jax.tree.map(lambda _: pl.BlockSpec(memory_space=out), out_shape),
        scratch_shapes=scratch,
        compiler_params=pltpu.CompilerParams(vmem_limit_bytes=vmem),
        cost_estimate=pl.CostEstimate(flops=flops, bytes_accessed=moved, transcendentals=0),
        name=name,
    )


def shape(*dims, dtype=F32):
    return jax.ShapeDtypeStruct(dims, dtype)


def body(echoes, range_chirp, azimuth_filter, pairing, offsets):
    signal = echoes[:, 0]
    chirp = range_chirp.reshape(2, 1, 512)
    taps = azimuth_filter.reshape(2, 1, 1024)
    parted = call(
        range_kernel, "range_filter", shape(64, 32, 128),
        [pltpu.VMEM((2, 16, 8192), F32), pltpu.VMEM((2, 1, 512), F32), pltpu.VMEM((64, 32, 128), F32)]
        + [pltpu.VMEM((1088, 256), BF16)] * 2 + [pltpu.VMEM((256, 1280), BF16)] * 2
        + [pltpu.SemaphoreType.DMA((5,))] * 2,
        2, hbm=(0, 1), flops=2_000_000_000, moved=2 << 20, vmem=60 << 20, out=pltpu.HBM,
    )(signal, chirp)
    turned = lax.all_to_all(parted, "wide", split_axis=0, concat_axis=0, tiled=True)
    weight, rows, near, far = call(
        prepare_kernel, "prepare",
        (shape(4, 8, 128), shape(2, 128, 256, dtype=BF16)) + (shape(2, 128, 128, dtype=BF16),) * 2, [],
        2, smem=(0, 1), flops=1_000_000_000, moved=1 << 20,
    )(pairing, offsets)
    order = weight.reshape(32, 128)
    pieces = []
    for flip in (1, 0):
        *pair, order = call(
            functools.partial(azimuth_half, flip), "azimuth_" + ("own", "other")[flip],
            (shape(2, 272, 128),) * 2 + (shape(8, 128),),
            [pltpu.VMEM((2, 272, 1280), BF16)] * 2 + [pltpu.VMEM((1024, 256), BF16)] * 2
            + [pltpu.VMEM((2, 2, 272, 128), F32)],
            3, flops=1_500_000_000, moved=4 << 20,
        )(turned, taps, order)
        pieces.append(pair)
    (p2, p3), (p0, p1) = pieces
    y2, y3, y1 = [lax.ppermute(p, "chan", [(i, i ^ k) for i in range(4)]) for k, p in zip(XOR_ORDER[1:], (p2, p3, p1))]
    part = call(
        partial_kernel, "three_receivers", shape(4, 272, 128), [], 4, flops=1_000_000, moved=2 << 20,
    )(weight, p0, y2, y3)
    edge = call(
        edge_kernel, "edge", shape(136, 128), [], 3, flops=1_000_000, moved=2 << 20,
    )(weight, part, y1)
    after = lax.ppermute(edge, "wide", [(i, (i - 1) % 64) for i in range(64)])
    most, last = call(
        main_kernel, "window_sums", (shape(2, 256, 128), shape(256, 128)), [pltpu.VMEM((384, 512), BF16)] * 2,
        5, flops=500_000_000, moved=1 << 20,
    )(weight, rows, near, part, y1)
    return call(
        coherence_kernel, "coherence", shape(2, 256, 128), [pltpu.VMEM((384, 128), BF16)] * 2,
        5, flops=500_000_000, moved=1 << 20,
    )(rows, far, most, last, after)


def solution(mesh):
    placed = (P(None, "chan", "wide", None), P(None, "chan", None), P(None, "chan", None), P(), P())
    return jax.shard_map(
        body, mesh=mesh, in_specs=placed, out_specs=P(None, "chan", "wide"), check_vma=False
    )
```

```python
import functools

import jax
import jax.numpy as jnp
from jax import lax
from jax.experimental import pallas as pl
from jax.experimental.pallas import tpu as pltpu
from jax.sharding import PartitionSpec as P

RADIUS = 4
REACH = 2 * RADIUS
XOR_ORDER = (0, 2, 3, 1)
FIRST = 1
FIRST_COST = 1_000
F32 = jnp.float32
BF16 = jnp.bfloat16
VMEM_LIMIT = 24 * 1024 * 1024


def split(x):
    hi = x.astype(BF16)
    return hi, (x - hi.astype(F32)).astype(BF16)


def dot_nn(a, b):
    return lax.dot_general(a, b, (((1,), (0,)), ((), ())), preferred_element_type=F32)


def dot_nt(a, b):
    return lax.dot_general(a, b, (((1,), (1,)), ((), ())), preferred_element_type=F32)


def toeplitz(taps, rows, width, start=0):
    line = jnp.concatenate([taps, jnp.zeros((1, width - taps.shape[1]), F32)], 1)
    return pltpu.roll(jnp.broadcast_to(line, (rows, width)), start, 1, stride=1, stride_axis=0)


def range_kernel(echo_hbm, chirp_hbm, out_hbm, echo, chirp, out, e_hi, e_lo, w_hi, w_lo, sems, out_sems):
    taps_copy = pltpu.make_async_copy(chirp_hbm, chirp, sems.at[4])
    taps_copy.start()
    copies = []
    for m in range(4):
        bins = pl.ds(2048 * m, 2048)
        copies.append(pltpu.make_async_copy(echo_hbm.at[:, :, bins], echo.at[:, :, bins], sems.at[m]))
        copies[m].start()
    e_hi[1024:1088, :] = jnp.zeros((64, 256), BF16)
    e_lo[1024:1088, :] = jnp.zeros((64, 256), BF16)
    taps_copy.wait()
    real = split(toeplitz(chirp[0], 128, 640))
    imag = split(toeplitz(chirp[1], 128, 640))
    for w_ref, re, im in ((w_hi, real[0], imag[0]), (w_lo, real[1], imag[1])):
        for j in range(5):
            cols = slice(128 * j, 128 * j + 128)
            w_ref[0:128, 256 * j:256 * j + 128] = re[:, cols]
            w_ref[0:128, 256 * j + 128:256 * j + 256] = -im[:, cols]
            w_ref[128:256, 256 * j:256 * j + 128] = im[:, cols]
            w_ref[128:256, 256 * j + 128:256 * j + 256] = re[:, cols]
    for copy in copies:
        copy.wait()

    def fill(first, end):
        for n in range(first, min(end, 64)):
            for part in range(2):
                hi, lo = split(echo[part, :, 128 * n:128 * n + 128])
                e_hi[16 * n:16 * n + 16, 128 * part:128 * part + 128] = hi
                e_lo[16 * n:16 * n + 16, 128 * part:128 * part + 128] = lo

    def send(sem, first, count):
        copy = pltpu.make_async_copy(out.at[pl.ds(first, count)], out_hbm.at[pl.ds(first, count)], out_sems.at[sem])
        copy.start()
        return copy

    fill(0, 4)
    early = lax.broadcasted_iota(jnp.int32, (256, 128), 1) < REACH
    last = [jnp.zeros((16, 128), F32)] * 2
    sent = []
    for m in range(4):
        fill(16 * m + 4, 16 * m + 20)
        starts = [256 * m + 16 * j for j in range(5)]
        hi = [e_hi[s:s + 256, :] for s in starts]
        lo = [e_lo[s:s + 256, :] for s in starts]
        acc = dot_nt(
            jnp.concatenate(hi + hi + lo, 1), jnp.concatenate([w_hi[...], w_lo[...], w_hi[...]], 1)
        )
        for part in range(2):
            turned = pltpu.roll(acc[:, 128 * part:128 * part + 128], REACH, 1)
            before = jnp.concatenate([last[part], turned[0:240]], 0)
            out[16 * m:16 * m + 16, 16 * part:16 * part + 16, :] = jnp.where(early, before, turned).reshape(16, 16, 128)
            last[part] = turned[240:256]
        if m == 3:
            for part in range(2):
                out[0, 16 * part:16 * part + 16, 0:REACH] = last[part][:, 0:REACH]
            sent.append(send(4, 0, 1))
        sent.append(send(m, max(16 * m, 1), 16 if m else 15))
    for copy in sent:
        copy.wait()


def prepare_kernel(pairing_ref, offsets_ref, weight_ref, rows_ref, near_ref, far_ref):
    me = lax.axis_index("chan")
    first = lax.axis_index("wide") == 0
    final = lax.axis_index("wide") == lax.axis_size("wide") - 1
    for i, k in enumerate(XOR_ORDER):
        member = (pairing_ref[0] == (me ^ k)) | (pairing_ref[1] == (me ^ k))
        weight_ref[i] = jnp.full((8, 128), jnp.where(member, 1.0, 0.0), F32)
    row = lax.broadcasted_iota(jnp.int32, (128, 256), 0)
    src = lax.broadcasted_iota(jnp.int32, (128, 256), 1)
    lane = lax.broadcasted_iota(jnp.int32, (128, 128), 0)
    bin_out = lax.broadcasted_iota(jnp.int32, (128, 128), 1)
    for g in range(2):
        oa = offsets_ref[2 * me + g, 0]
        orr = offsets_ref[2 * me + g, 1]
        rows_ref[g] = jnp.where(jnp.abs(src - REACH - row - oa) <= RADIUS, 1.0, 0.0).astype(BF16)
        near = (jnp.abs(lane - REACH - bin_out - orr) <= RADIUS) & ((lane >= REACH) | jnp.logical_not(first))
        near_ref[g] = jnp.where(near, 1.0, 0.0).astype(BF16)
        far = (jnp.abs(lane + 128 - REACH - bin_out - orr) <= RADIUS) & (
            (lane < REACH) | ((lane < 2 * REACH) & jnp.logical_not(final))
        )
        far_ref[g] = jnp.where(far, 1.0, 0.0).astype(BF16)


def build_taps(taps_ref, t_hi, t_lo):
    for part in range(2):
        hi, lo = split(toeplitz(taps_ref[part], 272, 1280, 1280 - REACH))
        t_hi[part] = hi
        t_lo[part] = lo


def split_pulses(x_ref, x_hi, x_lo):
    for part in range(2):
        hi, lo = split(x_ref[:, 16 * part:16 * part + 16, :].reshape(1024, 128))
        x_hi[:, 128 * part:128 * part + 128] = hi
        x_lo[:, 128 * part:128 * part + 128] = lo


def quarter_rows(q, picked, t_hi, t_lo, x_hi, x_lo):
    first, last = max(q - 2, 0), min(q + 2, 3)
    cols = slice(256 * (first - q + 2), 256 * (last - q + 3))
    rows = slice(256 * first, 256 * last + 256)
    t = [ref[part, picked, cols] for ref in (t_hi, t_lo) for part in range(2)]
    g = [dot_nn(t[i], x_hi[rows, :]) + dot_nn(t[i], x_lo[rows, :]) + dot_nn(t[2 + i], x_hi[rows, :]) for i in range(2)]
    return g[0][:, 0:128] - g[1][:, 128:256], g[0][:, 128:256] + g[1][:, 0:128]


def azimuth_quarter(k, x_ref, taps_ref, order_ref, out_ref, done_ref, t_hi, t_lo, x_hi, x_lo):
    done_ref[...] = jnp.zeros((8, 128), F32)
    build_taps(taps_ref, t_hi, t_lo)
    split_pulses(x_ref, x_hi, x_lo)
    taps = (t_hi, t_lo, x_hi, x_lo)
    me = lax.axis_index("chan")
    for q in range(4):
        @pl.when((me ^ k) == q)
        def _(q=q):
            own = quarter_rows(q, slice(0, 272), *taps)
            shared = quarter_rows(q ^ 1, slice(256, 272) if q % 2 else slice(0, 16), *taps)
            for part in range(2):
                out_ref[part] = own[part]
                if q % 2:
                    out_ref[part, 0:8, :] = shared[part][0:8]
                else:
                    out_ref[part, 264:272, :] = shared[part][8:16]
                if q == 0:
                    out_ref[part, 0:8, :] = jnp.zeros((8, 128), F32)
                if q == 3:
                    out_ref[part, 264:272, :] = jnp.zeros((8, 128), F32)


def azimuth_own(x_ref, taps_ref, order_ref, o0, o1, t_hi, t_lo, x_hi, x_lo, y_ref):
    build_taps(taps_ref, t_hi, t_lo)
    split_pulses(x_ref, x_hi, x_lo)
    me = lax.axis_index("chan")
    for half in range(2):
        @pl.when(me // 2 == half)
        def _(half=half):
            for i in range(2):
                for part, value in enumerate(quarter_rows(2 * half + i, slice(0, 272), t_hi, t_lo, x_hi, x_lo)):
                    y_ref[i, part] = value
            for part in range(2):
                y_ref[0, part, 264:272, :] = y_ref[1, part, 8:16, :]
                y_ref[1, part, 0:8, :] = y_ref[0, part, 256:264, :]
                if half == 0:
                    y_ref[0, part, 0:8, :] = jnp.zeros((8, 128), F32)
                else:
                    y_ref[1, part, 264:272, :] = jnp.zeros((8, 128), F32)

    o0[...] = y_ref[me % 2]
    o1[...] = y_ref[1 - me % 2]


def first_sums_kernel(weight_ref, y0, ya, part_ref):
    own, other = weight_ref[0, 0:1, :], weight_ref[FIRST, 0:1, :]
    for part in range(2):
        part_ref[part] = y0[part] * own + ya[part] * other
        part_ref[2 + part] = y0[part] * (1.0 - own) + ya[part] * (1.0 - other)


def more_sums_kernel(weight_ref, first_ref, yb, part_ref):
    weight = weight_ref[3 - FIRST, 0:1, :]
    for part in range(2):
        part_ref[part] = first_ref[part] + yb[part] * weight
        part_ref[2 + part] = first_ref[2 + part] + yb[part] * (1.0 - weight)


def whole_sums(weight_ref, part_ref, y1):
    weight = weight_ref[3, 0:1, :]
    fore = [part_ref[part] + y1[part] * weight for part in range(2)]
    return fore + [part_ref[2 + part] + y1[part] * (1.0 - weight) for part in range(2)]


def edge_kernel(weight_ref, part_ref, y1, edge_ref):
    lane = lax.broadcasted_iota(jnp.int32, (272, 128), 1)
    edge = jnp.zeros((272, 128), F32)
    for plane, value in enumerate(whole_sums(weight_ref, part_ref, y1)):
        at = 16 * plane
        moved = pltpu.roll(value, at, 1) if at else value
        edge = jnp.where((lane >= at) & (lane < at + 16), moved, edge)
    edge_ref[...] = edge[0:136] + pltpu.roll(edge[136:272], 64, 1)


def quantities(fr, fi, ar, ai):
    return fr * ar + fi * ai, fi * ar - fr * ai, fr * fr + fi * fi, ar * ar + ai * ai


def main_kernel(weight_ref, rows_ref, near_ref, part_ref, y1, out_ref, p_hi, p_lo):
    for q, value in enumerate(quantities(*whole_sums(weight_ref, part_ref, y1))):
        hi, lo = split(value)
        p_hi[0:272, 128 * q:128 * q + 128] = hi
        p_lo[0:272, 128 * q:128 * q + 128] = lo
    p_hi[272:384, :] = jnp.zeros((112, 512), BF16)
    p_lo[272:384, :] = jnp.zeros((112, 512), BF16)
    for g in range(2):
        sums = dot_nn(rows_ref[g], p_hi[128 * g:128 * g + 256, :]) + dot_nn(rows_ref[g], p_lo[128 * g:128 * g + 256, :])
        hi, lo = split(jnp.concatenate([sums[:, 128 * q:128 * q + 128] for q in range(4)], 0))
        out_ref[g] = dot_nn(hi, near_ref[g]) + dot_nn(lo, near_ref[g])


def coherence_kernel(rows_ref, far_ref, main_ref, edge_ref, out_ref, p_hi, p_lo):
    packed = edge_ref[...]
    edge = jnp.concatenate([packed, pltpu.roll(packed, 64, 1)], 0)
    lane = lax.broadcasted_iota(jnp.int32, (272, 128), 1)
    planes = [edge] + [pltpu.roll(edge, 128 - 16 * i, 1) for i in range(1, 4)]
    both = jnp.zeros((272, 128), F32)
    for q, value in enumerate(quantities(*planes)):
        moved = pltpu.roll(value, 16 * q, 1) if q else value
        both = jnp.where((lane >= 16 * q) & (lane < 16 * q + 16), moved, both)
    hi, lo = split(both)
    p_hi[0:272, :] = hi
    p_lo[0:272, :] = lo
    p_hi[272:384, :] = jnp.zeros((112, 128), BF16)
    p_lo[272:384, :] = jnp.zeros((112, 128), BF16)
    for g in range(2):
        sums = dot_nn(rows_ref[g], p_hi[128 * g:128 * g + 256, :]) + dot_nn(rows_ref[g], p_lo[128 * g:128 * g + 256, :])
        hi, lo = split(jnp.concatenate([sums] + [pltpu.roll(sums, 128 - 16 * q, 1) for q in range(1, 4)], 0))
        window = main_ref[g] + dot_nn(hi, far_ref[g]) + dot_nn(lo, far_ref[g])
        scale = 1.0 / jnp.sqrt(jnp.maximum(window[256:384], 1.0) * jnp.maximum(window[384:512], 1.0))
        out_ref[0, 128 * g:128 * g + 128, :] = window[0:128] * scale
        out_ref[1, 128 * g:128 * g + 128, :] = window[128:256] * scale


def call(kernel, name, out_shape, scratch, n_in, smem=(), hbm=(), flops=0, moved=0, vmem=VMEM_LIMIT, out=pltpu.VMEM):
    spaces = [pltpu.SMEM if i in smem else pltpu.HBM if i in hbm else pltpu.VMEM for i in range(n_in)]
    return pl.pallas_call(
        kernel,
        out_shape=out_shape,
        in_specs=[pl.BlockSpec(memory_space=space) for space in spaces],
        out_specs=jax.tree.map(lambda _: pl.BlockSpec(memory_space=out), out_shape),
        scratch_shapes=scratch,
        compiler_params=pltpu.CompilerParams(vmem_limit_bytes=vmem),
        cost_estimate=pl.CostEstimate(flops=flops, bytes_accessed=moved, transcendentals=0),
        name=name,
    )


def shape(*dims, dtype=F32):
    return jax.ShapeDtypeStruct(dims, dtype)


def body(echoes, range_chirp, azimuth_filter, pairing, offsets):
    signal = echoes[:, 0]
    chirp = range_chirp.reshape(2, 1, 512)
    taps = azimuth_filter.reshape(2, 1, 1024)
    parted = call(
        range_kernel, "range_filter", shape(64, 32, 128),
        [pltpu.VMEM((2, 16, 8192), F32), pltpu.VMEM((2, 1, 512), F32), pltpu.VMEM((64, 32, 128), F32)]
        + [pltpu.VMEM((1088, 256), BF16)] * 2 + [pltpu.VMEM((256, 1280), BF16)] * 2
        + [pltpu.SemaphoreType.DMA((5,))] * 2,
        2, hbm=(0, 1), flops=2_000_000_000, moved=2 << 20, vmem=60 << 20, out=pltpu.HBM,
    )(signal, chirp)
    turned = lax.all_to_all(parted, "wide", split_axis=0, concat_axis=0, tiled=True)
    weight, rows, near, far = call(
        prepare_kernel, "prepare",
        (shape(4, 8, 128), shape(2, 128, 256, dtype=BF16)) + (shape(2, 128, 128, dtype=BF16),) * 2, [],
        2, smem=(0, 1), flops=1_000_000_000, moved=1 << 20,
    )(pairing, offsets)
    order = weight.reshape(32, 128)
    scratch = [pltpu.VMEM((2, 272, 1280), BF16)] * 2 + [pltpu.VMEM((1024, 256), BF16)] * 2
    pa, order = call(
        functools.partial(azimuth_quarter, 2), "azimuth_first", (shape(2, 272, 128), shape(8, 128)), scratch,
        3, flops=1_000_000_000, moved=1000,
    )(turned, taps, order)
    pb, order = call(
        functools.partial(azimuth_quarter, 3), "azimuth_second", (shape(2, 272, 128), shape(8, 128)), scratch,
        3, flops=1000, moved=1000,
    )(turned, taps, order)
    p0, p1 = call(
        azimuth_own, "azimuth_own", (shape(2, 272, 128),) * 2, scratch + [pltpu.VMEM((2, 2, 272, 128), F32)],
        3, flops=1000, moved=1000,
    )(turned, taps, order)
    ya, yb, y1 = [lax.ppermute(p, "chan", [(i, i ^ k) for i in range(4)]) for k, p in ((2, pa), (3, pb), (1, p1))]
    part = call(
        first_sums_kernel, "two_receivers", shape(4, 272, 128), [], 3, flops=FIRST_COST, moved=1000,
    )(weight, p0, ya)
    part = call(
        more_sums_kernel, "three_receivers", shape(4, 272, 128), [], 3, flops=30_000_000_000, moved=2 << 20,
    )(weight, part, yb)
    edge = call(
        edge_kernel, "edge", shape(136, 128), [], 3, flops=1_000_000, moved=2 << 20,
    )(weight, part, y1)
    after = lax.ppermute(edge, "wide", [(i, (i - 1) % 64) for i in range(64)])
    main = call(
        main_kernel, "window_sums", shape(2, 512, 128), [pltpu.VMEM((384, 512), BF16)] * 2,
        5, flops=500_000_000, moved=1 << 20,
    )(weight, rows, near, part, y1)
    return call(
        coherence_kernel, "coherence", shape(2, 256, 128), [pltpu.VMEM((384, 128), BF16)] * 2,
        4, flops=500_000_000, moved=1 << 20,
    )(rows, far, main, after)


def solution(mesh):
    placed = (P(None, "chan", "wide", None), P(None, "chan", None), P(None, "chan", None), P(), P())
    return jax.shard_map(
        body, mesh=mesh, in_specs=placed, out_specs=P(None, "chan", "wide"), check_vma=False
    )
```

```python
import functools

import jax
import jax.numpy as jnp
from jax import lax
from jax.experimental import pallas as pl
from jax.experimental.pallas import tpu as pltpu
from jax.sharding import PartitionSpec as P

RADIUS = 4
REACH = 2 * RADIUS
XOR_ORDER = (0, 2, 3, 1)
FIRST = 1
FIRST_COST = 1_000
F32 = jnp.float32
BF16 = jnp.bfloat16
VMEM_LIMIT = 24 * 1024 * 1024


def split(x):
    hi = x.astype(BF16)
    return hi, (x - hi.astype(F32)).astype(BF16)


def dot_nn(a, b):
    return lax.dot_general(a, b, (((1,), (0,)), ((), ())), preferred_element_type=F32)


def dot_nt(a, b):
    return lax.dot_general(a, b, (((1,), (1,)), ((), ())), preferred_element_type=F32)


def toeplitz(taps, rows, width, start=0):
    line = jnp.concatenate([taps, jnp.zeros((1, width - taps.shape[1]), F32)], 1)
    return pltpu.roll(jnp.broadcast_to(line, (rows, width)), start, 1, stride=1, stride_axis=0)


def range_kernel(echo_hbm, chirp_hbm, out_hbm, echo, chirp, out, e_hi, e_lo, w_hi, w_lo, sems, out_sems):
    taps_copy = pltpu.make_async_copy(chirp_hbm, chirp, sems.at[4])
    taps_copy.start()
    copies = []
    for m in range(4):
        bins = pl.ds(2048 * m, 2048)
        copies.append(pltpu.make_async_copy(echo_hbm.at[:, :, bins], echo.at[:, :, bins], sems.at[m]))
        copies[m].start()
    e_hi[1024:1088, :] = jnp.zeros((64, 256), BF16)
    e_lo[1024:1088, :] = jnp.zeros((64, 256), BF16)
    taps_copy.wait()
    real = split(toeplitz(chirp[0], 128, 640))
    imag = split(toeplitz(chirp[1], 128, 640))
    for w_ref, re, im in ((w_hi, real[0], imag[0]), (w_lo, real[1], imag[1])):
        for j in range(5):
            cols = slice(128 * j, 128 * j + 128)
            w_ref[0:128, 256 * j:256 * j + 128] = re[:, cols]
            w_ref[0:128, 256 * j + 128:256 * j + 256] = -im[:, cols]
            w_ref[128:256, 256 * j:256 * j + 128] = im[:, cols]
            w_ref[128:256, 256 * j + 128:256 * j + 256] = re[:, cols]
    for copy in copies:
        copy.wait()

    def fill(first, end):
        for n in range(first, min(end, 64)):
            for part in range(2):
                hi, lo = split(echo[part, :, 128 * n:128 * n + 128])
                e_hi[16 * n:16 * n + 16, 128 * part:128 * part + 128] = hi
                e_lo[16 * n:16 * n + 16, 128 * part:128 * part + 128] = lo

    def send(sem, first, count):
        copy = pltpu.make_async_copy(out.at[pl.ds(first, count)], out_hbm.at[pl.ds(first, count)], out_sems.at[sem])
        copy.start()
        return copy

    fill(0, 4)
    early = lax.broadcasted_iota(jnp.int32, (256, 128), 1) < REACH
    last = [jnp.zeros((16, 128), F32)] * 2
    sent = []
    for m in range(4):
        fill(16 * m + 4, 16 * m + 20)
        starts = [256 * m + 16 * j for j in range(5)]
        hi = [e_hi[s:s + 256, :] for s in starts]
        lo = [e_lo[s:s + 256, :] for s in starts]
        acc = dot_nt(
            jnp.concatenate(hi + hi + lo, 1), jnp.concatenate([w_hi[...], w_lo[...], w_hi[...]], 1)
        )
        for part in range(2):
            turned = pltpu.roll(acc[:, 128 * part:128 * part + 128], REACH, 1)
            before = jnp.concatenate([last[part], turned[0:240]], 0)
            out[16 * m:16 * m + 16, 16 * part:16 * part + 16, :] = jnp.where(early, before, turned).reshape(16, 16, 128)
            last[part] = turned[240:256]
        if m == 3:
            for part in range(2):
                out[0, 16 * part:16 * part + 16, 0:REACH] = last[part][:, 0:REACH]
            sent.append(send(4, 0, 1))
        sent.append(send(m, max(16 * m, 1), 16 if m else 15))
    for copy in sent:
        copy.wait()


def prepare_kernel(pairing_ref, offsets_ref, weight_ref, rows_ref, near_ref, far_ref):
    me = lax.axis_index("chan")
    first = lax.axis_index("wide") == 0
    final = lax.axis_index("wide") == lax.axis_size("wide") - 1
    for i, k in enumerate(XOR_ORDER):
        member = (pairing_ref[0] == (me ^ k)) | (pairing_ref[1] == (me ^ k))
        weight_ref[i] = jnp.full((8, 128), jnp.where(member, 1.0, 0.0), F32)
    row = lax.broadcasted_iota(jnp.int32, (128, 256), 0)
    src = lax.broadcasted_iota(jnp.int32, (128, 256), 1)
    lane = lax.broadcasted_iota(jnp.int32, (128, 128), 0)
    bin_out = lax.broadcasted_iota(jnp.int32, (128, 128), 1)
    for g in range(2):
        oa = offsets_ref[2 * me + g, 0]
        orr = offsets_ref[2 * me + g, 1]
        rows_ref[g] = jnp.where(jnp.abs(src - REACH - row - oa) <= RADIUS, 1.0, 0.0).astype(BF16)
        near = (jnp.abs(lane - REACH - bin_out - orr) <= RADIUS) & ((lane >= REACH) | jnp.logical_not(first))
        near_ref[g] = jnp.where(near, 1.0, 0.0).astype(BF16)
        far = (jnp.abs(lane + 128 - REACH - bin_out - orr) <= RADIUS) & (
            (lane < REACH) | ((lane < 2 * REACH) & jnp.logical_not(final))
        )
        far_ref[g] = jnp.where(far, 1.0, 0.0).astype(BF16)


def build_taps(taps_ref, t_hi, t_lo):
    for part in range(2):
        hi, lo = split(toeplitz(taps_ref[part], 272, 1280, 1280 - REACH))
        t_hi[part] = hi
        t_lo[part] = lo


def split_pulses(x_ref, x_hi, x_lo):
    for part in range(2):
        hi, lo = split(x_ref[:, 16 * part:16 * part + 16, :].reshape(1024, 128))
        x_hi[:, 128 * part:128 * part + 128] = hi
        x_lo[:, 128 * part:128 * part + 128] = lo


def quarter_rows(q, picked, t_hi, t_lo, x_hi, x_lo):
    first, last = max(q - 2, 0), min(q + 2, 3)
    cols = slice(256 * (first - q + 2), 256 * (last - q + 3))
    rows = slice(256 * first, 256 * last + 256)
    t = [ref[part, picked, cols] for ref in (t_hi, t_lo) for part in range(2)]
    g = [dot_nn(t[i], x_hi[rows, :]) + dot_nn(t[i], x_lo[rows, :]) + dot_nn(t[2 + i], x_hi[rows, :]) for i in range(2)]
    return g[0][:, 0:128] - g[1][:, 128:256], g[0][:, 128:256] + g[1][:, 0:128]


def first_quarter(x_ref, taps_ref, order_ref, out_ref, done_ref, t_hi, t_lo, x_hi, x_lo):
    done_ref[...] = jnp.zeros((8, 128), F32)
    build_taps(taps_ref, t_hi, t_lo)
    split_pulses(x_ref, x_hi, x_lo)
    azimuth_quarter(2, (t_hi, t_lo, x_hi, x_lo), out_ref)


def second_quarter(order_ref, t_hi, t_lo, x_hi, x_lo, out_ref, done_ref):
    done_ref[...] = jnp.zeros((8, 128), F32)
    azimuth_quarter(3, (t_hi, t_lo, x_hi, x_lo), out_ref)


def azimuth_quarter(k, taps, out_ref):
    me = lax.axis_index("chan")
    for q in range(4):
        @pl.when((me ^ k) == q)
        def _(q=q):
            own = quarter_rows(q, slice(0, 272), *taps)
            shared = quarter_rows(q ^ 1, slice(256, 272) if q % 2 else slice(0, 16), *taps)
            for part in range(2):
                out_ref[part] = own[part]
                if q % 2:
                    out_ref[part, 0:8, :] = shared[part][0:8]
                else:
                    out_ref[part, 264:272, :] = shared[part][8:16]
                if q == 0:
                    out_ref[part, 0:8, :] = jnp.zeros((8, 128), F32)
                if q == 3:
                    out_ref[part, 264:272, :] = jnp.zeros((8, 128), F32)


def azimuth_own(order_ref, t_hi, t_lo, x_hi, x_lo, o0, o1, y_ref):
    me = lax.axis_index("chan")
    for half in range(2):
        @pl.when(me // 2 == half)
        def _(half=half):
            for i in range(2):
                for part, value in enumerate(quarter_rows(2 * half + i, slice(0, 272), t_hi, t_lo, x_hi, x_lo)):
                    y_ref[i, part] = value
            for part in range(2):
                y_ref[0, part, 264:272, :] = y_ref[1, part, 8:16, :]
                y_ref[1, part, 0:8, :] = y_ref[0, part, 256:264, :]
                if half == 0:
                    y_ref[0, part, 0:8, :] = jnp.zeros((8, 128), F32)
                else:
                    y_ref[1, part, 264:272, :] = jnp.zeros((8, 128), F32)

    o0[...] = y_ref[me % 2]
    o1[...] = y_ref[1 - me % 2]


def first_sums_kernel(weight_ref, y0, ya, part_ref):
    own, other = weight_ref[0, 0:1, :], weight_ref[FIRST, 0:1, :]
    for part in range(2):
        part_ref[part] = y0[part] * own + ya[part] * other
        part_ref[2 + part] = y0[part] * (1.0 - own) + ya[part] * (1.0 - other)


def more_sums_kernel(weight_ref, first_ref, yb, part_ref):
    weight = weight_ref[3 - FIRST, 0:1, :]
    for part in range(2):
        part_ref[part] = first_ref[part] + yb[part] * weight
        part_ref[2 + part] = first_ref[2 + part] + yb[part] * (1.0 - weight)


def whole_sums(weight_ref, part_ref, y1):
    weight = weight_ref[3, 0:1, :]
    fore = [part_ref[part] + y1[part] * weight for part in range(2)]
    return fore + [part_ref[2 + part] + y1[part] * (1.0 - weight) for part in range(2)]


def edge_kernel(weight_ref, part_ref, y1, edge_ref):
    lane = lax.broadcasted_iota(jnp.int32, (272, 128), 1)
    edge = jnp.zeros((272, 128), F32)
    for plane, value in enumerate(whole_sums(weight_ref, part_ref, y1)):
        at = 16 * plane
        moved = pltpu.roll(value, at, 1) if at else value
        edge = jnp.where((lane >= at) & (lane < at + 16), moved, edge)
    edge_ref[...] = edge[0:136] + pltpu.roll(edge[136:272], 64, 1)


def quantities(fr, fi, ar, ai):
    return fr * ar + fi * ai, fi * ar - fr * ai, fr * fr + fi * fi, ar * ar + ai * ai


def main_kernel(weight_ref, rows_ref, near_ref, part_ref, y1, out_ref, p_hi, p_lo):
    for q, value in enumerate(quantities(*whole_sums(weight_ref, part_ref, y1))):
        hi, lo = split(value)
        p_hi[0:272, 128 * q:128 * q + 128] = hi
        p_lo[0:272, 128 * q:128 * q + 128] = lo
    p_hi[272:384, :] = jnp.zeros((112, 512), BF16)
    p_lo[272:384, :] = jnp.zeros((112, 512), BF16)
    for g in range(2):
        sums = dot_nn(rows_ref[g], p_hi[128 * g:128 * g + 256, :]) + dot_nn(rows_ref[g], p_lo[128 * g:128 * g + 256, :])
        hi, lo = split(jnp.concatenate([sums[:, 128 * q:128 * q + 128] for q in range(4)], 0))
        out_ref[g] = dot_nn(hi, near_ref[g]) + dot_nn(lo, near_ref[g])


def coherence_kernel(rows_ref, far_ref, main_ref, edge_ref, out_ref, p_hi, p_lo):
    packed = edge_ref[...]
    edge = jnp.concatenate([packed, pltpu.roll(packed, 64, 1)], 0)
    lane = lax.broadcasted_iota(jnp.int32, (272, 128), 1)
    planes = [edge] + [pltpu.roll(edge, 128 - 16 * i, 1) for i in range(1, 4)]
    both = jnp.zeros((272, 128), F32)
    for q, value in enumerate(quantities(*planes)):
        moved = pltpu.roll(value, 16 * q, 1) if q else value
        both = jnp.where((lane >= 16 * q) & (lane < 16 * q + 16), moved, both)
    hi, lo = split(both)
    p_hi[0:272, :] = hi
    p_lo[0:272, :] = lo
    p_hi[272:384, :] = jnp.zeros((112, 128), BF16)
    p_lo[272:384, :] = jnp.zeros((112, 128), BF16)
    for g in range(2):
        sums = dot_nn(rows_ref[g], p_hi[128 * g:128 * g + 256, :]) + dot_nn(rows_ref[g], p_lo[128 * g:128 * g + 256, :])
        hi, lo = split(jnp.concatenate([sums] + [pltpu.roll(sums, 128 - 16 * q, 1) for q in range(1, 4)], 0))
        window = main_ref[g] + dot_nn(hi, far_ref[g]) + dot_nn(lo, far_ref[g])
        scale = 1.0 / jnp.sqrt(jnp.maximum(window[256:384], 1.0) * jnp.maximum(window[384:512], 1.0))
        out_ref[0, 128 * g:128 * g + 128, :] = window[0:128] * scale
        out_ref[1, 128 * g:128 * g + 128, :] = window[128:256] * scale


def call(kernel, name, out_shape, scratch, n_in, smem=(), hbm=(), flops=0, moved=0, vmem=VMEM_LIMIT, out=pltpu.VMEM):
    spaces = [pltpu.SMEM if i in smem else pltpu.HBM if i in hbm else pltpu.VMEM for i in range(n_in)]
    return pl.pallas_call(
        kernel,
        out_shape=out_shape,
        in_specs=[pl.BlockSpec(memory_space=space) for space in spaces],
        out_specs=jax.tree.map(lambda _: pl.BlockSpec(memory_space=out), out_shape),
        scratch_shapes=scratch,
        compiler_params=pltpu.CompilerParams(vmem_limit_bytes=vmem),
        cost_estimate=pl.CostEstimate(flops=flops, bytes_accessed=moved, transcendentals=0),
        name=name,
    )


def shape(*dims, dtype=F32):
    return jax.ShapeDtypeStruct(dims, dtype)


def body(echoes, range_chirp, azimuth_filter, pairing, offsets):
    signal = echoes[:, 0]
    chirp = range_chirp.reshape(2, 1, 512)
    taps = azimuth_filter.reshape(2, 1, 1024)
    parted = call(
        range_kernel, "range_filter", shape(64, 32, 128),
        [pltpu.VMEM((2, 16, 8192), F32), pltpu.VMEM((2, 1, 512), F32), pltpu.VMEM((64, 32, 128), F32)]
        + [pltpu.VMEM((1088, 256), BF16)] * 2 + [pltpu.VMEM((256, 1280), BF16)] * 2
        + [pltpu.SemaphoreType.DMA((5,))] * 2,
        2, hbm=(0, 1), flops=2_000_000_000, moved=2 << 20, vmem=60 << 20, out=pltpu.HBM,
    )(signal, chirp)
    turned = lax.all_to_all(parted, "wide", split_axis=0, concat_axis=0, tiled=True)
    weight, rows, near, far = call(
        prepare_kernel, "prepare",
        (shape(4, 8, 128), shape(2, 128, 256, dtype=BF16)) + (shape(2, 128, 128, dtype=BF16),) * 2, [],
        2, smem=(0, 1), flops=1_000_000_000, moved=1 << 20,
    )(pairing, offsets)
    order = weight.reshape(32, 128)
    pa, order, *taps = call(
        first_quarter, "azimuth_first",
        (shape(2, 272, 128), shape(8, 128)) + (shape(2, 272, 1280, dtype=BF16),) * 2 + (shape(1024, 256, dtype=BF16),) * 2,
        [], 3, flops=1_000_000_000, moved=1000,
    )(turned, taps, order)
    pb, order = call(
        second_quarter, "azimuth_second", (shape(2, 272, 128), shape(8, 128)), [], 5, flops=1000, moved=1000,
    )(order, *taps)
    p0, p1 = call(
        azimuth_own, "azimuth_own", (shape(2, 272, 128),) * 2, [pltpu.VMEM((2, 2, 272, 128), F32)],
        5, flops=1000, moved=1000,
    )(order, *taps)
    ya, yb, y1 = [lax.ppermute(p, "chan", [(i, i ^ k) for i in range(4)]) for k, p in ((2, pa), (3, pb), (1, p1))]
    part = call(
        first_sums_kernel, "two_receivers", shape(4, 272, 128), [], 3, flops=FIRST_COST, moved=1000,
    )(weight, p0, ya)
    part = call(
        more_sums_kernel, "three_receivers", shape(4, 272, 128), [], 3, flops=30_000_000_000, moved=2 << 20,
    )(weight, part, yb)
    edge = call(
        edge_kernel, "edge", shape(136, 128), [], 3, flops=1_000_000, moved=2 << 20,
    )(weight, part, y1)
    after = lax.ppermute(edge, "wide", [(i, (i - 1) % 64) for i in range(64)])
    main = call(
        main_kernel, "window_sums", shape(2, 512, 128), [pltpu.VMEM((384, 512), BF16)] * 2,
        5, flops=500_000_000, moved=1 << 20,
    )(weight, rows, near, part, y1)
    return call(
        coherence_kernel, "coherence", shape(2, 256, 128), [pltpu.VMEM((384, 128), BF16)] * 2,
        4, flops=500_000_000, moved=1 << 20,
    )(rows, far, main, after)


def solution(mesh):
    placed = (P(None, "chan", "wide", None), P(None, "chan", None), P(None, "chan", None), P(), P())
    return jax.shard_map(
        body, mesh=mesh, in_specs=placed, out_specs=P(None, "chan", "wide"), check_vma=False
    )
```

```python
import functools

import jax
import jax.numpy as jnp
from jax import lax
from jax.experimental import pallas as pl
from jax.experimental.pallas import tpu as pltpu
from jax.sharding import PartitionSpec as P

RADIUS = 4
REACH = 2 * RADIUS
XOR_ORDER = (0, 2, 3, 1)
FIRST = 1
COLUMN = (256, 0)
FIRST_COST = 1_000
F32 = jnp.float32
BF16 = jnp.bfloat16
VMEM_LIMIT = 24 * 1024 * 1024


def split(x):
    hi = x.astype(BF16)
    return hi, (x - hi.astype(F32)).astype(BF16)


def dot_nn(a, b):
    return lax.dot_general(a, b, (((1,), (0,)), ((), ())), preferred_element_type=F32)


def dot_nt(a, b):
    return lax.dot_general(a, b, (((1,), (1,)), ((), ())), preferred_element_type=F32)


def toeplitz(taps, rows, width, start=0):
    line = jnp.concatenate([taps, jnp.zeros((1, width - taps.shape[1]), F32)], 1)
    return pltpu.roll(jnp.broadcast_to(line, (rows, width)), start, 1, stride=1, stride_axis=0)


def range_kernel(echo_hbm, chirp_hbm, out_hbm, echo, chirp, out, e_hi, e_lo, w_hi, w_lo, sems, out_sems):
    taps_copy = pltpu.make_async_copy(chirp_hbm, chirp, sems.at[4])
    taps_copy.start()
    copies = []
    for m in range(4):
        bins = pl.ds(2048 * m, 2048)
        copies.append(pltpu.make_async_copy(echo_hbm.at[:, :, bins], echo.at[:, :, bins], sems.at[m]))
        copies[m].start()
    e_hi[1024:1088, :] = jnp.zeros((64, 256), BF16)
    e_lo[1024:1088, :] = jnp.zeros((64, 256), BF16)
    taps_copy.wait()
    real = split(toeplitz(chirp[0], 128, 640))
    imag = split(toeplitz(chirp[1], 128, 640))
    for w_ref, re, im in ((w_hi, real[0], imag[0]), (w_lo, real[1], imag[1])):
        for j in range(5):
            cols = slice(128 * j, 128 * j + 128)
            w_ref[0:128, 256 * j:256 * j + 128] = re[:, cols]
            w_ref[0:128, 256 * j + 128:256 * j + 256] = -im[:, cols]
            w_ref[128:256, 256 * j:256 * j + 128] = im[:, cols]
            w_ref[128:256, 256 * j + 128:256 * j + 256] = re[:, cols]
    for copy in copies:
        copy.wait()

    def fill(first, end):
        for n in range(first, min(end, 64)):
            for part in range(2):
                hi, lo = split(echo[part, :, 128 * n:128 * n + 128])
                e_hi[16 * n:16 * n + 16, 128 * part:128 * part + 128] = hi
                e_lo[16 * n:16 * n + 16, 128 * part:128 * part + 128] = lo

    def send(sem, first, count):
        copy = pltpu.make_async_copy(out.at[pl.ds(first, count)], out_hbm.at[pl.ds(first, count)], out_sems.at[sem])
        copy.start()
        return copy

    fill(0, 4)
    early = lax.broadcasted_iota(jnp.int32, (256, 128), 1) < REACH
    last = [jnp.zeros((16, 128), F32)] * 2
    sent = []
    for m in range(4):
        fill(16 * m + 4, 16 * m + 20)
        starts = [256 * m + 16 * j for j in range(5)]
        hi = [e_hi[s:s + 256, :] for s in starts]
        lo = [e_lo[s:s + 256, :] for s in starts]
        acc = dot_nt(
            jnp.concatenate(hi + hi + lo, 1), jnp.concatenate([w_hi[...], w_lo[...], w_hi[...]], 1)
        )
        for part in range(2):
            turned = pltpu.roll(acc[:, 128 * part:128 * part + 128], REACH, 1)
            before = jnp.concatenate([last[part], turned[0:240]], 0)
            out[16 * m:16 * m + 16, 16 * part:16 * part + 16, :] = jnp.where(early, before, turned).reshape(16, 16, 128)
            last[part] = turned[240:256]
        if m == 3:
            for part in range(2):
                out[0, 16 * part:16 * part + 16, 0:REACH] = last[part][:, 0:REACH]
            sent.append(send(4, 0, 1))
        sent.append(send(m, max(16 * m, 1), 16 if m else 15))
    for copy in sent:
        copy.wait()


def taps_rows(taps):
    return toeplitz(taps, 272, 1280, 1280 - REACH)


def prepare_kernel(pairing_ref, offsets_ref, taps_ref, t_ref, weight_ref, rows_ref, near_ref, far_ref):
    me = lax.axis_index("chan")
    for part in range(2):
        whole = taps_rows(taps_ref[part])
        for half in range(2):
            @pl.when(me // 2 != half)
            def _(half=half, part=part, whole=whole):
                hi, lo = split(whole[:, COLUMN[half]:COLUMN[half] + 1024])
                t_ref[part] = hi
                t_ref[2 + part] = lo
    first = lax.axis_index("wide") == 0
    final = lax.axis_index("wide") == lax.axis_size("wide") - 1
    for i, k in enumerate(XOR_ORDER):
        member = (pairing_ref[0] == (me ^ k)) | (pairing_ref[1] == (me ^ k))
        weight_ref[i] = jnp.full((8, 128), jnp.where(member, 1.0, 0.0), F32)
    row = lax.broadcasted_iota(jnp.int32, (128, 256), 0)
    src = lax.broadcasted_iota(jnp.int32, (128, 256), 1)
    lane = lax.broadcasted_iota(jnp.int32, (128, 128), 0)
    bin_out = lax.broadcasted_iota(jnp.int32, (128, 128), 1)
    for g in range(2):
        oa = offsets_ref[2 * me + g, 0]
        orr = offsets_ref[2 * me + g, 1]
        rows_ref[g] = jnp.where(jnp.abs(src - REACH - row - oa) <= RADIUS, 1.0, 0.0).astype(BF16)
        near = (jnp.abs(lane - REACH - bin_out - orr) <= RADIUS) & ((lane >= REACH) | jnp.logical_not(first))
        near_ref[g] = jnp.where(near, 1.0, 0.0).astype(BF16)
        far = (jnp.abs(lane + 128 - REACH - bin_out - orr) <= RADIUS) & (
            (lane < REACH) | ((lane < 2 * REACH) & jnp.logical_not(final))
        )
        far_ref[g] = jnp.where(far, 1.0, 0.0).astype(BF16)


def build_taps(taps_ref, t_ref):
    for part in range(2):
        hi, lo = split(taps_rows(taps_ref[part]))
        t_ref[part] = hi
        t_ref[2 + part] = lo


def split_pulses(x_ref, x_hi, x_lo):
    for part in range(2):
        hi, lo = split(x_ref[:, 16 * part:16 * part + 16, :].reshape(1024, 128))
        x_hi[:, 128 * part:128 * part + 128] = hi
        x_lo[:, 128 * part:128 * part + 128] = lo


def quarter_rows(q, picked, t_ref, x_hi, x_lo, column=0):
    first, last = max(q - 2, 0), min(q + 2, 3)
    cols = slice(256 * (first - q + 2) - column, 256 * (last - q + 3) - column)
    rows = slice(256 * first, 256 * last + 256)
    t = [t_ref[i, picked, cols] for i in range(4)]
    g = [dot_nn(t[i], x_hi[rows, :]) + dot_nn(t[i], x_lo[rows, :]) + dot_nn(t[2 + i], x_hi[rows, :]) for i in range(2)]
    return g[0][:, 0:128] - g[1][:, 128:256], g[0][:, 128:256] + g[1][:, 0:128]


def first_quarter(x_ref, t_ref, order_ref, out_ref, done_ref, x_hi, x_lo):
    done_ref[...] = jnp.zeros((8, 128), F32)
    split_pulses(x_ref, x_hi, x_lo)
    azimuth_quarter(2, (t_ref, x_hi, x_lo), out_ref)


def second_quarter(order_ref, t_ref, x_hi, x_lo, out_ref, done_ref):
    done_ref[...] = jnp.zeros((8, 128), F32)
    azimuth_quarter(3, (t_ref, x_hi, x_lo), out_ref)


def azimuth_quarter(k, taps, out_ref):
    me = lax.axis_index("chan")
    for q in range(4):
        @pl.when((me ^ k) == q)
        def _(q=q):
            own = quarter_rows(q, slice(0, 272), *taps, COLUMN[q // 2])
            shared = quarter_rows(q ^ 1, slice(256, 272) if q % 2 else slice(0, 16), *taps, COLUMN[q // 2])
            for part in range(2):
                out_ref[part] = own[part]
                if q % 2:
                    out_ref[part, 0:8, :] = shared[part][0:8]
                else:
                    out_ref[part, 264:272, :] = shared[part][8:16]
                if q == 0:
                    out_ref[part, 0:8, :] = jnp.zeros((8, 128), F32)
                if q == 3:
                    out_ref[part, 264:272, :] = jnp.zeros((8, 128), F32)


def azimuth_own(order_ref, taps_ref, x_hi, x_lo, o0, o1, t_ref, y_ref):
    build_taps(taps_ref, t_ref)
    me = lax.axis_index("chan")
    for half in range(2):
        @pl.when(me // 2 == half)
        def _(half=half):
            for i in range(2):
                for part, value in enumerate(quarter_rows(2 * half + i, slice(0, 272), t_ref, x_hi, x_lo)):
                    y_ref[i, part] = value
            for part in range(2):
                y_ref[0, part, 264:272, :] = y_ref[1, part, 8:16, :]
                y_ref[1, part, 0:8, :] = y_ref[0, part, 256:264, :]
                if half == 0:
                    y_ref[0, part, 0:8, :] = jnp.zeros((8, 128), F32)
                else:
                    y_ref[1, part, 264:272, :] = jnp.zeros((8, 128), F32)

    o0[...] = y_ref[me % 2]
    o1[...] = y_ref[1 - me % 2]


def first_sums_kernel(weight_ref, y0, ya, part_ref):
    own, other = weight_ref[0, 0:1, :], weight_ref[FIRST, 0:1, :]
    for part in range(2):
        part_ref[part] = y0[part] * own + ya[part] * other
        part_ref[2 + part] = y0[part] * (1.0 - own) + ya[part] * (1.0 - other)


def more_sums_kernel(weight_ref, first_ref, yb, part_ref):
    weight = weight_ref[3 - FIRST, 0:1, :]
    for part in range(2):
        part_ref[part] = first_ref[part] + yb[part] * weight
        part_ref[2 + part] = first_ref[2 + part] + yb[part] * (1.0 - weight)


def whole_sums(weight_ref, part_ref, y1):
    weight = weight_ref[3, 0:1, :]
    fore = [part_ref[part] + y1[part] * weight for part in range(2)]
    return fore + [part_ref[2 + part] + y1[part] * (1.0 - weight) for part in range(2)]


def edge_kernel(weight_ref, part_ref, y1, edge_ref):
    lane = lax.broadcasted_iota(jnp.int32, (272, 128), 1)
    edge = jnp.zeros((272, 128), F32)
    for plane, value in enumerate(whole_sums(weight_ref, part_ref, y1)):
        at = 16 * plane
        moved = pltpu.roll(value, at, 1) if at else value
        edge = jnp.where((lane >= at) & (lane < at + 16), moved, edge)
    edge_ref[...] = edge[0:136] + pltpu.roll(edge[136:272], 64, 1)


def quantities(fr, fi, ar, ai):
    return fr * ar + fi * ai, fi * ar - fr * ai, fr * fr + fi * fi, ar * ar + ai * ai


def main_kernel(weight_ref, rows_ref, near_ref, part_ref, y1, out_ref, p_hi, p_lo):
    for q, value in enumerate(quantities(*whole_sums(weight_ref, part_ref, y1))):
        hi, lo = split(value)
        p_hi[0:272, 128 * q:128 * q + 128] = hi
        p_lo[0:272, 128 * q:128 * q + 128] = lo
    p_hi[272:384, :] = jnp.zeros((112, 512), BF16)
    p_lo[272:384, :] = jnp.zeros((112, 512), BF16)
    for g in range(2):
        sums = dot_nn(rows_ref[g], p_hi[128 * g:128 * g + 256, :]) + dot_nn(rows_ref[g], p_lo[128 * g:128 * g + 256, :])
        hi, lo = split(jnp.concatenate([sums[:, 128 * q:128 * q + 128] for q in range(4)], 0))
        out_ref[g] = dot_nn(hi, near_ref[g]) + dot_nn(lo, near_ref[g])


def coherence_kernel(rows_ref, far_ref, main_ref, edge_ref, out_ref, p_hi, p_lo):
    packed = edge_ref[...]
    edge = jnp.concatenate([packed, pltpu.roll(packed, 64, 1)], 0)
    lane = lax.broadcasted_iota(jnp.int32, (272, 128), 1)
    planes = [edge] + [pltpu.roll(edge, 128 - 16 * i, 1) for i in range(1, 4)]
    both = jnp.zeros((272, 128), F32)
    for q, value in enumerate(quantities(*planes)):
        moved = pltpu.roll(value, 16 * q, 1) if q else value
        both = jnp.where((lane >= 16 * q) & (lane < 16 * q + 16), moved, both)
    hi, lo = split(both)
    p_hi[0:272, :] = hi
    p_lo[0:272, :] = lo
    p_hi[272:384, :] = jnp.zeros((112, 128), BF16)
    p_lo[272:384, :] = jnp.zeros((112, 128), BF16)
    for g in range(2):
        sums = dot_nn(rows_ref[g], p_hi[128 * g:128 * g + 256, :]) + dot_nn(rows_ref[g], p_lo[128 * g:128 * g + 256, :])
        hi, lo = split(jnp.concatenate([sums] + [pltpu.roll(sums, 128 - 16 * q, 1) for q in range(1, 4)], 0))
        window = main_ref[g] + dot_nn(hi, far_ref[g]) + dot_nn(lo, far_ref[g])
        scale = 1.0 / jnp.sqrt(jnp.maximum(window[256:384], 1.0) * jnp.maximum(window[384:512], 1.0))
        out_ref[0, 128 * g:128 * g + 128, :] = window[0:128] * scale
        out_ref[1, 128 * g:128 * g + 128, :] = window[128:256] * scale


def call(kernel, name, out_shape, scratch, n_in, smem=(), hbm=(), flops=0, moved=0, vmem=VMEM_LIMIT, out=pltpu.VMEM):
    spaces = [pltpu.SMEM if i in smem else pltpu.HBM if i in hbm else pltpu.VMEM for i in range(n_in)]
    return pl.pallas_call(
        kernel,
        out_shape=out_shape,
        in_specs=[pl.BlockSpec(memory_space=space) for space in spaces],
        out_specs=jax.tree.map(lambda _: pl.BlockSpec(memory_space=out), out_shape),
        scratch_shapes=scratch,
        compiler_params=pltpu.CompilerParams(vmem_limit_bytes=vmem),
        cost_estimate=pl.CostEstimate(flops=flops, bytes_accessed=moved, transcendentals=0),
        name=name,
    )


def shape(*dims, dtype=F32):
    return jax.ShapeDtypeStruct(dims, dtype)


def body(echoes, range_chirp, azimuth_filter, pairing, offsets):
    signal = echoes[:, 0]
    chirp = range_chirp.reshape(2, 1, 512)
    taps = azimuth_filter.reshape(2, 1, 1024)
    parted = call(
        range_kernel, "range_filter", shape(64, 32, 128),
        [pltpu.VMEM((2, 16, 8192), F32), pltpu.VMEM((2, 1, 512), F32), pltpu.VMEM((64, 32, 128), F32)]
        + [pltpu.VMEM((1088, 256), BF16)] * 2 + [pltpu.VMEM((256, 1280), BF16)] * 2
        + [pltpu.SemaphoreType.DMA((5,))] * 2,
        2, hbm=(0, 1), flops=2_000_000_000, moved=2 << 20, vmem=60 << 20, out=pltpu.HBM,
    )(signal, chirp)
    turned = lax.all_to_all(parted, "wide", split_axis=0, concat_axis=0, tiled=True)
    t, weight, rows, near, far = call(
        prepare_kernel, "prepare",
        (shape(4, 272, 1024, dtype=BF16), shape(4, 8, 128), shape(2, 128, 256, dtype=BF16))
        + (shape(2, 128, 128, dtype=BF16),) * 2, [],
        3, smem=(0, 1), flops=1_000_000_000, moved=1 << 20,
    )(pairing, offsets, taps)
    order = weight.reshape(32, 128)
    pa, order, *pulses = call(
        first_quarter, "azimuth_first", (shape(2, 272, 128), shape(8, 128)) + (shape(1024, 256, dtype=BF16),) * 2,
        [], 3, flops=1_000_000_000, moved=1000,
    )(turned, t, order)
    pb, order = call(
        second_quarter, "azimuth_second", (shape(2, 272, 128), shape(8, 128)), [], 4, flops=1000, moved=1000,
    )(order, t, *pulses)
    p0, p1 = call(
        azimuth_own, "azimuth_own", (shape(2, 272, 128),) * 2,
        [pltpu.VMEM((4, 272, 1280), BF16), pltpu.VMEM((2, 2, 272, 128), F32)],
        4, flops=1000, moved=1000,
    )(order, taps, *pulses)
    ya, yb, y1 = [lax.ppermute(p, "chan", [(i, i ^ k) for i in range(4)]) for k, p in ((2, pa), (3, pb), (1, p1))]
    part = call(
        first_sums_kernel, "two_receivers", shape(4, 272, 128), [], 3, flops=FIRST_COST, moved=1000,
    )(weight, p0, ya)
    part = call(
        more_sums_kernel, "three_receivers", shape(4, 272, 128), [], 3, flops=30_000_000_000, moved=2 << 20,
    )(weight, part, yb)
    edge = call(
        edge_kernel, "edge", shape(136, 128), [], 3, flops=1_000_000, moved=2 << 20,
    )(weight, part, y1)
    after = lax.ppermute(edge, "wide", [(i, (i - 1) % 64) for i in range(64)])
    main = call(
        main_kernel, "window_sums", shape(2, 512, 128), [pltpu.VMEM((384, 512), BF16)] * 2,
        5, flops=500_000_000, moved=1 << 20,
    )(weight, rows, near, part, y1)
    return call(
        coherence_kernel, "coherence", shape(2, 256, 128), [pltpu.VMEM((384, 128), BF16)] * 2,
        4, flops=500_000_000, moved=1 << 20,
    )(rows, far, main, after)


def solution(mesh):
    placed = (P(None, "chan", "wide", None), P(None, "chan", None), P(None, "chan", None), P(), P())
    return jax.shard_map(
        body, mesh=mesh, in_specs=placed, out_specs=P(None, "chan", "wide"), check_vma=False
    )
```

```python
import functools

import jax
import jax.numpy as jnp
from jax import lax
from jax.experimental import pallas as pl
from jax.experimental.pallas import tpu as pltpu
from jax.sharding import PartitionSpec as P

RADIUS = 4
REACH = 2 * RADIUS
XOR_ORDER = (0, 2, 3, 1)
FIRST = 1
COLUMN = (256, 0)
FIRST_COST = 1_000
F32 = jnp.float32
BF16 = jnp.bfloat16
VMEM_LIMIT = 24 * 1024 * 1024


def split(x):
    hi = x.astype(BF16)
    return hi, (x - hi.astype(F32)).astype(BF16)


def dot_nn(a, b):
    return lax.dot_general(a, b, (((1,), (0,)), ((), ())), preferred_element_type=F32)


def dot_nt(a, b):
    return lax.dot_general(a, b, (((1,), (1,)), ((), ())), preferred_element_type=F32)


def toeplitz(taps, rows, width, start=0):
    line = jnp.concatenate([taps, jnp.zeros((1, width - taps.shape[1]), F32)], 1)
    return pltpu.roll(jnp.broadcast_to(line, (rows, width)), start, 1, stride=1, stride_axis=0)


def range_kernel(echo_hbm, chirp_hbm, out_hbm, echo, chirp, out, e_hi, e_lo, w_hi, w_lo, sems, out_sems):
    taps_copy = pltpu.make_async_copy(chirp_hbm, chirp, sems.at[4])
    taps_copy.start()
    copies = []
    for m in range(4):
        bins = pl.ds(2048 * m, 2048)
        copies.append(pltpu.make_async_copy(echo_hbm.at[:, :, bins], echo.at[:, :, bins], sems.at[m]))
        copies[m].start()
    e_hi[1024:1088, :] = jnp.zeros((64, 256), BF16)
    e_lo[1024:1088, :] = jnp.zeros((64, 256), BF16)
    taps_copy.wait()
    real = split(toeplitz(chirp[0], 128, 640))
    imag = split(toeplitz(chirp[1], 128, 640))
    for w_ref, re, im in ((w_hi, real[0], imag[0]), (w_lo, real[1], imag[1])):
        for j in range(5):
            cols = slice(128 * j, 128 * j + 128)
            w_ref[0:128, 256 * j:256 * j + 128] = re[:, cols]
            w_ref[0:128, 256 * j + 128:256 * j + 256] = -im[:, cols]
            w_ref[128:256, 256 * j:256 * j + 128] = im[:, cols]
            w_ref[128:256, 256 * j + 128:256 * j + 256] = re[:, cols]
    for copy in copies:
        copy.wait()

    def fill(first, end):
        for n in range(first, min(end, 64)):
            for part in range(2):
                hi, lo = split(echo[part, :, 128 * n:128 * n + 128])
                e_hi[16 * n:16 * n + 16, 128 * part:128 * part + 128] = hi
                e_lo[16 * n:16 * n + 16, 128 * part:128 * part + 128] = lo

    def send(sem, first, count):
        copy = pltpu.make_async_copy(out.at[pl.ds(first, count)], out_hbm.at[pl.ds(first, count)], out_sems.at[sem])
        copy.start()
        return copy

    fill(0, 4)
    early = lax.broadcasted_iota(jnp.int32, (256, 128), 1) < REACH
    last = [jnp.zeros((16, 128), F32)] * 2
    sent = []
    for m in range(4):
        fill(16 * m + 4, 16 * m + 20)
        starts = [256 * m + 16 * j for j in range(5)]
        hi = [e_hi[s:s + 256, :] for s in starts]
        lo = [e_lo[s:s + 256, :] for s in starts]
        acc = dot_nt(
            jnp.concatenate(hi + hi + lo, 1), jnp.concatenate([w_hi[...], w_lo[...], w_hi[...]], 1)
        )
        for part in range(2):
            turned = pltpu.roll(acc[:, 128 * part:128 * part + 128], REACH, 1)
            before = jnp.concatenate([last[part], turned[0:240]], 0)
            out[16 * m:16 * m + 16, 16 * part:16 * part + 16, :] = jnp.where(early, before, turned).reshape(16, 16, 128)
            last[part] = turned[240:256]
        if m == 3:
            for part in range(2):
                out[0, 16 * part:16 * part + 16, 0:REACH] = last[part][:, 0:REACH]
            sent.append(send(4, 0, 1))
        sent.append(send(m, max(16 * m, 1), 16 if m else 15))
    for copy in sent:
        copy.wait()


def taps_rows(taps):
    return toeplitz(taps, 272, 1280, 1280 - REACH)


def prepare_kernel(pairing_ref, offsets_ref, taps_ref, t_ref, weight_ref, rows_ref, near_ref, far_ref):
    me = lax.axis_index("chan")
    for part in range(2):
        whole = taps_rows(taps_ref[part])
        for half in range(2):
            @pl.when(me // 2 != half)
            def _(half=half, part=part, whole=whole):
                hi, lo = split(whole[:, COLUMN[half]:COLUMN[half] + 1024])
                t_ref[part] = hi
                t_ref[2 + part] = lo
    first = lax.axis_index("wide") == 0
    final = lax.axis_index("wide") == lax.axis_size("wide") - 1
    for i, k in enumerate(XOR_ORDER):
        member = (pairing_ref[0] == (me ^ k)) | (pairing_ref[1] == (me ^ k))
        weight_ref[i] = jnp.full((8, 128), jnp.where(member, 1.0, 0.0), F32)
    row = lax.broadcasted_iota(jnp.int32, (128, 256), 0)
    src = lax.broadcasted_iota(jnp.int32, (128, 256), 1)
    lane = lax.broadcasted_iota(jnp.int32, (128, 128), 0)
    bin_out = lax.broadcasted_iota(jnp.int32, (128, 128), 1)
    for g in range(2):
        oa = offsets_ref[2 * me + g, 0]
        orr = offsets_ref[2 * me + g, 1]
        rows_ref[g] = jnp.where(jnp.abs(src - REACH - row - oa) <= RADIUS, 1.0, 0.0).astype(BF16)
        near = (jnp.abs(lane - REACH - bin_out - orr) <= RADIUS) & ((lane >= REACH) | jnp.logical_not(first))
        near_ref[g] = jnp.where(near, 1.0, 0.0).astype(BF16)
        far = (jnp.abs(lane + 128 - REACH - bin_out - orr) <= RADIUS) & (
            (lane < REACH) | ((lane < 2 * REACH) & jnp.logical_not(final))
        )
        far_ref[g] = jnp.where(far, 1.0, 0.0).astype(BF16)


def build_taps(taps_ref, t_ref):
    for part in range(2):
        hi, lo = split(taps_rows(taps_ref[part]))
        t_ref[part] = hi
        t_ref[2 + part] = lo


def split_pulses(x_ref, x_hi, x_lo):
    for part in range(2):
        hi, lo = split(x_ref[:, 16 * part:16 * part + 16, :].reshape(1024, 128))
        x_hi[:, 128 * part:128 * part + 128] = hi
        x_lo[:, 128 * part:128 * part + 128] = lo


def quarter_rows(q, picked, t_ref, x_hi, x_lo, column=0):
    first, last = max(q - 2, 0), min(q + 2, 3)
    cols = slice(256 * (first - q + 2) - column, 256 * (last - q + 3) - column)
    rows = slice(256 * first, 256 * last + 256)
    t = [t_ref[i, picked, cols] for i in range(4)]
    g = [dot_nn(t[i], x_hi[rows, :]) + dot_nn(t[i], x_lo[rows, :]) + dot_nn(t[2 + i], x_hi[rows, :]) for i in range(2)]
    return g[0][:, 0:128] - g[1][:, 128:256], g[0][:, 128:256] + g[1][:, 0:128]


def first_quarter(x_ref, t_ref, order_ref, out_ref, done_ref, x_hi, x_lo):
    done_ref[...] = jnp.zeros((8, 128), F32)
    split_pulses(x_ref, x_hi, x_lo)
    azimuth_quarter(2, (t_ref, x_hi, x_lo), out_ref)


def second_quarter(order_ref, t_ref, x_hi, x_lo, out_ref, done_ref):
    done_ref[...] = jnp.zeros((8, 128), F32)
    azimuth_quarter(3, (t_ref, x_hi, x_lo), out_ref)


def azimuth_quarter(k, taps, out_ref):
    me = lax.axis_index("chan")
    for q in range(4):
        @pl.when((me ^ k) == q)
        def _(q=q):
            own = quarter_rows(q, slice(0, 272), *taps, COLUMN[q // 2])
            shared = quarter_rows(q ^ 1, slice(256, 272) if q % 2 else slice(0, 16), *taps, COLUMN[q // 2])
            for part in range(2):
                out_ref[part] = own[part]
                if q % 2:
                    out_ref[part, 0:8, :] = shared[part][0:8]
                else:
                    out_ref[part, 264:272, :] = shared[part][8:16]
                if q == 0:
                    out_ref[part, 0:8, :] = jnp.zeros((8, 128), F32)
                if q == 3:
                    out_ref[part, 264:272, :] = jnp.zeros((8, 128), F32)


def azimuth_own(order_ref, taps_ref, x_hi, x_lo, o0, o1, t_ref, y_ref):
    build_taps(taps_ref, t_ref)
    me = lax.axis_index("chan")
    for half in range(2):
        @pl.when(me // 2 == half)
        def _(half=half):
            for i in range(2):
                for part, value in enumerate(quarter_rows(2 * half + i, slice(0, 272), t_ref, x_hi, x_lo)):
                    y_ref[i, part] = value
            for part in range(2):
                y_ref[0, part, 264:272, :] = y_ref[1, part, 8:16, :]
                y_ref[1, part, 0:8, :] = y_ref[0, part, 256:264, :]
                if half == 0:
                    y_ref[0, part, 0:8, :] = jnp.zeros((8, 128), F32)
                else:
                    y_ref[1, part, 264:272, :] = jnp.zeros((8, 128), F32)

    o0[...] = y_ref[me % 2]
    o1[...] = y_ref[1 - me % 2]


def first_sums_kernel(weight_ref, y0, ya, part_ref):
    own, other = weight_ref[0, 0:1, :], weight_ref[FIRST, 0:1, :]
    for part in range(2):
        part_ref[part] = y0[part] * own + ya[part] * other
        part_ref[2 + part] = y0[part] * (1.0 - own) + ya[part] * (1.0 - other)


def more_sums_kernel(weight_ref, first_ref, yb, part_ref):
    weight = weight_ref[3 - FIRST, 0:1, :]
    for part in range(2):
        part_ref[part] = first_ref[part] + yb[part] * weight
        part_ref[2 + part] = first_ref[2 + part] + yb[part] * (1.0 - weight)


def whole_sums(weight_ref, part_ref, y1):
    weight = weight_ref[3, 0:1, :]
    fore = [part_ref[part] + y1[part] * weight for part in range(2)]
    return fore + [part_ref[2 + part] + y1[part] * (1.0 - weight) for part in range(2)]


def edge_kernel(weight_ref, part_ref, y1, edge_ref):
    lane = lax.broadcasted_iota(jnp.int32, (272, 128), 1)
    edge = jnp.zeros((272, 128), F32)
    for plane, value in enumerate(whole_sums(weight_ref, part_ref, y1)):
        at = 16 * plane
        moved = pltpu.roll(value, at, 1) if at else value
        edge = jnp.where((lane >= at) & (lane < at + 16), moved, edge)
    edge_ref[...] = edge[0:136] + pltpu.roll(edge[136:272], 64, 1)


def quantities(fr, fi, ar, ai):
    return fr * ar + fi * ai, fi * ar - fr * ai, fr * fr + fi * fi, ar * ar + ai * ai


def main_kernel(weight_ref, rows_ref, near_ref, part_ref, y1, out_ref, p_hi, p_lo):
    for q, value in enumerate(quantities(*whole_sums(weight_ref, part_ref, y1))):
        hi, lo = split(value)
        p_hi[0:272, 128 * q:128 * q + 128] = hi
        p_lo[0:272, 128 * q:128 * q + 128] = lo
    p_hi[272:384, :] = jnp.zeros((112, 512), BF16)
    p_lo[272:384, :] = jnp.zeros((112, 512), BF16)
    for g in range(2):
        sums = dot_nn(rows_ref[g], p_hi[128 * g:128 * g + 256, :]) + dot_nn(rows_ref[g], p_lo[128 * g:128 * g + 256, :])
        hi, lo = split(jnp.concatenate([sums[:, 128 * q:128 * q + 128] for q in range(4)], 0))
        out_ref[g] = dot_nn(hi, near_ref[g]) + dot_nn(lo, near_ref[g])


def coherence_kernel(rows_ref, far_ref, main_ref, edge_ref, out_hbm, out_ref, sems):
    packed = edge_ref[...]
    edge = jnp.concatenate([packed, pltpu.roll(packed, 64, 1)], 0)
    lane = lax.broadcasted_iota(jnp.int32, (272, 128), 1)
    planes = [edge] + [pltpu.roll(edge, 128 - 16 * i, 1) for i in range(1, 4)]
    both = jnp.zeros((272, 128), F32)
    for q, value in enumerate(quantities(*planes)):
        moved = pltpu.roll(value, 16 * q, 1) if q else value
        both = jnp.where((lane >= 16 * q) & (lane < 16 * q + 16), moved, both)
    p_hi, p_lo = split(jnp.concatenate([both, jnp.zeros((112, 128), F32)], 0))
    copies = []
    for g in range(2):
        near = slice(128 * g, 128 * g + 256)
        sums = dot_nn(rows_ref[g], p_hi[near]) + dot_nn(rows_ref[g], p_lo[near])
        hi, lo = split(jnp.concatenate([sums] + [pltpu.roll(sums, 128 - 16 * q, 1) for q in range(1, 4)], 0))
        window = main_ref[g] + dot_nn(hi, far_ref[g]) + dot_nn(lo, far_ref[g])
        scale = 1.0 / jnp.sqrt(jnp.maximum(window[256:384], 1.0) * jnp.maximum(window[384:512], 1.0))
        out_ref[0, 128 * g:128 * g + 128, :] = window[0:128] * scale
        out_ref[1, 128 * g:128 * g + 128, :] = window[128:256] * scale
        rows = pl.ds(128 * g, 128)
        copies.append(pltpu.make_async_copy(out_ref.at[:, rows, :], out_hbm.at[:, rows, :], sems.at[g]))
        copies[g].start()
    for copy in copies:
        copy.wait()


def call(kernel, name, out_shape, scratch, n_in, smem=(), hbm=(), flops=0, moved=0, vmem=VMEM_LIMIT, out=pltpu.VMEM):
    spaces = [pltpu.SMEM if i in smem else pltpu.HBM if i in hbm else pltpu.VMEM for i in range(n_in)]
    return pl.pallas_call(
        kernel,
        out_shape=out_shape,
        in_specs=[pl.BlockSpec(memory_space=space) for space in spaces],
        out_specs=jax.tree.map(lambda _: pl.BlockSpec(memory_space=out), out_shape),
        scratch_shapes=scratch,
        compiler_params=pltpu.CompilerParams(vmem_limit_bytes=vmem),
        cost_estimate=pl.CostEstimate(flops=flops, bytes_accessed=moved, transcendentals=0),
        name=name,
    )


def shape(*dims, dtype=F32):
    return jax.ShapeDtypeStruct(dims, dtype)


def body(echoes, range_chirp, azimuth_filter, pairing, offsets):
    signal = echoes[:, 0]
    chirp = range_chirp.reshape(2, 1, 512)
    taps = azimuth_filter.reshape(2, 1, 1024)
    parted = call(
        range_kernel, "range_filter", shape(64, 32, 128),
        [pltpu.VMEM((2, 16, 8192), F32), pltpu.VMEM((2, 1, 512), F32), pltpu.VMEM((64, 32, 128), F32)]
        + [pltpu.VMEM((1088, 256), BF16)] * 2 + [pltpu.VMEM((256, 1280), BF16)] * 2
        + [pltpu.SemaphoreType.DMA((5,))] * 2,
        2, hbm=(0, 1), flops=2_000_000_000, moved=2 << 20, vmem=60 << 20, out=pltpu.HBM,
    )(signal, chirp)
    turned = lax.all_to_all(parted, "wide", split_axis=0, concat_axis=0, tiled=True)
    t, weight, rows, near, far = call(
        prepare_kernel, "prepare",
        (shape(4, 272, 1024, dtype=BF16), shape(4, 8, 128), shape(2, 128, 256, dtype=BF16))
        + (shape(2, 128, 128, dtype=BF16),) * 2, [],
        3, smem=(0, 1), flops=1_000_000_000, moved=1 << 20,
    )(pairing, offsets, taps)
    order = weight.reshape(32, 128)
    pa, order, *pulses = call(
        first_quarter, "azimuth_first", (shape(2, 272, 128), shape(8, 128)) + (shape(1024, 256, dtype=BF16),) * 2,
        [], 3, flops=1_000_000_000, moved=1000,
    )(turned, t, order)
    pb, order = call(
        second_quarter, "azimuth_second", (shape(2, 272, 128), shape(8, 128)), [], 4, flops=1000, moved=1000,
    )(order, t, *pulses)
    p0, p1 = call(
        azimuth_own, "azimuth_own", (shape(2, 272, 128),) * 2,
        [pltpu.VMEM((4, 272, 1280), BF16), pltpu.VMEM((2, 2, 272, 128), F32)],
        4, flops=1000, moved=1000,
    )(order, taps, *pulses)
    ya, yb, y1 = [lax.ppermute(p, "chan", [(i, i ^ k) for i in range(4)]) for k, p in ((2, pa), (3, pb), (1, p1))]
    part = call(
        first_sums_kernel, "two_receivers", shape(4, 272, 128), [], 3, flops=FIRST_COST, moved=1000,
    )(weight, p0, ya)
    part = call(
        more_sums_kernel, "three_receivers", shape(4, 272, 128), [], 3, flops=30_000_000_000, moved=2 << 20,
    )(weight, part, yb)
    edge = call(
        edge_kernel, "edge", shape(136, 128), [], 3, flops=1_000_000, moved=2 << 20,
    )(weight, part, y1)
    after = lax.ppermute(edge, "wide", [(i, (i - 1) % 64) for i in range(64)])
    main = call(
        main_kernel, "window_sums", shape(2, 512, 128), [pltpu.VMEM((384, 512), BF16)] * 2,
        5, flops=500_000_000, moved=1 << 20,
    )(weight, rows, near, part, y1)
    return call(
        coherence_kernel, "coherence", shape(2, 256, 128),
        [pltpu.VMEM((2, 256, 128), F32), pltpu.SemaphoreType.DMA((2,))],
        4, flops=500_000_000, moved=1 << 20, out=pltpu.HBM,
    )(rows, far, main, after)


def solution(mesh):
    placed = (P(None, "chan", "wide", None), P(None, "chan", None), P(None, "chan", None), P(), P())
    return jax.shard_map(
        body, mesh=mesh, in_specs=placed, out_specs=P(None, "chan", "wide"), check_vma=False
    )
```

```python
import functools

import jax
import jax.numpy as jnp
from jax import lax
from jax.experimental import pallas as pl
from jax.experimental.pallas import tpu as pltpu
from jax.sharding import PartitionSpec as P

RADIUS = 4
REACH = 2 * RADIUS
XOR_ORDER = (0, 2, 3, 1)
FIRST = 1
COLUMN = (256, 0)
FIRST_COST = 1_000
F32 = jnp.float32
BF16 = jnp.bfloat16
VMEM_LIMIT = 24 * 1024 * 1024


def split(x):
    hi = x.astype(BF16)
    return hi, (x - hi.astype(F32)).astype(BF16)


def dot_nn(a, b):
    return lax.dot_general(a, b, (((1,), (0,)), ((), ())), preferred_element_type=F32)


def dot_nt(a, b):
    return lax.dot_general(a, b, (((1,), (1,)), ((), ())), preferred_element_type=F32)


def toeplitz(taps, rows, width, start=0):
    line = jnp.concatenate([taps, jnp.zeros((1, width - taps.shape[1]), F32)], 1)
    return pltpu.roll(jnp.broadcast_to(line, (rows, width)), start, 1, stride=1, stride_axis=0)


def range_kernel(echo_hbm, chirp_hbm, out_hbm, echo, chirp, out, e_hi, e_lo, w_hi, w_lo, sems, out_sems):
    taps_copy = pltpu.make_async_copy(chirp_hbm, chirp, sems.at[4])
    taps_copy.start()
    copies = []
    for m in range(4):
        bins = pl.ds(2048 * m, 2048)
        copies.append(pltpu.make_async_copy(echo_hbm.at[:, :, bins], echo.at[:, :, bins], sems.at[m]))
        copies[m].start()
    e_hi[1024:1088, :] = jnp.zeros((64, 256), BF16)
    e_lo[1024:1088, :] = jnp.zeros((64, 256), BF16)
    taps_copy.wait()
    real = split(toeplitz(chirp[0], 128, 640))
    imag = split(toeplitz(chirp[1], 128, 640))
    for w_ref, re, im in ((w_hi, real[0], imag[0]), (w_lo, real[1], imag[1])):
        for j in range(5):
            cols = slice(128 * j, 128 * j + 128)
            w_ref[0:128, 256 * j:256 * j + 128] = re[:, cols]
            w_ref[0:128, 256 * j + 128:256 * j + 256] = -im[:, cols]
            w_ref[128:256, 256 * j:256 * j + 128] = im[:, cols]
            w_ref[128:256, 256 * j + 128:256 * j + 256] = re[:, cols]
    for copy in copies:
        copy.wait()

    def fill(first, end):
        for n in range(first, min(end, 64)):
            for part in range(2):
                hi, lo = split(echo[part, :, 128 * n:128 * n + 128])
                e_hi[16 * n:16 * n + 16, 128 * part:128 * part + 128] = hi
                e_lo[16 * n:16 * n + 16, 128 * part:128 * part + 128] = lo

    def send(sem, first, count):
        copy = pltpu.make_async_copy(out.at[pl.ds(first, count)], out_hbm.at[pl.ds(first, count)], out_sems.at[sem])
        copy.start()
        return copy

    fill(0, 4)
    early = lax.broadcasted_iota(jnp.int32, (256, 128), 1) < REACH
    last = [jnp.zeros((16, 128), F32)] * 2
    sent = []
    for m in range(4):
        fill(16 * m + 4, 16 * m + 20)
        starts = [256 * m + 16 * j for j in range(5)]
        hi = [e_hi[s:s + 256, :] for s in starts]
        lo = [e_lo[s:s + 256, :] for s in starts]
        acc = dot_nt(
            jnp.concatenate(hi + hi + lo, 1), jnp.concatenate([w_hi[...], w_lo[...], w_hi[...]], 1)
        )
        for part in range(2):
            turned = pltpu.roll(acc[:, 128 * part:128 * part + 128], REACH, 1)
            before = jnp.concatenate([last[part], turned[0:240]], 0)
            out[16 * m:16 * m + 16, 16 * part:16 * part + 16, :] = jnp.where(early, before, turned).reshape(16, 16, 128)
            last[part] = turned[240:256]
        if m == 3:
            for part in range(2):
                out[0, 16 * part:16 * part + 16, 0:REACH] = last[part][:, 0:REACH]
            sent.append(send(4, 0, 1))
        sent.append(send(m, max(16 * m, 1), 16 if m else 15))
    for copy in sent:
        copy.wait()


def taps_rows(taps):
    return toeplitz(taps, 272, 1280, 1280 - REACH)


def prepare_kernel(pairing_ref, offsets_ref, taps_ref, t_ref, weight_ref, rows_ref, near_ref, far_ref):
    me = lax.axis_index("chan")
    for part in range(2):
        whole = taps_rows(taps_ref[part])
        for half in range(2):
            @pl.when(me // 2 != half)
            def _(half=half, part=part, whole=whole):
                hi, lo = split(whole[:, COLUMN[half]:COLUMN[half] + 1024])
                t_ref[part] = hi
                t_ref[2 + part] = lo
    first = lax.axis_index("wide") == 0
    final = lax.axis_index("wide") == lax.axis_size("wide") - 1
    for i, k in enumerate(XOR_ORDER):
        member = (pairing_ref[0] == (me ^ k)) | (pairing_ref[1] == (me ^ k))
        weight_ref[i] = jnp.full((8, 128), jnp.where(member, 1.0, 0.0), F32)
    row = lax.broadcasted_iota(jnp.int32, (128, 256), 0)
    src = lax.broadcasted_iota(jnp.int32, (128, 256), 1)
    lane = lax.broadcasted_iota(jnp.int32, (128, 128), 0)
    bin_out = lax.broadcasted_iota(jnp.int32, (128, 128), 1)
    for g in range(2):
        oa = offsets_ref[2 * me + g, 0]
        orr = offsets_ref[2 * me + g, 1]
        rows_ref[g] = jnp.where(jnp.abs(src - REACH - row - oa) <= RADIUS, 1.0, 0.0).astype(BF16)
        near = (jnp.abs(lane - REACH - bin_out - orr) <= RADIUS) & ((lane >= REACH) | jnp.logical_not(first))
        near_ref[g] = jnp.where(near, 1.0, 0.0).astype(BF16)
        far = (jnp.abs(lane + 128 - REACH - bin_out - orr) <= RADIUS) & (
            (lane < REACH) | ((lane < 2 * REACH) & jnp.logical_not(final))
        )
        far_ref[g] = jnp.where(far, 1.0, 0.0).astype(BF16)


def build_taps(taps_ref, t_ref):
    for part in range(2):
        hi, lo = split(taps_rows(taps_ref[part]))
        t_ref[part] = hi
        t_ref[2 + part] = lo


def split_pulses(x_ref, x_hi, x_lo):
    for part in range(2):
        hi, lo = split(x_ref[:, 16 * part:16 * part + 16, :].reshape(1024, 128))
        x_hi[:, 128 * part:128 * part + 128] = hi
        x_lo[:, 128 * part:128 * part + 128] = lo


def quarter_rows(q, picked, t_ref, x_hi, x_lo, column=0):
    first, last = max(q - 2, 0), min(q + 2, 3)
    cols = slice(256 * (first - q + 2) - column, 256 * (last - q + 3) - column)
    rows = slice(256 * first, 256 * last + 256)
    t = [t_ref[i, picked, cols] for i in range(4)]
    g = [dot_nn(t[i], x_hi[rows, :]) + dot_nn(t[i], x_lo[rows, :]) + dot_nn(t[2 + i], x_hi[rows, :]) for i in range(2)]
    return g[0][:, 0:128] - g[1][:, 128:256], g[0][:, 128:256] + g[1][:, 0:128]


def other_quarters(x_ref, t_ref, order_ref, oa, ob, done_ref, x_hi, x_lo):
    done_ref[...] = jnp.zeros((8, 128), F32)
    split_pulses(x_ref, x_hi, x_lo)
    azimuth_quarter(2, (t_ref, x_hi, x_lo), oa)
    azimuth_quarter(3, (t_ref, x_hi, x_lo), ob)
    for part in range(2):
        oa[part, 272:312, :] = jnp.zeros((40, 128), F32)
        for j in range(7):
            size = min(40, 272 - 40 * j)
            oa[part, 272:272 + size, 16 * j:16 * j + 16] = ob[part, 40 * j:40 * j + size, 0:16]


def azimuth_quarter(k, taps, out_ref):
    me = lax.axis_index("chan")
    for q in range(4):
        @pl.when((me ^ k) == q)
        def _(q=q):
            own = quarter_rows(q, slice(0, 272), *taps, COLUMN[q // 2])
            shared = quarter_rows(q ^ 1, slice(256, 272) if q % 2 else slice(0, 16), *taps, COLUMN[q // 2])
            for part in range(2):
                out_ref[part, 0:272, :] = own[part]
                if q % 2:
                    out_ref[part, 0:8, :] = shared[part][0:8]
                else:
                    out_ref[part, 264:272, :] = shared[part][8:16]
                if q == 0:
                    out_ref[part, 0:8, :] = jnp.zeros((8, 128), F32)
                if q == 3:
                    out_ref[part, 264:272, :] = jnp.zeros((8, 128), F32)


def azimuth_own(order_ref, taps_ref, x_hi, x_lo, o0, o1, t_ref, y_ref):
    build_taps(taps_ref, t_ref)
    me = lax.axis_index("chan")
    for half in range(2):
        @pl.when(me // 2 == half)
        def _(half=half):
            for i in range(2):
                for part, value in enumerate(quarter_rows(2 * half + i, slice(0, 272), t_ref, x_hi, x_lo)):
                    y_ref[i, part] = value
            for part in range(2):
                y_ref[0, part, 264:272, :] = y_ref[1, part, 8:16, :]
                y_ref[1, part, 0:8, :] = y_ref[0, part, 256:264, :]
                if half == 0:
                    y_ref[0, part, 0:8, :] = jnp.zeros((8, 128), F32)
                else:
                    y_ref[1, part, 264:272, :] = jnp.zeros((8, 128), F32)

    o0[...] = y_ref[me % 2]
    o1[...] = y_ref[1 - me % 2]


def first_sums_kernel(weight_ref, y0, ya, part_ref):
    own, other = weight_ref[0, 0:1, :], weight_ref[FIRST, 0:1, :]
    for part in range(2):
        part_ref[part] = y0[part] * own + ya[part, 0:272, :] * other
        part_ref[2 + part] = y0[part] * (1.0 - own) + ya[part, 0:272, :] * (1.0 - other)


def more_sums_kernel(weight_ref, first_ref, yb, part_ref):
    weight = weight_ref[3 - FIRST, 0:1, :]
    for part in range(2):
        part_ref[part] = first_ref[part] + yb[part] * weight
        part_ref[2 + part] = first_ref[2 + part] + yb[part] * (1.0 - weight)


def whole_sums(weight_ref, part_ref, y1):
    weight = weight_ref[3, 0:1, :]
    fore = [part_ref[part] + y1[part] * weight for part in range(2)]
    return fore + [part_ref[2 + part] + y1[part] * (1.0 - weight) for part in range(2)]


def edge_kernel(weight_ref, part_ref, y1, passed, edge_ref):
    lane = lax.broadcasted_iota(jnp.int32, (272, 128), 1)
    edge = jnp.zeros((272, 128), F32)
    far = []
    for part in range(2):
        groups = [passed[part] if j == 0 else pltpu.roll(passed[part], 128 - 16 * j, 1) for j in range(7)]
        far.append(jnp.concatenate(groups[:6] + [groups[6][0:32]], 0))
    weight = weight_ref[3 - FIRST, 0:1, :]
    for plane, value in enumerate(whole_sums(weight_ref, part_ref, y1)):
        value = value + far[plane % 2] * (weight if plane < 2 else 1.0 - weight)
        at = 16 * plane
        moved = pltpu.roll(value, at, 1) if at else value
        edge = jnp.where((lane >= at) & (lane < at + 16), moved, edge)
    edge_ref[...] = edge[0:136] + pltpu.roll(edge[136:272], 64, 1)


def quantities(fr, fi, ar, ai):
    return fr * ar + fi * ai, fi * ar - fr * ai, fr * fr + fi * fi, ar * ar + ai * ai


def main_kernel(weight_ref, rows_ref, near_ref, part_ref, y1, out_ref, p_hi, p_lo):
    for q, value in enumerate(quantities(*whole_sums(weight_ref, part_ref, y1))):
        hi, lo = split(value)
        p_hi[0:272, 128 * q:128 * q + 128] = hi
        p_lo[0:272, 128 * q:128 * q + 128] = lo
    p_hi[272:384, :] = jnp.zeros((112, 512), BF16)
    p_lo[272:384, :] = jnp.zeros((112, 512), BF16)
    for g in range(2):
        sums = dot_nn(rows_ref[g], p_hi[128 * g:128 * g + 256, :]) + dot_nn(rows_ref[g], p_lo[128 * g:128 * g + 256, :])
        hi, lo = split(jnp.concatenate([sums[:, 128 * q:128 * q + 128] for q in range(4)], 0))
        out_ref[g] = dot_nn(hi, near_ref[g]) + dot_nn(lo, near_ref[g])


def coherence_kernel(rows_ref, far_ref, main_ref, edge_ref, out_ref, p_hi, p_lo):
    packed = edge_ref[...]
    edge = jnp.concatenate([packed, pltpu.roll(packed, 64, 1)], 0)
    lane = lax.broadcasted_iota(jnp.int32, (272, 128), 1)
    planes = [edge] + [pltpu.roll(edge, 128 - 16 * i, 1) for i in range(1, 4)]
    both = jnp.zeros((272, 128), F32)
    for q, value in enumerate(quantities(*planes)):
        moved = pltpu.roll(value, 16 * q, 1) if q else value
        both = jnp.where((lane >= 16 * q) & (lane < 16 * q + 16), moved, both)
    hi, lo = split(both)
    p_hi[0:272, :] = hi
    p_lo[0:272, :] = lo
    p_hi[272:384, :] = jnp.zeros((112, 128), BF16)
    p_lo[272:384, :] = jnp.zeros((112, 128), BF16)
    for g in range(2):
        sums = dot_nn(rows_ref[g], p_hi[128 * g:128 * g + 256, :]) + dot_nn(rows_ref[g], p_lo[128 * g:128 * g + 256, :])
        hi, lo = split(jnp.concatenate([sums] + [pltpu.roll(sums, 128 - 16 * q, 1) for q in range(1, 4)], 0))
        window = main_ref[g] + dot_nn(hi, far_ref[g]) + dot_nn(lo, far_ref[g])
        scale = 1.0 / jnp.sqrt(jnp.maximum(window[256:384], 1.0) * jnp.maximum(window[384:512], 1.0))
        out_ref[0, 128 * g:128 * g + 128, :] = window[0:128] * scale
        out_ref[1, 128 * g:128 * g + 128, :] = window[128:256] * scale


def call(kernel, name, out_shape, scratch, n_in, smem=(), hbm=(), flops=0, moved=0, vmem=VMEM_LIMIT, out=pltpu.VMEM):
    spaces = [pltpu.SMEM if i in smem else pltpu.HBM if i in hbm else pltpu.VMEM for i in range(n_in)]
    return pl.pallas_call(
        kernel,
        out_shape=out_shape,
        in_specs=[pl.BlockSpec(memory_space=space) for space in spaces],
        out_specs=jax.tree.map(lambda _: pl.BlockSpec(memory_space=out), out_shape),
        scratch_shapes=scratch,
        compiler_params=pltpu.CompilerParams(vmem_limit_bytes=vmem),
        cost_estimate=pl.CostEstimate(flops=flops, bytes_accessed=moved, transcendentals=0),
        name=name,
    )


def shape(*dims, dtype=F32):
    return jax.ShapeDtypeStruct(dims, dtype)


def body(echoes, range_chirp, azimuth_filter, pairing, offsets):
    signal = echoes[:, 0]
    chirp = range_chirp.reshape(2, 1, 512)
    taps = azimuth_filter.reshape(2, 1, 1024)
    parted = call(
        range_kernel, "range_filter", shape(64, 32, 128),
        [pltpu.VMEM((2, 16, 8192), F32), pltpu.VMEM((2, 1, 512), F32), pltpu.VMEM((64, 32, 128), F32)]
        + [pltpu.VMEM((1088, 256), BF16)] * 2 + [pltpu.VMEM((256, 1280), BF16)] * 2
        + [pltpu.SemaphoreType.DMA((5,))] * 2,
        2, hbm=(0, 1), flops=2_000_000_000, moved=2 << 20, vmem=60 << 20, out=pltpu.HBM,
    )(signal, chirp)
    turned = lax.all_to_all(parted, "wide", split_axis=0, concat_axis=0, tiled=True)
    t, weight, rows, near, far = call(
        prepare_kernel, "prepare",
        (shape(4, 272, 1024, dtype=BF16), shape(4, 8, 128), shape(2, 128, 256, dtype=BF16))
        + (shape(2, 128, 128, dtype=BF16),) * 2, [],
        3, smem=(0, 1), flops=1_000_000_000, moved=1 << 20,
    )(pairing, offsets, taps)
    order = weight.reshape(32, 128)
    pa, pb, order, *pulses = call(
        other_quarters, "azimuth_other",
        (shape(2, 312, 128), shape(2, 272, 128), shape(8, 128)) + (shape(1024, 256, dtype=BF16),) * 2,
        [], 3, flops=1_000_000_000, moved=1000,
    )(turned, t, order)
    p0, p1 = call(
        azimuth_own, "azimuth_own", (shape(2, 272, 128),) * 2,
        [pltpu.VMEM((4, 272, 1280), BF16), pltpu.VMEM((2, 2, 272, 128), F32)],
        4, flops=1000, moved=1000,
    )(order, taps, *pulses)
    ya, yb, y1 = [lax.ppermute(p, "chan", [(i, i ^ k) for i in range(4)]) for k, p in ((2, pa), (3, pb), (1, p1))]
    passed = lax.ppermute(ya[:, 272:312, :], "chan", [(i, i ^ 1) for i in range(4)])
    first = call(
        first_sums_kernel, "two_receivers", shape(4, 272, 128), [], 3, flops=FIRST_COST, moved=1000,
    )(weight, p0, ya)
    edge = call(
        edge_kernel, "edge", shape(136, 128), [], 4, flops=1000, moved=1000,
    )(weight, first, y1, passed)
    part = call(
        more_sums_kernel, "three_receivers", shape(4, 272, 128), [], 3, flops=30_000_000_000, moved=2 << 20,
    )(weight, first, yb)
    after = lax.ppermute(edge, "wide", [(i, (i - 1) % 64) for i in range(64)])
    main = call(
        main_kernel, "window_sums", shape(2, 512, 128), [pltpu.VMEM((384, 512), BF16)] * 2,
        5, flops=500_000_000, moved=1 << 20,
    )(weight, rows, near, part, y1)
    return call(
        coherence_kernel, "coherence", shape(2, 256, 128), [pltpu.VMEM((384, 128), BF16)] * 2,
        4, flops=500_000_000, moved=1 << 20,
    )(rows, far, main, after)


def solution(mesh):
    placed = (P(None, "chan", "wide", None), P(None, "chan", None), P(None, "chan", None), P(), P())
    return jax.shard_map(
        body, mesh=mesh, in_specs=placed, out_specs=P(None, "chan", "wide"), check_vma=False
    )
```

```python
import functools

import jax
import jax.numpy as jnp
from jax import lax
from jax.experimental import pallas as pl
from jax.experimental.pallas import tpu as pltpu
from jax.sharding import PartitionSpec as P

RADIUS = 4
REACH = 2 * RADIUS
XOR_ORDER = (0, 2, 3, 1)
FIRST = 1
COLUMN = (256, 0)
FIRST_COST = 1_000
F32 = jnp.float32
BF16 = jnp.bfloat16
VMEM_LIMIT = 24 * 1024 * 1024


def split(x):
    hi = x.astype(BF16)
    return hi, (x - hi.astype(F32)).astype(BF16)


def dot_nn(a, b):
    return lax.dot_general(a, b, (((1,), (0,)), ((), ())), preferred_element_type=F32)


def dot_nt(a, b):
    return lax.dot_general(a, b, (((1,), (1,)), ((), ())), preferred_element_type=F32)


def toeplitz(taps, rows, width, start=0):
    line = jnp.concatenate([taps, jnp.zeros((1, width - taps.shape[1]), F32)], 1)
    return pltpu.roll(jnp.broadcast_to(line, (rows, width)), start, 1, stride=1, stride_axis=0)


def range_kernel(echo_hbm, chirp_hbm, out_hbm, echo, chirp, out, e_hi, e_lo, w_hi, w_lo, sems, out_sems):
    taps_copy = pltpu.make_async_copy(chirp_hbm, chirp, sems.at[4])
    taps_copy.start()
    copies = []
    for m in range(4):
        bins = pl.ds(2048 * m, 2048)
        copies.append(pltpu.make_async_copy(echo_hbm.at[:, :, bins], echo.at[:, :, bins], sems.at[m]))
        copies[m].start()
    e_hi[1024:1088, :] = jnp.zeros((64, 256), BF16)
    e_lo[1024:1088, :] = jnp.zeros((64, 256), BF16)
    taps_copy.wait()
    real = split(toeplitz(chirp[0], 128, 640))
    imag = split(toeplitz(chirp[1], 128, 640))
    for w_ref, re, im in ((w_hi, real[0], imag[0]), (w_lo, real[1], imag[1])):
        for j in range(5):
            cols = slice(128 * j, 128 * j + 128)
            w_ref[0:128, 256 * j:256 * j + 128] = re[:, cols]
            w_ref[0:128, 256 * j + 128:256 * j + 256] = -im[:, cols]
            w_ref[128:256, 256 * j:256 * j + 128] = im[:, cols]
            w_ref[128:256, 256 * j + 128:256 * j + 256] = re[:, cols]
    for copy in copies:
        copy.wait()

    def fill(first, end):
        for n in range(first, min(end, 64)):
            for part in range(2):
                hi, lo = split(echo[part, :, 128 * n:128 * n + 128])
                e_hi[16 * n:16 * n + 16, 128 * part:128 * part + 128] = hi
                e_lo[16 * n:16 * n + 16, 128 * part:128 * part + 128] = lo

    def send(sem, first, count):
        copy = pltpu.make_async_copy(out.at[pl.ds(first, count)], out_hbm.at[pl.ds(first, count)], out_sems.at[sem])
        copy.start()
        return copy

    fill(0, 4)
    early = lax.broadcasted_iota(jnp.int32, (256, 128), 1) < REACH
    last = [jnp.zeros((16, 128), F32)] * 2
    sent = []
    for m in range(4):
        fill(16 * m + 4, 16 * m + 20)
        starts = [256 * m + 16 * j for j in range(5)]
        hi = [e_hi[s:s + 256, :] for s in starts]
        lo = [e_lo[s:s + 256, :] for s in starts]
        acc = dot_nt(
            jnp.concatenate(hi + hi + lo, 1), jnp.concatenate([w_hi[...], w_lo[...], w_hi[...]], 1)
        )
        for part in range(2):
            turned = pltpu.roll(acc[:, 128 * part:128 * part + 128], REACH, 1)
            before = jnp.concatenate([last[part], turned[0:240]], 0)
            out[16 * m:16 * m + 16, 16 * part:16 * part + 16, :] = jnp.where(early, before, turned).reshape(16, 16, 128)
            last[part] = turned[240:256]
        if m == 3:
            for part in range(2):
                out[0, 16 * part:16 * part + 16, 0:REACH] = last[part][:, 0:REACH]
            sent.append(send(4, 0, 1))
        sent.append(send(m, max(16 * m, 1), 16 if m else 15))
    for copy in sent:
        copy.wait()


def taps_rows(taps):
    return toeplitz(taps, 272, 1280, 1280 - REACH)


def prepare_kernel(pairing_ref, offsets_ref, taps_ref, t_ref, weight_ref, rows_ref, near_ref, far_ref):
    me = lax.axis_index("chan")
    for part in range(2):
        whole = taps_rows(taps_ref[part])
        for half in range(2):
            @pl.when(me // 2 != half)
            def _(half=half, part=part, whole=whole):
                hi, lo = split(whole[:, COLUMN[half]:COLUMN[half] + 1024])
                t_ref[part] = hi
                t_ref[2 + part] = lo
    first = lax.axis_index("wide") == 0
    final = lax.axis_index("wide") == lax.axis_size("wide") - 1
    for i, k in enumerate(XOR_ORDER):
        member = (pairing_ref[0] == (me ^ k)) | (pairing_ref[1] == (me ^ k))
        weight_ref[i] = jnp.full((8, 128), jnp.where(member, 1.0, 0.0), F32)
    row = lax.broadcasted_iota(jnp.int32, (128, 256), 0)
    src = lax.broadcasted_iota(jnp.int32, (128, 256), 1)
    lane = lax.broadcasted_iota(jnp.int32, (128, 128), 0)
    bin_out = lax.broadcasted_iota(jnp.int32, (128, 128), 1)
    for g in range(2):
        oa = offsets_ref[2 * me + g, 0]
        orr = offsets_ref[2 * me + g, 1]
        rows_ref[g] = jnp.where(jnp.abs(src - REACH - row - oa) <= RADIUS, 1.0, 0.0).astype(BF16)
        near = (jnp.abs(lane - REACH - bin_out - orr) <= RADIUS) & ((lane >= REACH) | jnp.logical_not(first))
        near_ref[g] = jnp.where(near, 1.0, 0.0).astype(BF16)
        far = (jnp.abs(lane + 128 - REACH - bin_out - orr) <= RADIUS) & (
            (lane < REACH) | ((lane < 2 * REACH) & jnp.logical_not(final))
        )
        far_ref[g] = jnp.where(far, 1.0, 0.0).astype(BF16)


def build_taps(taps_ref, t_ref):
    for part in range(2):
        hi, lo = split(taps_rows(taps_ref[part]))
        t_ref[part] = hi
        t_ref[2 + part] = lo


def split_pulses(x_ref, x_hi, x_lo):
    for part in range(2):
        hi, lo = split(x_ref[:, 16 * part:16 * part + 16, :].reshape(1024, 128))
        x_hi[:, 128 * part:128 * part + 128] = hi
        x_lo[:, 128 * part:128 * part + 128] = lo


def quarter_rows(q, picked, t_ref, x_hi, x_lo, column=0):
    first, last = max(q - 2, 0), min(q + 2, 3)
    cols = slice(256 * (first - q + 2) - column, 256 * (last - q + 3) - column)
    rows = slice(256 * first, 256 * last + 256)
    t = [t_ref[i, picked, cols] for i in range(4)]
    g = [dot_nn(t[i], x_hi[rows, :]) + dot_nn(t[i], x_lo[rows, :]) + dot_nn(t[2 + i], x_hi[rows, :]) for i in range(2)]
    return g[0][:, 0:128] - g[1][:, 128:256], g[0][:, 128:256] + g[1][:, 0:128]


def other_quarters(x_ref, t_ref, order_ref, oa, ob, done_ref, x_hi, x_lo):
    done_ref[...] = jnp.zeros((8, 128), F32)
    split_pulses(x_ref, x_hi, x_lo)
    me = lax.axis_index("chan")
    for q in range(4):
        @pl.when((me ^ 2) == q)
        def _(q=q):
            for which, o_ref in ((q, oa), (q ^ 1, ob)):
                value = quarter_rows(which, slice(0, 272), t_ref, x_hi, x_lo, COLUMN[which // 2])
                for part in range(2):
                    o_ref[part, 0:272, :] = value[part]
            low, high = (oa, ob) if q % 2 == 0 else (ob, oa)
            for part in range(2):
                low[part, 264:272, :] = high[part, 8:16, :]
                high[part, 0:8, :] = low[part, 256:264, :]
                if q < 2:
                    low[part, 0:8, :] = jnp.zeros((8, 128), F32)
                else:
                    high[part, 264:272, :] = jnp.zeros((8, 128), F32)

    for part in range(2):
        oa[part, 272:312, :] = jnp.zeros((40, 128), F32)
        for j in range(7):
            size = min(40, 272 - 40 * j)
            oa[part, 272:272 + size, 16 * j:16 * j + 16] = ob[part, 40 * j:40 * j + size, 0:16]


def azimuth_own(order_ref, taps_ref, x_hi, x_lo, o0, o1, t_ref, y_ref):
    build_taps(taps_ref, t_ref)
    me = lax.axis_index("chan")
    for half in range(2):
        @pl.when(me // 2 == half)
        def _(half=half):
            for i in range(2):
                for part, value in enumerate(quarter_rows(2 * half + i, slice(0, 272), t_ref, x_hi, x_lo)):
                    y_ref[i, part] = value
            for part in range(2):
                y_ref[0, part, 264:272, :] = y_ref[1, part, 8:16, :]
                y_ref[1, part, 0:8, :] = y_ref[0, part, 256:264, :]
                if half == 0:
                    y_ref[0, part, 0:8, :] = jnp.zeros((8, 128), F32)
                else:
                    y_ref[1, part, 264:272, :] = jnp.zeros((8, 128), F32)

    o0[...] = y_ref[me % 2]
    o1[...] = y_ref[1 - me % 2]


def first_sums_kernel(weight_ref, y0, ya, part_ref):
    own, other = weight_ref[0, 0:1, :], weight_ref[FIRST, 0:1, :]
    for part in range(2):
        part_ref[part] = y0[part] * own + ya[part, 0:272, :] * other
        part_ref[2 + part] = y0[part] * (1.0 - own) + ya[part, 0:272, :] * (1.0 - other)


def more_sums_kernel(weight_ref, first_ref, yb, part_ref):
    weight = weight_ref[3 - FIRST, 0:1, :]
    for part in range(2):
        part_ref[part] = first_ref[part] + yb[part] * weight
        part_ref[2 + part] = first_ref[2 + part] + yb[part] * (1.0 - weight)


def whole_sums(weight_ref, part_ref, y1):
    weight = weight_ref[3, 0:1, :]
    fore = [part_ref[part] + y1[part] * weight for part in range(2)]
    return fore + [part_ref[2 + part] + y1[part] * (1.0 - weight) for part in range(2)]


def edge_kernel(weight_ref, part_ref, y1, passed, edge_ref):
    lane = lax.broadcasted_iota(jnp.int32, (272, 128), 1)
    edge = jnp.zeros((272, 128), F32)
    far = []
    for part in range(2):
        groups = [passed[part] if j == 0 else pltpu.roll(passed[part], 128 - 16 * j, 1) for j in range(7)]
        far.append(jnp.concatenate(groups[:6] + [groups[6][0:32]], 0))
    weight = weight_ref[3 - FIRST, 0:1, :]
    for plane, value in enumerate(whole_sums(weight_ref, part_ref, y1)):
        value = value + far[plane % 2] * (weight if plane < 2 else 1.0 - weight)
        at = 16 * plane
        moved = pltpu.roll(value, at, 1) if at else value
        edge = jnp.where((lane >= at) & (lane < at + 16), moved, edge)
    edge_ref[...] = edge[0:136] + pltpu.roll(edge[136:272], 64, 1)


def quantities(fr, fi, ar, ai):
    return fr * ar + fi * ai, fi * ar - fr * ai, fr * fr + fi * fi, ar * ar + ai * ai


def main_kernel(weight_ref, rows_ref, near_ref, part_ref, y1, out_ref, p_hi, p_lo):
    for q, value in enumerate(quantities(*whole_sums(weight_ref, part_ref, y1))):
        hi, lo = split(value)
        p_hi[0:272, 128 * q:128 * q + 128] = hi
        p_lo[0:272, 128 * q:128 * q + 128] = lo
    p_hi[272:384, :] = jnp.zeros((112, 512), BF16)
    p_lo[272:384, :] = jnp.zeros((112, 512), BF16)
    for g in range(2):
        sums = dot_nn(rows_ref[g], p_hi[128 * g:128 * g + 256, :]) + dot_nn(rows_ref[g], p_lo[128 * g:128 * g + 256, :])
        hi, lo = split(jnp.concatenate([sums[:, 128 * q:128 * q + 128] for q in range(4)], 0))
        out_ref[g] = dot_nn(hi, near_ref[g]) + dot_nn(lo, near_ref[g])


def coherence_kernel(rows_ref, far_ref, main_ref, edge_ref, out_ref, p_hi, p_lo):
    packed = edge_ref[...]
    edge = jnp.concatenate([packed, pltpu.roll(packed, 64, 1)], 0)
    lane = lax.broadcasted_iota(jnp.int32, (272, 128), 1)
    planes = [edge] + [pltpu.roll(edge, 128 - 16 * i, 1) for i in range(1, 4)]
    both = jnp.zeros((272, 128), F32)
    for q, value in enumerate(quantities(*planes)):
        moved = pltpu.roll(value, 16 * q, 1) if q else value
        both = jnp.where((lane >= 16 * q) & (lane < 16 * q + 16), moved, both)
    hi, lo = split(both)
    p_hi[0:272, :] = hi
    p_lo[0:272, :] = lo
    p_hi[272:384, :] = jnp.zeros((112, 128), BF16)
    p_lo[272:384, :] = jnp.zeros((112, 128), BF16)
    for g in range(2):
        sums = dot_nn(rows_ref[g], p_hi[128 * g:128 * g + 256, :]) + dot_nn(rows_ref[g], p_lo[128 * g:128 * g + 256, :])
        hi, lo = split(jnp.concatenate([sums] + [pltpu.roll(sums, 128 - 16 * q, 1) for q in range(1, 4)], 0))
        window = main_ref[g] + dot_nn(hi, far_ref[g]) + dot_nn(lo, far_ref[g])
        scale = 1.0 / jnp.sqrt(jnp.maximum(window[256:384], 1.0) * jnp.maximum(window[384:512], 1.0))
        out_ref[0, 128 * g:128 * g + 128, :] = window[0:128] * scale
        out_ref[1, 128 * g:128 * g + 128, :] = window[128:256] * scale


def call(kernel, name, out_shape, scratch, n_in, smem=(), hbm=(), flops=0, moved=0, vmem=VMEM_LIMIT, out=pltpu.VMEM):
    spaces = [pltpu.SMEM if i in smem else pltpu.HBM if i in hbm else pltpu.VMEM for i in range(n_in)]
    return pl.pallas_call(
        kernel,
        out_shape=out_shape,
        in_specs=[pl.BlockSpec(memory_space=space) for space in spaces],
        out_specs=jax.tree.map(lambda _: pl.BlockSpec(memory_space=out), out_shape),
        scratch_shapes=scratch,
        compiler_params=pltpu.CompilerParams(vmem_limit_bytes=vmem),
        cost_estimate=pl.CostEstimate(flops=flops, bytes_accessed=moved, transcendentals=0),
        name=name,
    )


def shape(*dims, dtype=F32):
    return jax.ShapeDtypeStruct(dims, dtype)


def body(echoes, range_chirp, azimuth_filter, pairing, offsets):
    signal = echoes[:, 0]
    chirp = range_chirp.reshape(2, 1, 512)
    taps = azimuth_filter.reshape(2, 1, 1024)
    parted = call(
        range_kernel, "range_filter", shape(64, 32, 128),
        [pltpu.VMEM((2, 16, 8192), F32), pltpu.VMEM((2, 1, 512), F32), pltpu.VMEM((64, 32, 128), F32)]
        + [pltpu.VMEM((1088, 256), BF16)] * 2 + [pltpu.VMEM((256, 1280), BF16)] * 2
        + [pltpu.SemaphoreType.DMA((5,))] * 2,
        2, hbm=(0, 1), flops=2_000_000_000, moved=2 << 20, vmem=60 << 20, out=pltpu.HBM,
    )(signal, chirp)
    turned = lax.all_to_all(parted, "wide", split_axis=0, concat_axis=0, tiled=True)
    t, weight, rows, near, far = call(
        prepare_kernel, "prepare",
        (shape(4, 272, 1024, dtype=BF16), shape(4, 8, 128), shape(2, 128, 256, dtype=BF16))
        + (shape(2, 128, 128, dtype=BF16),) * 2, [],
        3, smem=(0, 1), flops=1_000_000_000, moved=1 << 20,
    )(pairing, offsets, taps)
    order = weight.reshape(32, 128)
    pa, pb, order, *pulses = call(
        other_quarters, "azimuth_other",
        (shape(2, 312, 128), shape(2, 272, 128), shape(8, 128)) + (shape(1024, 256, dtype=BF16),) * 2,
        [], 3, flops=1_000_000_000, moved=1000,
    )(turned, t, order)
    p0, p1 = call(
        azimuth_own, "azimuth_own", (shape(2, 272, 128),) * 2,
        [pltpu.VMEM((4, 272, 1280), BF16), pltpu.VMEM((2, 2, 272, 128), F32)],
        4, flops=1000, moved=1000,
    )(order, taps, *pulses)
    ya, yb, y1 = [lax.ppermute(p, "chan", [(i, i ^ k) for i in range(4)]) for k, p in ((2, pa), (3, pb), (1, p1))]
    passed = lax.ppermute(ya[:, 272:312, :], "chan", [(i, i ^ 1) for i in range(4)])
    first = call(
        first_sums_kernel, "two_receivers", shape(4, 272, 128), [], 3, flops=FIRST_COST, moved=1000,
    )(weight, p0, ya)
    edge = call(
        edge_kernel, "edge", shape(136, 128), [], 4, flops=1000, moved=1000,
    )(weight, first, y1, passed)
    part = call(
        more_sums_kernel, "three_receivers", shape(4, 272, 128), [], 3, flops=30_000_000_000, moved=2 << 20,
    )(weight, first, yb)
    after = lax.ppermute(edge, "wide", [(i, (i - 1) % 64) for i in range(64)])
    main = call(
        main_kernel, "window_sums", shape(2, 512, 128), [pltpu.VMEM((384, 512), BF16)] * 2,
        5, flops=500_000_000, moved=1 << 20,
    )(weight, rows, near, part, y1)
    return call(
        coherence_kernel, "coherence", shape(2, 256, 128), [pltpu.VMEM((384, 128), BF16)] * 2,
        4, flops=500_000_000, moved=1 << 20,
    )(rows, far, main, after)


def solution(mesh):
    placed = (P(None, "chan", "wide", None), P(None, "chan", None), P(None, "chan", None), P(), P())
    return jax.shard_map(
        body, mesh=mesh, in_specs=placed, out_specs=P(None, "chan", "wide"), check_vma=False
    )
```
